256 devices in a mesh: pairs: 32 (over y, x, core), ri: 8 (over z).
Axes of the slice: x: 4, y: 4, z: 8, core: 2. Of those that a mesh axis runs over, the one named last changes fastest.
Arguments:
- atom_blocks: bfloat16 [512, 20, 14336], P('pairs', None, 'ri'), may hold values from -6 to 6
- domains: int32 [1024, 12], P('pairs'), may hold values from 0 to 511, as said below
- pno_counts: int32 [1024], P('pairs'), may hold values from 20 to 200
- pno_coeffs: bfloat16 [1024, 240, 256], P('pairs'), may hold values from -0.375 to 0.375
- amplitudes: bfloat16 [1024, 256, 256], P(('pairs', 'ri')), may hold values from -3 to 3
- pno_energies: float32 [1024, 256], P(('pairs', 'ri')), may hold values from 0.2 to 4
Outputs:
- residual: float32 [1024, 256, 256], P(('pairs', 'ri'))
The draws below stay inside these ranges and needn't reach their ends.
Inputs may be any that keep to these rules, and one draw needn't show every extreme that they name: `domains`: atom a belongs to owner a // 16 along pairs. The pairs of one device (aligned blocks of 32 rows) name atoms of at most 16 owners and at most 3 distinct atoms of any one owner; in every draw some owner gives exactly 3 distinct atoms to every device.
All inputs are finite; a program needn't handle non-finite values.
Results may differ from the reference program's by a relative error of at most 0.0003.
Values may be sent and summed in bfloat16 or wider, within the bound.
A program may use at most 192 MiB of HBM per device.

```python
import math
from functools import partial
import jax
import jax.numpy as jnp
from jax import lax

W = 20
NAUX = 14336
PMAX = 256
MAXPNO = 200
MINPNO = 20
DOM = 12
CAP = 3
PAIR_DEV = 32
ATOM_DEV = 16
PAIRS = 1024
ATOMS = 512


def draw_domains(key, part):
    key = jax.random.fold_in(key, 7)
    owners = PAIRS // PAIR_DEV
    groups = owners // 2
    set_size = groups * CAP
    subkeys = jax.random.split(key, 6)
    hot_owner = jax.random.randint(subkeys[0], (), 0, owners)
    offsets = jax.vmap(lambda k: jax.random.permutation(k, owners - 1))(jax.random.split(subkeys[1], owners)) + 1
    relative = jnp.concatenate([jnp.zeros((owners, 1), jnp.int32), offsets[:, :groups - 1].astype(jnp.int32)], axis=1)
    chosen = (hot_owner + relative) % owners
    local_atoms = jax.vmap(lambda k: jax.random.permutation(k, ATOM_DEV))(jax.random.split(subkeys[2], owners * groups))
    local_atoms = local_atoms[:, :CAP].reshape(owners, groups, CAP).astype(jnp.int32)
    distinct = jax.random.randint(subkeys[3], (owners, groups), 1, CAP + 1)
    group_ids = jnp.arange(groups, dtype=jnp.int32)
    distinct = jnp.where(group_ids[None, :] == 0, CAP, distinct)
    slot_ids = jnp.arange(CAP, dtype=jnp.int32)
    local_pick = jnp.where(slot_ids[None, None, :] < distinct[:, :, None], local_atoms, local_atoms[:, :, :1])
    atom_set = (chosen[:, :, None] * ATOM_DEV + local_pick).reshape(owners, set_size)
    atom_set = jax.vmap(lambda k, row: jax.random.permutation(k, row))(jax.random.split(subkeys[4], owners), atom_set)
    starts = jax.random.randint(subkeys[5], (owners, PAIR_DEV), 0, set_size)
    pair_ids = jnp.arange(PAIR_DEV, dtype=jnp.int32)
    starts = jnp.where(pair_ids[None, :] < set_size // DOM, pair_ids[None, :] * DOM, starts)
    positions = (starts[:, :, None] + jnp.arange(DOM, dtype=jnp.int32)[None, None, :]) % set_size
    picked = jax.vmap(lambda row, where_at: row[where_at])(atom_set, positions)
    return picked.reshape(PAIRS, DOM).astype(jnp.int32)


def draw_pno_counts(key, part):
    key = jax.random.fold_in(key, 3)
    subkeys = jax.random.split(key, 3)
    counts = jax.random.randint(subkeys[0], (PAIRS,), MINPNO, MAXPNO + 1)
    top_pair = jax.random.randint(subkeys[1], (), 0, PAIRS)
    low_pair = (top_pair + 1 + jax.random.randint(subkeys[2], (), 0, PAIRS - 1)) % PAIRS
    pair_ids = jnp.arange(PAIRS, dtype=jnp.int32)
    counts = jnp.where(pair_ids == top_pair, MAXPNO, counts)
    counts = jnp.where(pair_ids == low_pair, MINPNO, counts)
    return counts.astype(jnp.int32)


def steps_of(key, shape, cuts, least, top_value):
    loudness, own = 1.0, jax.random.fold_in(key, 6)
    for axis_at, shards_of in cuts:
        steps = jnp.exp(jax.random.uniform(jax.random.fold_in(own, axis_at), (shards_of,), jnp.float32, least / len(cuts), top_value / len(cuts)))
        loudness = loudness * jnp.repeat(steps, shape[axis_at] // shards_of).reshape([-1 if axis == axis_at else 1 for axis in range(len(shape))])
    return loudness


def bell_draw(stream_key, shape, spread, reach, pieces=(), held_as=jnp.bfloat16):
    entries = spread * jax.random.normal(stream_key, shape, jnp.float32)
    if pieces:
        entries = entries * steps_of(stream_key, shape, pieces, -0.22, 0.18)
    return jnp.clip(entries, -reach, reach).astype(held_as)


def setup_inputs(seed: int = 0) -> dict:
    arg_keys = jax.random.split(jax.random.key(seed), 7)
    atom_blocks = bell_draw(arg_keys[0], (ATOMS, W, NAUX), 1.0, 6.0, ((0, 32), (2, 8)))
    domains = draw_domains(jax.random.fold_in(arg_keys[6], 71), 0)
    pno_counts = draw_pno_counts(jax.random.fold_in(arg_keys[6], 71), 0)
    pno_coeffs = bell_draw(arg_keys[3], (PAIRS, DOM * W, PMAX), (DOM * W) ** -0.5, 0.375, ((0, 32),))
    amplitudes = bell_draw(arg_keys[4], (PAIRS, PMAX, PMAX), 0.5, 3.0, ((0, 256),))
    pno_energies = jnp.clip(jnp.exp(math.log(4.0) - 2.9957323 * jax.random.uniform(arg_keys[5], (PAIRS, PMAX), jnp.float32) ** steps_of(arg_keys[5], (PAIRS, PMAX), ((0, 256),), -0.2, 0.2)), 0.2, 4.0)
    return dict(atom_blocks=atom_blocks, domains=domains, pno_counts=pno_counts, pno_coeffs=pno_coeffs, amplitudes=amplitudes, pno_energies=pno_energies)


def one_pair(atom_blocks, item):
    doms, count, coeff, amp, energy = item
    block = jnp.take(atom_blocks, doms.astype(jnp.int32), axis=0).reshape(-1, atom_blocks.shape[2])
    projected = jnp.dot(coeff.T, block, preferred_element_type=jnp.float32)
    valid = jnp.arange(coeff.shape[1], dtype=jnp.int32) < count
    vectors = jnp.where(valid[:, None], projected, jnp.zeros_like(projected)).astype(jnp.bfloat16)
    products = jnp.dot(vectors, vectors.T, preferred_element_type=jnp.float32) / NAUX
    amp_full = amp.astype(jnp.float32)
    coupled = jnp.dot(products, amp_full.T, precision=lax.Precision.HIGHEST)
    result = products + coupled + (energy[:, None] + energy[None, :]) * amp_full
    mask = valid[:, None] & valid[None, :]
    return jnp.where(mask, result, jnp.zeros_like(result))


def reference(atom_blocks, domains, pno_counts, pno_coeffs, amplitudes, pno_energies):
    return lax.map(partial(one_pair, atom_blocks), (domains, pno_counts, pno_coeffs, amplitudes, pno_energies))
```

```python
import jax
import jax.numpy as jnp
from jax import lax
from jax.experimental import pallas as pl
from jax.experimental.pallas import tpu as pltpu
from jax.sharding import PartitionSpec as P

NAUX = 14336
CAP = 3
MAXPNO = 200
MAIN = 16
REM = 4
SPLIT = 128
REST = MAXPNO - SPLIT
LANES = 128
MIB = 1 << 20
RING = 4
CORES = 2
ATOMS = 16
DOM = 12
BAND = MAIN + REM
PICKS = RING * CAP
HALF = PICKS // 2
DEPTH = 256
DUO = SPLIT + 3 * REST + 8
TILES = (4, 4, 3, 3)
FIRST = (0, 4, 8, 11)
MESH = pl.DeviceIdType.MESH


def params(mib, **kw):
    return pltpu.CompilerParams(vmem_limit_bytes=mib * MIB, **kw)


def widths(chunk):
    return TILES[chunk] * LANES, TILES[chunk] * LANES + LANES


class Ports:
    def __init__(self, chunk, gather_to, deliver_to, wire, ring, send, relay, recv, out_sems, in_sems, core):
        self.gather_to, self.deliver_to, self.core = gather_to, deliver_to, core
        self.wire, self.ring, self.send, self.relay, self.recv = wire, ring, send, relay, recv
        self.out_sems, self.in_sems, self.chunk = out_sems, in_sems, chunk

    def copy(self, src, dst, out_at, in_at, to):
        return pltpu.make_async_remote_copy(
            src_ref=src,
            dst_ref=dst,
            send_sem=self.out_sems.at[self.chunk, out_at],
            recv_sem=self.in_sems.at[self.chunk, in_at],
            device_id={"pairs": to},
            device_id_type=MESH,
        )

    def gather_first(self):
        up = self.copy(self.wire, self.ring.at[2], 0, 1, self.gather_to(1, self.core))
        down = self.copy(self.wire, self.ring.at[0], 1, 0, self.gather_to(3, self.core))
        return up, down

    def gather_second(self):
        half = ATOMS // 2
        low, high = pl.ds(0, half), pl.ds(half, half)
        up = self.copy(self.ring.at[2, low], self.ring.at[1, low], 2, 2, self.gather_to(1, self.core))
        down = self.copy(self.ring.at[0, high], self.ring.at[1, high], 3, 3, self.gather_to(3, self.core))
        return up, down

    def place(self, rel, core):
        return (rel * CORES + core) * PICKS

    def far(self):
        up = self.copy(self.send.at[2, :, pl.ds(0, HALF)], self.relay.at[0], 4, 4, self.deliver_to(1, self.core))
        down = self.copy(self.send.at[2, :, pl.ds(HALF, HALF)], self.relay.at[1], 5, 5, self.deliver_to(3, self.core))
        return up, down

    def near(self):
        copies = []
        for n, step in enumerate((1, 3)):
            for core in range(CORES):
                dst = self.recv.at[pl.ds(self.place(RING - step, self.core), PICKS)]
                at = 6 + 2 * n
                copies.append(self.copy(self.send.at[step, core], dst, at + core, at + self.core, self.deliver_to(step, core)))
        other = 1 - self.core
        dst = self.recv.at[pl.ds(self.place(0, self.core), PICKS)]
        copies.append(self.copy(self.send.at[0, other], dst, 10, 10, self.deliver_to(0, other)))
        return copies

    def own(self):
        return pltpu.make_async_copy(
            self.send.at[0, self.core],
            self.recv.at[pl.ds(self.place(0, self.core), PICKS)],
            self.in_sems.at[self.chunk, 11],
        )

    def onward(self):
        copies = []
        for way, step in enumerate((1, 3)):
            for core in range(CORES):
                dst = self.recv.at[pl.ds(self.place(2, self.core) + way * HALF, HALF)]
                at = 12 + 2 * way
                copies.append(self.copy(self.relay.at[way, core], dst, at + core, at + self.core, self.deliver_to(step, core)))
        return copies

    def start_gather(self):
        for copy in self.gather_first():
            copy.start()

    def forward_gather(self):
        up, down = self.gather_second()
        first_up, first_down = self.gather_first()
        first_up.wait_recv()
        up.start()
        first_down.wait_recv()
        down.start()

    def finish_gather(self):
        for copy in self.gather_second():
            copy.wait_recv()

    def start_delivery(self):
        for copy in self.far() + tuple(self.near()):
            copy.start()
        self.own().start()

    def forward_delivery(self):
        far, onward = self.far(), self.onward()
        for way in range(2):
            far[way].wait_recv()
            for copy in onward[2 * way : 2 * way + 2]:
                copy.start()

    def finish_delivery(self):
        for n, step in enumerate((1, 3)):
            for core in range(CORES):
                dst = self.recv.at[pl.ds(self.place(step, core), PICKS)]
                at = 6 + 2 * (1 - n)
                self.copy(dst, dst, at + core, at + core, self.deliver_to(1, self.core)).wait_recv()
        other = 1 - self.core
        dst = self.recv.at[pl.ds(self.place(0, other), PICKS)]
        self.copy(dst, dst, 10, 10, self.deliver_to(1, self.core)).wait_recv()
        self.own().wait()
        for way in range(2):
            for core in range(CORES):
                dst = self.recv.at[pl.ds(self.place(2, core) + way * HALF, HALF)]
                at = 12 + 2 * way
                self.copy(dst, dst, at + core, at + core, self.deliver_to(1, self.core)).wait_recv()

    def finish_served(self):
        for copy in self.far() + tuple(self.near()):
            copy.wait_send()

    def finish_sends(self):
        for copy in self.gather_first() + self.gather_second() + tuple(self.onward()):
            copy.wait_send()


def main_kernel(
    blocks, domains, coeff_hbm, out, *scratch
):
    wires, rings, sends, relays, recvs = (scratch[4 * n : 4 * n + 4] for n in range(5))
    asked, asked_smem, tables, places, request, ids, perm_main, perm_rest = scratch[20:28]
    coeff, coeff_t, perm, blk, total, sums, fresh = scratch[28:35]
    out_sems, in_sems, ask_out, ask_in, local_sems, sum_out, sum_in = scratch[35:42]
    me = lax.axis_index("pairs")
    at_z = lax.axis_index("ri")
    planes = 2 * (sums.shape[1] - 1)
    above, below = lax.rem(at_z + 1, planes), lax.rem(at_z + planes - 1, planes)
    core = lax.rem(me, CORES)
    chip = lax.div(me, CORES)
    at_x = lax.rem(chip, RING)
    at_y = lax.div(chip, RING)

    def along_x(step, to_core):
        return (at_y * RING + lax.rem(at_x + step, RING)) * CORES + to_core

    def along_y(step, to_core):
        return (lax.rem(at_y + step, RING) * RING + at_x) * CORES + to_core

    peers = []
    for to_core in range(2):
        for step in range(1, RING):
            peers.append((along_y(step, to_core), step * CORES + to_core, (RING - step) * CORES + core))
            peers.append(
                (along_x(step, to_core), (RING + step) * CORES + to_core, (2 * RING - step) * CORES + core)
            )
    peers.append((along_x(0, 1 - core), 1 - core, core))

    fetch = pltpu.make_async_copy(coeff_hbm, coeff, local_sems.at[0])
    fetch.start()
    barrier = pltpu.get_barrier_semaphore()
    for peer, _, _ in peers:
        pl.semaphore_signal(barrier, inc=1, device_id={"pairs": peer}, device_id_type=MESH)
    for plane in (above, below):
        pl.semaphore_signal(barrier, inc=1, device_id={"ri": plane}, device_id_type=MESH)

    def ask(n):
        peer, _, there = peers[n]
        return pltpu.make_async_remote_copy(
            src_ref=request,
            dst_ref=asked.at[there],
            send_sem=ask_out.at[n],
            recv_sem=ask_in.at[there],
            device_id={"pairs": peer},
            device_id_type=MESH,
        )

    ports = []
    for chunk in range(4):
        gather_to, deliver_to = (along_x, along_y) if chunk % 2 == 0 else (along_y, along_x)
        ports.append(
            Ports(
                chunk, gather_to, deliver_to, wires[chunk], rings[chunk], sends[chunk],
                relays[chunk], recvs[chunk], out_sems, in_sems, core,
            )
        )

    square = (ATOMS * MAIN, ATOMS * MAIN)
    out_at = lax.broadcasted_iota(jnp.int32, square, 0)
    from_at = lax.broadcasted_iota(jnp.int32, square, 1)
    band_at, atom_at = out_at % MAIN, out_at // MAIN
    perm_main[...] = jnp.where(band_at * ATOMS + atom_at == from_at, 1.0, 0.0).astype(jnp.bfloat16)
    rest_at = (band_at // REM) * (REM * ATOMS) + (band_at % REM) * ATOMS + atom_at
    perm_rest[...] = jnp.where(rest_at == from_at, 1.0, 0.0).astype(jnp.bfloat16)

    def form(chunk):
        cols, _ = widths(chunk)
        begin = FIRST[chunk] * LANES
        flat = blocks[:MAIN, :, begin : begin + cols].reshape(MAIN * ATOMS, cols)
        main = jnp.dot(perm_main[...], flat, preferred_element_type=jnp.float32).astype(jnp.bfloat16)
        wires[chunk][:, :, :cols] = main.reshape(ATOMS, MAIN, cols)
        rest = blocks[MAIN:, :, begin : begin + cols].reshape(REM * ATOMS, cols)
        stacked = jnp.concatenate([rest[:, q * LANES : (q + 1) * LANES] for q in range(TILES[chunk])], axis=0)
        depth = stacked.shape[0]
        late = jnp.dot(perm_rest[:, :depth], stacked, preferred_element_type=jnp.float32).astype(jnp.bfloat16)
        wires[chunk][:, :, cols:] = late.reshape(ATOMS, MAIN, LANES)

    form(0)
    form(1)

    ids[...] = jnp.zeros_like(ids)
    pairs = domains.shape[1]
    fold = LANES // pairs
    ids[: domains.shape[0], :pairs] = domains[...]
    held = ids[...]
    lane = lax.broadcasted_iota(jnp.int32, held.shape, 1)
    turned = [held if n == 0 else pltpu.roll(held, n * pairs, 1) for n in range(fold)]
    lines = []
    for line in range(DOM // fold):
        row = jnp.zeros((1, LANES), jnp.int32)
        for n in range(fold):
            k = line * fold + n
            row = jnp.where(lane[:1] // pairs == n, turned[n][k : k + 1], row)
        lines.append(row)
    flat_shape = (ATOMS * RING * RING * CORES, LANES)
    atom = lax.broadcasted_iota(jnp.int32, flat_shape, 0)
    lane_at = lax.broadcasted_iota(jnp.int32, flat_shape, 1)
    named = jnp.zeros(flat_shape, jnp.int32)
    for line in lines:
        named = jnp.where(atom == line, 1, named)
    named = jnp.broadcast_to(jnp.max(named, axis=1, keepdims=True), flat_shape)
    local = atom % ATOMS
    owner = atom // ATOMS
    rank = named
    for shift in (1, 2, 4, 8):
        rank = rank + jnp.where(local >= shift, pltpu.roll(rank, shift, 0), 0)
    own_lane = jnp.where((owner == lane_at) & (named > 0), local, 0)
    for j in range(CAP):
        request[j : j + 1, :] = jnp.sum(jnp.where(rank == j + 1, own_lane, 0), axis=0, keepdims=True)
    request[CAP:, :] = jnp.zeros((8 - CAP, LANES), jnp.int32)

    pl.semaphore_wait(barrier, len(peers) + 2)
    ports[0].start_gather()
    ports[1].start_gather()
    for n in range(len(peers)):
        ask(n).start()
    own_ask = pltpu.make_async_copy(request, asked.at[core], local_sems.at[1])
    own_ask.start()

    form(2)
    form(3)
    owner_chip = owner // CORES
    rel_x = (owner_chip + RING - at_x) % RING
    rel_y = (owner_chip // RING + RING - at_y) % RING
    owner_core = owner % CORES
    place_x = ((rel_y * CORES + owner_core) * RING + rel_x) * CAP + rank - 1
    place_y = ((rel_x * CORES + owner_core) * RING + rel_y) * CAP + rank - 1
    tables[...] = jnp.zeros_like(tables)
    for n, line in enumerate(lines):
        for table, place in enumerate((place_x, place_y)):
            tables[table, n : n + 1, :] = jnp.sum(jnp.where(atom == line, place, 0), axis=0, keepdims=True)
    table_copy = pltpu.make_async_copy(tables, places, local_sems.at[3])
    table_copy.start()
    table_copy.wait()

    shape = (DEPTH, DOM * BAND)
    row = lax.broadcasted_iota(jnp.int32, shape, 0)
    col = lax.broadcasted_iota(jnp.int32, shape, 1)
    split = DOM * MAIN
    late = row - split
    source = jnp.where(
        row < split,
        (row // MAIN) * BAND + row % MAIN,
        (late // REM) * BAND + MAIN + late % REM,
    )
    perm[...] = jnp.where((source == col) & (row < DOM * BAND), 1.0, 0.0).astype(jnp.bfloat16)
    for n in range(2):
        blk[n, DOM * BAND :, :] = jnp.zeros((DEPTH - DOM * BAND, blk.shape[2]), jnp.bfloat16)
    fetch.wait()

    def prepare(begin, end):
        def turn(pair, _):
            ordered = jnp.dot(perm[...], coeff[pair], preferred_element_type=jnp.float32)
            coeff_t[pair] = ordered.T[:MAXPNO].astype(jnp.bfloat16)
            return 0

        lax.fori_loop(begin, end, turn, 0)

    half_pairs = coeff.shape[0] // 2
    quarter = half_pairs // 2
    prepare(0, half_pairs - REM)
    ports[0].forward_gather()
    ports[1].forward_gather()
    ports[2].start_gather()
    ports[3].start_gather()
    prepare(half_pairs - REM, half_pairs + REM)

    own_ask.wait()
    for n in range(len(peers)):
        _, here, _ = peers[n]
        pltpu.make_async_remote_copy(
            src_ref=request,
            dst_ref=asked.at[here],
            send_sem=ask_out.at[n],
            recv_sem=ask_in.at[here],
            device_id={"pairs": peers[n][0]},
            device_id_type=MESH,
        ).wait_recv()
    to_smem = pltpu.make_async_copy(asked, asked_smem, local_sems.at[2])
    to_smem.start()
    to_smem.wait()

    def pick(chunk):
        port = ports[chunk]
        owner_of = along_x if chunk % 2 == 0 else along_y

        def serve(dest, _):
            line = dest if chunk % 2 == 0 else jnp.where(dest < CORES, dest, dest + RING * CORES)
            step, to_core = dest // CORES, dest % CORES
            for r in range(RING):
                for j in range(CAP):
                    atom = asked_smem[line, j, owner_of(r, core)]
                    found = port.wire[atom] if r == 0 else port.ring[r - 1, atom]
                    port.send[step, to_core, r * CAP + j] = found
            return 0

        lax.fori_loop(0, RING * CORES, serve, 0)

    for chunk in (0, 1):
        ports[chunk].finish_gather()
        pick(chunk)
        ports[chunk].start_delivery()
    for chunk in (2, 3):
        ports[chunk].forward_gather()
    prepare(half_pairs + REM, half_pairs + quarter)
    ports[0].forward_delivery()
    ports[1].forward_delivery()
    for chunk in (2, 3):
        ports[chunk].finish_gather()
        pick(chunk)
    prepare(half_pairs + quarter, 2 * half_pairs)
    for chunk in (2, 3):
        ports[chunk - 2].finish_served()
        ports[chunk].start_delivery()

    pack_row = lax.broadcasted_iota(jnp.int32, (SPLIT, LANES), 0)
    pack_col = lax.broadcasted_iota(jnp.int32, (SPLIT, LANES), 1)
    rest_row = lax.broadcasted_iota(jnp.int32, (REST, REST), 0)
    rest_col = lax.broadcasted_iota(jnp.int32, (REST, REST), 1)

    def assemble(pair, slot, chunks):
        base = MAIN * DOM
        begin = 0
        for table, chunk in enumerate(chunks):
            cols, _ = widths(chunk)
            upper = lax.broadcasted_iota(jnp.int32, (8, LANES), 0) < REM
            at = [places[table, k // fold, (k % fold) * pairs + pair] for k in range(DOM)]
            for k in range(DOM):
                blk[slot, MAIN * k : MAIN * (k + 1), begin : begin + cols] = recvs[chunk][at[k], :, :cols]
            for k in range(0, DOM, 4):
                rest = [recvs[chunk][at[k + n], :, cols:].astype(jnp.float32) for n in range(4)]
                for half in range((TILES[chunk] + 1) // 2):
                    parts = [r[8 * half : 8 * half + 8] for r in rest]
                    shifted = [pltpu.roll(part, REM, 0) for part in parts]
                    for q in range(2 * half, min(2 * half + 2, TILES[chunk])):
                        first, second = (parts, shifted) if q % 2 == 0 else (shifted, parts)
                        low = jnp.where(upper, first[0], second[1])
                        high = jnp.where(upper, first[2], second[3])
                        both = jnp.concatenate([low, high], axis=0).astype(jnp.bfloat16)
                        tile = slice(begin + q * LANES, begin + (q + 1) * LANES)
                        blk[slot, base + REM * k : base + REM * (k + 4), tile] = both
            begin += cols
        return begin

    def multiply(pair, slot, cols):
        weights = coeff_t[pair]
        result = jnp.zeros((MAXPNO, MAXPNO), jnp.float32)
        for at in range(0, cols, 256):
            vec = jnp.dot(weights, blk[slot, :, at : at + 256], preferred_element_type=jnp.float32)
            vec = vec.astype(jnp.bfloat16)
            result += lax.dot_general(vec, vec, (((1,), (1,)), ((), ())), preferred_element_type=jnp.float32)
        return result

    def first_half(step, _):
        for n in range(2):
            cols = assemble(2 * step + n, n, (0, 1))
        for n in range(2):
            total[2 * step + n] = multiply(2 * step + n, n, cols)
        return 0

    group = coeff.shape[0] // planes
    half_ring = planes // 2
    part = DUO // 2

    def chain(way, step, duo, piece):
        rows = pl.ds(piece * part, part)
        return pltpu.make_async_remote_copy(
            src_ref=sums.at[way, step, duo, rows],
            dst_ref=sums.at[way, step + 1, duo, rows],
            send_sem=sum_out.at[(way * half_ring + step) * 2 + duo, piece],
            recv_sem=sum_in.at[(way * half_ring + step) * 2 + duo, piece],
            device_id={"ri": jnp.where(way == 0, above, below)},
            device_id_type=MESH,
        )

    def second_half(owner, duo):
        first = owner * group + 2 * duo
        for n in range(2):
            cols = assemble(first + n, n, (2, 3))
        whole = [total[first + n] + multiply(first + n, n, cols) for n in range(2)]
        here, there = [w[:SPLIT, :SPLIT] for w in whole]
        fresh[:SPLIT, :] = jnp.where(pack_row >= pack_col, here, there)
        for n in range(2):
            fresh[SPLIT + n * REST : SPLIT + (n + 1) * REST, :] = whole[n][SPLIT:, :SPLIT]
        at = SPLIT + 2 * REST
        low_here, low_there = [w[SPLIT:, SPLIT:] for w in whole]
        fresh[at : at + REST, :REST] = jnp.where(rest_row >= rest_col, low_here, low_there)
        at += REST
        fresh[at : at + 1, :] = jnp.sum(jnp.where(pack_row == pack_col, there, 0.0), axis=0, keepdims=True)
        fresh[at + 1 : at + 2, :REST] = jnp.sum(
            jnp.where(rest_row == rest_col, low_there, 0.0), axis=0, keepdims=True
        )

    def send_on(item, _):
        later = jnp.maximum(item - 2, 0)
        turn = later % 4
        opening = item < 2
        step = jnp.where(opening, 0, 1 + later // 4)
        way = jnp.where(opening, item, turn % 2)
        early = jnp.logical_and(jnp.logical_not(opening), turn < 2)
        duo = jnp.where(early, 1 - way, way)
        away = jnp.where(way == 0, half_ring - step, half_ring + step)
        second_half(lax.rem(at_z + away, planes), duo)
        alone = jnp.logical_or(opening, jnp.logical_and(early, step == 1))

        @pl.when(alone)
        def _():
            sums[way, step, duo] = fresh[...]
            for piece in range(2):
                chain(way, step, duo, piece).start()

        @pl.when(jnp.logical_not(alone))
        def _():
            for piece in range(2):
                rows = slice(piece * part, (piece + 1) * part)
                chain(way, step - 1, duo, piece).wait_recv()
                sums[way, step, duo, rows, :] = sums[way, step, duo, rows, :] + fresh[rows, :]
                chain(way, step, duo, piece).start()

        return 0

    def send_done(item, _):
        later = jnp.maximum(item - 2, 0)
        turn = later % 4
        opening = item < 2
        step = jnp.where(opening, 0, 1 + later // 4)
        way = jnp.where(opening, item, turn % 2)
        early = jnp.logical_and(jnp.logical_not(opening), turn < 2)
        duo = jnp.where(early, 1 - way, way)
        for piece in range(2):
            chain(way, step, duo, piece).wait_send()
        return 0

    ports[0].finish_delivery()
    ports[1].finish_delivery()
    lax.fori_loop(0, half_pairs // 2, first_half, 0)
    ports[2].forward_delivery()
    ports[3].forward_delivery()
    lax.fori_loop(half_pairs // 2, half_pairs, first_half, 0)
    ports[2].finish_delivery()
    ports[3].finish_delivery()
    fresh[...] = jnp.zeros_like(fresh)
    items = 2 + 4 * (half_ring - 1)
    lax.fori_loop(0, items, send_on, 0)
    for duo in range(2):
        second_half(at_z, duo)
        for piece in range(2):
            rows = slice(piece * part, (piece + 1) * part)
            for way in range(2):
                chain(way, half_ring - 1, duo, piece).wait_recv()
            arrived = sums[0, half_ring, duo, rows, :] + sums[1, half_ring, duo, rows, :]
            out[duo, rows, :] = arrived + fresh[rows, :]
    lax.fori_loop(0, items, send_done, 0)
    for chunk in (2, 3):
        ports[chunk].finish_served()
    for n in range(len(peers)):
        ask(n).wait_send()
    for chunk in range(4):
        ports[chunk].finish_sends()


def pair_products(blocks, domains, coeff, planes):
    pair_dev, depth, slots = coeff.shape
    lines = 2 * RING * CORES
    wide = [widths(chunk)[1] for chunk in range(4)]
    half_cols = widths(0)[0] + widths(1)[0]
    bf16 = jnp.bfloat16
    scratch = [pltpu.VMEM((ATOMS, MAIN, w), bf16) for w in wide]
    scratch += [pltpu.VMEM((RING - 1, ATOMS, MAIN, w), bf16) for w in wide]
    scratch += [pltpu.VMEM((RING, CORES, PICKS, MAIN, w), bf16) for w in wide]
    scratch += [pltpu.VMEM((2, CORES, HALF, MAIN, w), bf16) for w in wide]
    scratch += [pltpu.VMEM((RING * CORES * PICKS, MAIN, w), bf16) for w in wide]
    scratch += [
        pltpu.VMEM((lines, 8, LANES), jnp.int32),
        pltpu.SMEM((lines, 8, LANES), jnp.int32),
        pltpu.VMEM((2, 8, LANES), jnp.int32),
        pltpu.SMEM((2, 8, LANES), jnp.int32),
        pltpu.VMEM((8, LANES), jnp.int32),
        pltpu.VMEM((16, LANES), jnp.int32),
        pltpu.VMEM((ATOMS * MAIN, ATOMS * MAIN), bf16),
        pltpu.VMEM((ATOMS * MAIN, ATOMS * MAIN), bf16),
        pltpu.VMEM((pair_dev, depth, slots), bf16),
        pltpu.VMEM((pair_dev, MAXPNO, DEPTH), bf16),
        pltpu.VMEM((DEPTH, depth), bf16),
        pltpu.VMEM((2, DEPTH, half_cols), bf16),
        pltpu.VMEM((pair_dev, MAXPNO, MAXPNO), jnp.float32),
        pltpu.VMEM((2, planes // 2 + 1, 2, DUO, LANES), jnp.float32),
        pltpu.VMEM((DUO, LANES), jnp.float32),
        pltpu.SemaphoreType.DMA((4, 16)),
        pltpu.SemaphoreType.DMA((4, 16)),
        pltpu.SemaphoreType.DMA((lines,)),
        pltpu.SemaphoreType.DMA((lines,)),
        pltpu.SemaphoreType.DMA((4,)),
        pltpu.SemaphoreType.DMA((2 * planes, 2)),
        pltpu.SemaphoreType.DMA((2 * planes, 2)),
    ]
    return pl.pallas_call(
        main_kernel,
        out_shape=jax.ShapeDtypeStruct((2, DUO, LANES), jnp.float32),
        in_specs=[
            pl.BlockSpec(memory_space=pltpu.VMEM),
            pl.BlockSpec(memory_space=pltpu.VMEM),
            pl.BlockSpec(memory_space=pl.ANY),
        ],
        out_specs=pl.BlockSpec(memory_space=pltpu.VMEM),
        scratch_shapes=scratch,
        compiler_params=params(60, collective_id=0, has_side_effects=True),
    )(blocks, domains, coeff)


def tail_kernel(counts, packed, amp, energy_row, energy_col, out, wide):
    slots = amp.shape[1]
    step = pl.program_id(0)
    row = lax.broadcasted_iota(jnp.int32, (SPLIT, LANES), 0)
    col = lax.broadcasted_iota(jnp.int32, (SPLIT, LANES), 1)
    low_row, low_col = row[:REST], col[:REST]
    full_row = lax.broadcasted_iota(jnp.int32, (slots, slots), 0)
    full_col = lax.broadcasted_iota(jnp.int32, (slots, slots), 1)
    for n in range(2):
        first = packed[0, :SPLIT, :]
        rest = packed[0, SPLIT + 2 * REST : SPLIT + 3 * REST, :]
        if n == 0:
            first = jnp.where(row >= col, first, 0.0)
            rest = jnp.where(low_row >= low_col, rest, 0.0)
        else:
            at = SPLIT + 3 * REST
            first = jnp.where(row < col, first, jnp.where(row == col, packed[0, at : at + 1, :], 0.0))
            rest = jnp.where((low_row < low_col) & (low_col < REST), rest, 0.0)
            rest = jnp.where(low_row == low_col, packed[0, at + 1 : at + 2, :], rest)
        wide[n, :SPLIT, :LANES] = first
        wide[n, :SPLIT, LANES:] = jnp.zeros((SPLIT, slots - LANES), jnp.float32)
        wide[n, SPLIT : SPLIT + REST, :LANES] = packed[0, SPLIT + n * REST : SPLIT + (n + 1) * REST, :]
        wide[n, SPLIT : SPLIT + REST, LANES:] = rest
        wide[n, MAXPNO:, :] = jnp.zeros((slots - MAXPNO, slots), jnp.float32)
    for n in range(2):
        count = counts[2 * step + n]
        held = wide[n]
        products = held + jnp.where(full_row == full_col, 0.0, held.T)
        valid = (full_row < count) & (full_col < count)
        products = jnp.where(valid, products / NAUX, 0.0)
        amps = amp[n]
        contract = (((1,), (1,)), ((), ()))
        high = products.astype(jnp.bfloat16)
        left = products - high.astype(jnp.float32)
        mid = left.astype(jnp.bfloat16)
        low = (left - mid.astype(jnp.float32)).astype(jnp.bfloat16)
        coupled = lax.dot_general(low, amps, contract, preferred_element_type=jnp.float32)
        coupled += lax.dot_general(mid, amps, contract, preferred_element_type=jnp.float32)
        coupled += lax.dot_general(high, amps, contract, preferred_element_type=jnp.float32)
        energies = energy_col[n] + energy_row[n]
        result = products + coupled + energies * amps.astype(jnp.float32)
        out[n] = jnp.where(valid, result, 0.0)


def tail(counts, packed, amp, energy):
    subs, slots, _ = amp.shape
    return pl.pallas_call(
        tail_kernel,
        out_shape=jax.ShapeDtypeStruct((subs, slots, slots), jnp.float32),
        grid=(subs // 2,),
        in_specs=[
            pl.BlockSpec(memory_space=pltpu.SMEM),
            pl.BlockSpec((1, DUO, LANES), lambda i: (i, 0, 0)),
            pl.BlockSpec((2, slots, slots), lambda i: (i, 0, 0)),
            pl.BlockSpec((2, 1, slots), lambda i: (i, 0, 0)),
            pl.BlockSpec((2, slots, 1), lambda i: (i, 0, 0)),
        ],
        out_specs=pl.BlockSpec((2, slots, slots), lambda i: (i, 0, 0)),
        scratch_shapes=[pltpu.VMEM((2, slots, slots), jnp.float32)],
        compiler_params=params(32),
    )(counts, packed, amp, energy[:, None, :], energy[:, :, None])


def on_device(atom_blocks, domains, pno_counts, pno_coeffs, amplitudes, pno_energies):
    lane_count = lax.axis_size("ri")
    pair_dev = domains.shape[0]
    mine = pair_products(atom_blocks.transpose(1, 0, 2), domains.T, pno_coeffs, lane_count)
    sub_count = pair_dev // lane_count
    start = lax.axis_index("ri") * sub_count
    counts_here = lax.dynamic_slice_in_dim(pno_counts, start, sub_count, 0)
    return tail(counts_here, mine, amplitudes, pno_energies)


def solution(mesh):
    placed = (
        P("pairs", None, "ri"),
        P("pairs", None),
        P("pairs"),
        P("pairs", None, None),
        P(("pairs", "ri"), None, None),
        P(("pairs", "ri"), None),
    )
    return jax.shard_map(
        on_device,
        mesh=mesh,
        in_specs=placed,
        out_specs=P(("pairs", "ri"), None, None),
        check_vma=False,
    )
```

```python
import jax
import jax.numpy as jnp
from jax import lax
from jax.experimental import pallas as pl
from jax.experimental.pallas import tpu as pltpu
from jax.sharding import PartitionSpec as P

NAUX = 14336
CAP = 3
MAXPNO = 200
MAIN = 16
REM = 4
SPLIT = 128
REST = MAXPNO - SPLIT
LANES = 128
MIB = 1 << 20
RING = 4
CORES = 2
ATOMS = 16
DOM = 12
BAND = MAIN + REM
PICKS = RING * CAP
HALF = PICKS // 2
DEPTH = 256
DUO = SPLIT + 3 * REST + 8
COUNTS = DUO - 6
SLOTS = 48
SHARE = SLOTS // CORES
HALF_SHARE = SHARE // 2
ROW_LINES = RING * CORES
MAINS = ((0, 1, 2), (3, 4, 5), (6, 7, 8), (10, 11, 12))
RESTS = ((0, 1, 2), (3, 4, 5), (6, 7, 8, 9), (10, 11, 12, 13))
SINGLES = (9, 13)
MESH = pl.DeviceIdType.MESH


def params(mib, **kw):
    return pltpu.CompilerParams(vmem_limit_bytes=mib * MIB, **kw)


class Ports:
    def __init__(self, chunk, gather_to, deliver_to, wire, ring, send, relay, recv, out_sems, in_sems, core):
        self.gather_to, self.deliver_to, self.core = gather_to, deliver_to, core
        self.wire, self.ring, self.send, self.relay, self.recv = wire, ring, send, relay, recv
        self.out_sems, self.in_sems, self.chunk = out_sems, in_sems, chunk

    def copy(self, src, dst, out_at, in_at, to):
        return pltpu.make_async_remote_copy(
            src_ref=src,
            dst_ref=dst,
            send_sem=self.out_sems.at[self.chunk, out_at],
            recv_sem=self.in_sems.at[self.chunk, in_at],
            device_id={"pairs": to},
            device_id_type=MESH,
        )

    def gather_first(self):
        up = self.copy(self.wire, self.ring.at[2], 0, 1, self.gather_to(1, self.core))
        down = self.copy(self.wire, self.ring.at[0], 1, 0, self.gather_to(3, self.core))
        return up, down

    def gather_second(self):
        half = ATOMS // 2
        low, high = pl.ds(0, half), pl.ds(half, half)
        up = self.copy(self.ring.at[2, low], self.ring.at[1, low], 2, 2, self.gather_to(1, self.core))
        down = self.copy(self.ring.at[0, high], self.ring.at[1, high], 3, 3, self.gather_to(3, self.core))
        return up, down

    def place(self, rel, core):
        return (rel * CORES + core) * PICKS

    def far(self):
        up = self.copy(self.send.at[2, :, pl.ds(0, HALF)], self.relay.at[0], 4, 4, self.deliver_to(1, self.core))
        down = self.copy(self.send.at[2, :, pl.ds(HALF, HALF)], self.relay.at[1], 5, 5, self.deliver_to(3, self.core))
        return up, down

    def near(self):
        copies = []
        for n, step in enumerate((1, 3)):
            for core in range(CORES):
                dst = self.recv.at[pl.ds(self.place(RING - step, self.core), PICKS)]
                at = 6 + 2 * n
                copies.append(self.copy(self.send.at[step, core], dst, at + core, at + self.core, self.deliver_to(step, core)))
        other = 1 - self.core
        dst = self.recv.at[pl.ds(self.place(0, self.core), PICKS)]
        copies.append(self.copy(self.send.at[0, other], dst, 10, 10, self.deliver_to(0, other)))
        return copies

    def own(self):
        return pltpu.make_async_copy(
            self.send.at[0, self.core],
            self.recv.at[pl.ds(self.place(0, self.core), PICKS)],
            self.in_sems.at[self.chunk, 11],
        )

    def onward(self):
        copies = []
        for way, step in enumerate((1, 3)):
            for core in range(CORES):
                dst = self.recv.at[pl.ds(self.place(2, self.core) + way * HALF, HALF)]
                at = 12 + 2 * way
                copies.append(self.copy(self.relay.at[way, core], dst, at + core, at + self.core, self.deliver_to(step, core)))
        return copies

    def start_gather(self):
        for copy in self.gather_first():
            copy.start()

    def forward_gather(self):
        up, down = self.gather_second()
        first_up, first_down = self.gather_first()
        first_up.wait_recv()
        up.start()
        first_down.wait_recv()
        down.start()

    def finish_gather(self):
        for copy in self.gather_second():
            copy.wait_recv()

    def start_delivery(self):
        for copy in self.far() + tuple(self.near()):
            copy.start()
        self.own().start()

    def forward_delivery(self):
        far, onward = self.far(), self.onward()
        for way in range(2):
            far[way].wait_recv()
            for copy in onward[2 * way : 2 * way + 2]:
                copy.start()

    def finish_delivery(self):
        for n, step in enumerate((1, 3)):
            for core in range(CORES):
                dst = self.recv.at[pl.ds(self.place(step, core), PICKS)]
                at = 6 + 2 * (1 - n)
                self.copy(dst, dst, at + core, at + core, self.deliver_to(1, self.core)).wait_recv()
        other = 1 - self.core
        dst = self.recv.at[pl.ds(self.place(0, other), PICKS)]
        self.copy(dst, dst, 10, 10, self.deliver_to(1, self.core)).wait_recv()
        self.own().wait()
        for way in range(2):
            for core in range(CORES):
                dst = self.recv.at[pl.ds(self.place(2, core) + way * HALF, HALF)]
                at = 12 + 2 * way
                self.copy(dst, dst, at + core, at + core, self.deliver_to(1, self.core)).wait_recv()

    def finish_served(self):
        for copy in self.far() + tuple(self.near()):
            copy.wait_send()

    def finish_sends(self):
        for copy in self.gather_first() + self.gather_second() + tuple(self.onward()):
            copy.wait_send()


class Relay:
    def __init__(self, chunk, first_to, other_to, u, v, core, bufs, out_sems, in_sems):
        self.chunk, self.first_to, self.other_to = chunk, first_to, other_to
        self.u, self.v, self.core = u, v, core
        self.wire, self.table, self.passing, self.send, self.relay, self.recv = bufs
        self.out_sems, self.in_sems = out_sems, in_sems

    def copy(self, src, dst, out_at, in_at, to):
        return pltpu.make_async_remote_copy(
            src_ref=src,
            dst_ref=dst,
            send_sem=self.out_sems.at[self.chunk, out_at],
            recv_sem=self.in_sems.at[self.chunk, in_at],
            device_id={"pairs": to},
            device_id_type=MESH,
        )

    def arrival(self, dst, at):
        return self.copy(dst, dst, at, at, self.first_to(1, self.core))

    def near_u(self, step):
        return lax.rem(self.u + step, RING)

    def near_v(self, step):
        return lax.rem(self.v + step, RING)

    def atoms(self, step, at=0, count=ATOMS):
        base = ((self.v * CORES + self.core) * RING + self.near_u(step)) * ATOMS
        return self.table.at[pl.ds(base + at, count)]

    def block(self, step, core, at=0, count=RING * ATOMS):
        return self.table.at[pl.ds((self.near_v(step) * CORES + core) * RING * ATOMS + at, count)]

    def spread_sends(self):
        half = ATOMS // 2
        far = self.near_u(2)
        up, down = self.first_to(1, self.core), self.first_to(3, self.core)
        return [
            self.copy(self.wire.at[far, pl.ds(0, half)], self.passing.at[0], 2, 2, up),
            self.copy(self.wire.at[far, pl.ds(half, half)], self.passing.at[1], 3, 3, down),
            self.copy(self.wire.at[self.near_u(1)], self.atoms(0), 0, 1, up),
            self.copy(self.wire.at[self.near_u(3)], self.atoms(0), 1, 0, down),
        ]

    def spread_own(self):
        return pltpu.make_async_copy(self.wire.at[self.u], self.atoms(0), self.in_sems.at[self.chunk, 25])

    def spread_onward(self):
        half = ATOMS // 2
        return [
            self.copy(self.passing.at[0], self.atoms(3, 0, half), 4, 4, self.first_to(1, self.core)),
            self.copy(self.passing.at[1], self.atoms(1, half, half), 5, 5, self.first_to(3, self.core)),
        ]

    def start_spread(self):
        for copy in self.spread_sends():
            copy.start()
        self.spread_own().start()

    def forward_spread(self):
        for way, copy in enumerate(self.spread_onward()):
            self.arrival(self.passing.at[way], 2 + way).wait_recv()
            copy.start()

    def finish_spread(self):
        half = ATOMS // 2
        self.spread_own().wait()
        self.arrival(self.atoms(1), 0).wait_recv()
        self.arrival(self.atoms(3), 1).wait_recv()
        self.arrival(self.atoms(2, 0, half), 4).wait_recv()
        self.arrival(self.atoms(2, half, half), 5).wait_recv()

    def gather_first(self):
        own = self.block(0, self.core)
        return [
            self.copy(own, own, 6, 7, self.other_to(1, self.core)),
            self.copy(own, own, 7, 6, self.other_to(3, self.core)),
        ]

    def gather_second(self):
        half = RING * ATOMS // 2
        low, high = self.block(3, self.core, 0, half), self.block(1, self.core, half, half)
        return [
            self.copy(low, low, 8, 8, self.other_to(1, self.core)),
            self.copy(high, high, 9, 9, self.other_to(3, self.core)),
        ]

    def share(self, step):
        mine = self.block(step, self.core)
        return self.copy(mine, mine, 10 + step, 10 + step, self.first_to(0, 1 - self.core))

    def start_gather(self):
        for copy in self.gather_first():
            copy.start()
        self.share(0).start()

    def forward_gather(self):
        low, high = self.gather_second()
        self.arrival(self.block(3, self.core), 7).wait_recv()
        low.start()
        self.share(3).start()
        self.arrival(self.block(1, self.core), 6).wait_recv()
        high.start()
        self.share(1).start()

    def finish_gather(self):
        half = RING * ATOMS // 2
        self.arrival(self.block(2, self.core, 0, half), 8).wait_recv()
        self.arrival(self.block(2, self.core, half, half), 9).wait_recv()
        self.share(2).start()

    def finish_share(self):
        for step in range(RING):
            self.arrival(self.block(step, 1 - self.core), 10 + step).wait_recv()

    def place(self, step, core, at=0, count=SHARE):
        return self.recv.at[self.near_u(step), pl.ds(core * SHARE + at, count)]

    def far(self):
        return [
            self.copy(self.send.at[2, :, pl.ds(0, HALF_SHARE)], self.relay.at[0], 19, 19, self.first_to(1, self.core)),
            self.copy(
                self.send.at[2, :, pl.ds(HALF_SHARE, HALF_SHARE)], self.relay.at[1], 20, 20, self.first_to(3, self.core)
            ),
        ]

    def near(self):
        copies = []
        dst = self.place(0, self.core)
        for n, step in enumerate((1, 3)):
            for core in range(CORES):
                at = 14 + 2 * n
                copies.append(self.copy(self.send.at[step, core], dst, at + core, at + self.core, self.first_to(step, core)))
        other = 1 - self.core
        copies.append(self.copy(self.send.at[0, other], dst, 18, 18, self.first_to(0, other)))
        return copies

    def own(self):
        return pltpu.make_async_copy(
            self.send.at[0, self.core], self.place(0, self.core), self.in_sems.at[self.chunk, 26]
        )

    def onward(self):
        copies = []
        for way, step in enumerate((1, 3)):
            dst = self.place(RING - step, self.core, way * HALF_SHARE, HALF_SHARE)
            for core in range(CORES):
                at = 21 + 2 * way
                copies.append(self.copy(self.relay.at[way, core], dst, at + core, at + self.core, self.first_to(step, core)))
        return copies

    def start_delivery(self):
        for copy in self.far() + self.near():
            copy.start()
        self.own().start()

    def forward_delivery(self):
        onward = self.onward()
        for way in range(2):
            self.arrival(self.relay.at[way], 19 + way).wait_recv()
            for copy in onward[2 * way : 2 * way + 2]:
                copy.start()

    def finish_delivery(self):
        for core in range(CORES):
            self.arrival(self.place(3, core), 14 + core).wait_recv()
            self.arrival(self.place(1, core), 16 + core).wait_recv()
            for way in range(2):
                at = 21 + 2 * way + core
                self.arrival(self.place(2, core, way * HALF_SHARE, HALF_SHARE), at).wait_recv()
        self.arrival(self.place(0, 1 - self.core), 18).wait_recv()
        self.own().wait()

    def finish_sends(self):
        copies = self.spread_sends() + self.spread_onward() + self.gather_first() + self.gather_second()
        copies += [self.share(step) for step in range(RING)] + self.far() + self.near() + self.onward()
        for copy in copies:
            copy.wait_send()


def main_kernel(
    blocks, domains, counts, coeff_hbm, out, *scratch
):
    relay_bufs = [scratch[4 * n : 4 * n + 4] for n in range(6)]
    single_bufs = [scratch[24 + 2 * n : 26 + 2 * n] for n in range(5)]
    wires, recvs = relay_bufs[0], relay_bufs[5]
    single_wires, single_recvs = single_bufs[0], single_bufs[4]
    asked, asked_smem, tables, places, request, ids, perm_main, perm_rest = scratch[34:42]
    coeff, coeff_t, perm, blk, total, sums, fresh, same = scratch[42:50]
    out_sems, in_sems, single_out, single_in, ask_out, ask_in, local_sems, sum_out, sum_in = scratch[50:59]
    me = lax.axis_index("pairs")
    at_z = lax.axis_index("ri")
    planes = 2 * (sums.shape[1] - 1)
    above, below = lax.rem(at_z + 1, planes), lax.rem(at_z + planes - 1, planes)
    core = lax.rem(me, CORES)
    chip = lax.div(me, CORES)
    at_x = lax.rem(chip, RING)
    at_y = lax.div(chip, RING)

    def along_x(step, to_core):
        return (at_y * RING + lax.rem(at_x + step, RING)) * CORES + to_core

    def along_y(step, to_core):
        return (lax.rem(at_y + step, RING) * RING + at_x) * CORES + to_core

    peers = []
    for to_core in range(2):
        for step in range(1, RING):
            peers.append((along_y(step, to_core), step * CORES + to_core, (RING - step) * CORES + core))
            peers.append(
                (along_x(step, to_core), (RING + step) * CORES + to_core, (2 * RING - step) * CORES + core)
            )
    peers.append((along_x(0, 1 - core), 1 - core, core))

    fetch = pltpu.make_async_copy(coeff_hbm, coeff, local_sems.at[0])
    fetch.start()
    barrier = pltpu.get_barrier_semaphore()
    for peer, _, _ in peers:
        pl.semaphore_signal(barrier, inc=1, device_id={"pairs": peer}, device_id_type=MESH)
    for plane in (above, below):
        pl.semaphore_signal(barrier, inc=1, device_id={"ri": plane}, device_id_type=MESH)

    def ask(n):
        peer, _, there = peers[n]
        return pltpu.make_async_remote_copy(
            src_ref=request,
            dst_ref=asked.at[there],
            send_sem=ask_out.at[n],
            recv_sem=ask_in.at[there],
            device_id={"pairs": peer},
            device_id_type=MESH,
        )

    ports = []
    for chunk in range(4):
        by_x = chunk % 2 == 0
        first_to, other_to = (along_x, along_y) if by_x else (along_y, along_x)
        u, v = (at_x, at_y) if by_x else (at_y, at_x)
        bufs = [group_bufs[chunk] for group_bufs in relay_bufs]
        ports.append(Relay(chunk, first_to, other_to, u, v, core, bufs, out_sems, in_sems))
    singles = []
    for n in range(2):
        gather_to, deliver_to = (along_x, along_y) if n == 0 else (along_y, along_x)
        bufs = [group_bufs[n] for group_bufs in single_bufs]
        singles.append(Ports(n, gather_to, deliver_to, *bufs, single_out, single_in, core))

    square = (ATOMS * MAIN, ATOMS * MAIN)
    out_at = lax.broadcasted_iota(jnp.int32, square, 0)
    from_at = lax.broadcasted_iota(jnp.int32, square, 1)
    band_at, atom_at = out_at & (MAIN - 1), lax.shift_right_logical(out_at, 4)
    perm_main[...] = jnp.where(band_at * ATOMS + atom_at == from_at, 1.0, 0.0).astype(jnp.bfloat16)
    rest_at = lax.shift_right_logical(band_at, 2) * (REM * ATOMS) + (band_at & (REM - 1)) * ATOMS + atom_at
    perm_rest[...] = jnp.where(rest_at == from_at, 1.0, 0.0).astype(jnp.bfloat16)

    def main_rows(tiles):
        flat = blocks[:MAIN, :, tiles[0] * LANES : (tiles[-1] + 1) * LANES]
        flat = flat.reshape(MAIN * ATOMS, len(tiles) * LANES)
        return jnp.dot(perm_main[...], flat, preferred_element_type=jnp.float32).astype(jnp.bfloat16)

    def form(chunk):
        main = main_rows(MAINS[chunk])
        for n in range(len(MAINS[chunk])):
            wires[chunk][n] = main[:, n * LANES : (n + 1) * LANES].reshape(ATOMS, MAIN, LANES)
        parts = [blocks[MAIN:, :, t * LANES : (t + 1) * LANES].reshape(REM * ATOMS, LANES) for t in RESTS[chunk]]
        stacked = jnp.concatenate(parts, axis=0)
        depth = stacked.shape[0]
        late = jnp.dot(perm_rest[:, :depth], stacked, preferred_element_type=jnp.float32).astype(jnp.bfloat16)
        wires[chunk][RING - 1] = late.reshape(ATOMS, MAIN, LANES)

    form(0)
    pl.semaphore_wait(barrier, len(peers) + 2)
    ports[0].start_spread()
    for chunk in range(1, 4):
        form(chunk)
        ports[chunk].start_spread()
    for n in range(2):
        single_wires[n][...] = main_rows(SINGLES[n : n + 1]).reshape(ATOMS, MAIN, LANES)
    for chunk in (0, 1):
        ports[chunk].forward_spread()
    for chunk in (0, 1):
        ports[chunk].finish_spread()
        ports[chunk].start_gather()

    ids[...] = jnp.zeros_like(ids)
    pairs = domains.shape[1]
    fold = LANES // pairs
    ids[: domains.shape[0], :pairs] = domains[...]
    held = ids[...]
    lane = lax.broadcasted_iota(jnp.int32, held.shape, 1)
    turned = [held if n == 0 else pltpu.roll(held, n * pairs, 1) for n in range(fold)]
    lines = []
    for line in range(DOM // fold):
        row = jnp.zeros((1, LANES), jnp.int32)
        for n in range(fold):
            k = line * fold + n
            row = jnp.where(lane[:1] // pairs == n, turned[n][k : k + 1], row)
        lines.append(row)
    flat_shape = (ATOMS * RING * RING * CORES, LANES)
    atom = lax.broadcasted_iota(jnp.int32, flat_shape, 0)
    lane_at = lax.broadcasted_iota(jnp.int32, flat_shape, 1)
    named = jnp.zeros(flat_shape, jnp.int32)
    for line in lines:
        named = jnp.where(atom == line, 1, named)
    named = jnp.broadcast_to(jnp.max(named, axis=1, keepdims=True), flat_shape)
    local = atom & (ATOMS - 1)
    owner = lax.shift_right_logical(atom, 4)
    rank = named
    for shift in (1, 2, 4, 8):
        rank = rank + jnp.where(local >= shift, pltpu.roll(rank, shift, 0), 0)
    order = named
    for shift in (1, 2, 4, 8, 16, 32, 64, 128, 256):
        order = order + jnp.where(atom >= shift, pltpu.roll(order, shift, 0), 0)
    own_lane = jnp.where((owner == lane_at) & (named > 0), local, 0)
    for j in range(CAP):
        request[j : j + 1, :] = jnp.sum(jnp.where(rank == j + 1, own_lane, 0), axis=0, keepdims=True)
    owner_chip = lax.shift_right_logical(owner, 1)
    owner_core = owner & (CORES - 1)
    owner_x, owner_y = owner_chip & (RING - 1), lax.shift_right_logical(owner_chip, 2)
    taken = (order == lane_at + 1) & (named > 0)
    for n, (u, v) in enumerate(((owner_x, owner_y), (owner_y, owner_x))):
        held_at = ((v * CORES + owner_core) * RING + u) * ATOMS + local
        request[CAP + n : CAP + n + 1, :] = jnp.sum(jnp.where(taken, held_at, 0), axis=0, keepdims=True)
    request[CAP + 2 :, :] = jnp.zeros((6 - CAP, LANES), jnp.int32)

    for n in range(len(peers)):
        ask(n).start()
    own_ask = pltpu.make_async_copy(request, asked.at[core], local_sems.at[1])
    own_ask.start()

    for chunk in (2, 3):
        ports[chunk].forward_spread()
    for chunk in (2, 3):
        ports[chunk].finish_spread()
    for chunk in (0, 1):
        ports[chunk].forward_gather()
    for chunk in (2, 3):
        ports[chunk].start_gather()

    rel_x = (owner_x + RING - at_x) & (RING - 1)
    rel_y = (owner_y + RING - at_y) & (RING - 1)
    place_x = ((rel_y * CORES + owner_core) * RING + rel_x) * CAP + rank - 1
    place_y = ((rel_x * CORES + owner_core) * RING + rel_y) * CAP + rank - 1
    tables[...] = jnp.zeros_like(tables)
    for n, line in enumerate(lines):
        for table, place in enumerate((order - 1, place_x, place_y)):
            tables[table, n : n + 1, :] = jnp.sum(jnp.where(atom == line, place, 0), axis=0, keepdims=True)
    table_copy = pltpu.make_async_copy(tables, places, local_sems.at[3])
    table_copy.start()
    table_copy.wait()

    shape = (DEPTH, DOM * BAND)
    row = lax.broadcasted_iota(jnp.int32, shape, 0)
    col = lax.broadcasted_iota(jnp.int32, shape, 1)
    split = DOM * MAIN
    late = row - split
    source = jnp.where(
        row < split,
        (row // MAIN) * BAND + row % MAIN,
        (late // REM) * BAND + MAIN + late % REM,
    )
    perm[...] = jnp.where((source == col) & (row < DOM * BAND), 1.0, 0.0).astype(jnp.bfloat16)
    same[...] = jnp.where(
        lax.broadcasted_iota(jnp.int32, same.shape, 0) == lax.broadcasted_iota(jnp.int32, same.shape, 1), 1.0, 0.0
    ).astype(jnp.bfloat16)
    for n in range(2):
        blk[n, DOM * BAND :, :] = jnp.zeros((DEPTH - DOM * BAND, blk.shape[2]), jnp.bfloat16)
    fetch.wait()

    def prepare(begin, end):
        def turn(pair, _):
            ordered = [
                jnp.dot(perm[...], coeff[4 * pair + n], preferred_element_type=jnp.float32).astype(jnp.bfloat16)
                for n in range(4)
            ]
            for n in range(4):
                turned = lax.dot_general(
                    same[...], ordered[n], (((1,), (1,)), ((), ())), preferred_element_type=jnp.float32
                )
                coeff_t[4 * pair + n] = turned.astype(jnp.bfloat16)
            return 0

        lax.fori_loop(begin // 4, end // 4, turn, 0)

    half_pairs = coeff.shape[0] // 2
    quarter = half_pairs // 2
    for single in singles:
        single.start_gather()
    prepare(0, quarter)

    own_ask.wait()
    for n in range(len(peers)):
        _, here, _ = peers[n]
        pltpu.make_async_remote_copy(
            src_ref=request,
            dst_ref=asked.at[here],
            send_sem=ask_out.at[n],
            recv_sem=ask_in.at[here],
            device_id={"pairs": peers[n][0]},
            device_id_type=MESH,
        ).wait_recv()
    to_smem = pltpu.make_async_copy(asked, asked_smem, local_sems.at[2])
    to_smem.start()
    to_smem.wait()

    def line_of(dest, on_row):
        return jnp.where(dest < CORES, dest, dest + ROW_LINES) if on_row else dest

    def pick_single(n):
        port = singles[n]
        owner_of = along_x if n == 0 else along_y

        def serve(dest, _):
            line = line_of(dest, n == 1)
            step, to_core = dest // CORES, dest % CORES
            for r in range(RING):
                for j in range(CAP):
                    atom = asked_smem[line, j, owner_of(r, core)]
                    found = port.wire[atom] if r == 0 else port.ring[r - 1, atom]
                    port.send[step, to_core, r * CAP + j] = found
            return 0

        lax.fori_loop(0, RING * CORES, serve, 0)

    def pick(chunk):
        port = ports[chunk]

        def serve(dest, _):
            line = line_of(dest, chunk % 2 == 0)
            step, to_core = dest // CORES, dest % CORES
            for n in range(SHARE):
                port.send[step, to_core, n] = port.table[asked_smem[line, CAP + chunk % 2, core * SHARE + n]]
            return 0

        lax.fori_loop(0, RING * CORES, serve, 0)

    for chunk in (0, 1):
        ports[chunk].finish_gather()
    for chunk in (0, 1):
        ports[chunk].finish_share()
        pick(chunk)
        ports[chunk].start_delivery()
    for chunk in (2, 3):
        ports[chunk].forward_gather()
    for single in singles:
        single.forward_gather()
    prepare(quarter, half_pairs)
    for chunk in (0, 1):
        ports[chunk].forward_delivery()
    for chunk in (2, 3):
        ports[chunk].finish_gather()
    for n in range(2):
        singles[n].finish_gather()
        pick_single(n)
        singles[n].start_delivery()
    for chunk in (2, 3):
        ports[chunk].finish_share()
        pick(chunk)
        ports[chunk].start_delivery()
    for single in singles:
        single.forward_delivery()
    prepare(half_pairs, 2 * half_pairs)

    pack_row = lax.broadcasted_iota(jnp.int32, (SPLIT, LANES), 0)
    pack_col = lax.broadcasted_iota(jnp.int32, (SPLIT, LANES), 1)
    rest_row = lax.broadcasted_iota(jnp.int32, (REST, REST), 0)
    rest_col = lax.broadcasted_iota(jnp.int32, (REST, REST), 1)

    def assemble(pair, slot, chunks):
        base = MAIN * DOM
        begin = 0
        upper = lax.broadcasted_iota(jnp.int32, (8, LANES), 0) < REM

        def named_at(table):
            return [places[table, k // fold, (k % fold) * pairs + pair] for k in range(DOM)]

        at = named_at(0)
        for chunk in chunks:
            tiles = len(RESTS[chunk])
            for n in range(RING - 1):
                span = slice(begin + n * LANES, begin + (n + 1) * LANES)
                for k in range(DOM):
                    blk[slot, MAIN * k : MAIN * (k + 1), span] = recvs[chunk][n, at[k]]
            if tiles == RING:
                span = slice(begin + (RING - 1) * LANES, begin + RING * LANES)
                single_at = named_at(1 + chunk % 2)
                for k in range(DOM):
                    blk[slot, MAIN * k : MAIN * (k + 1), span] = single_recvs[chunk % 2][single_at[k]]
            for k in range(0, DOM, 4):
                rest = [recvs[chunk][RING - 1, at[k + n]].astype(jnp.float32) for n in range(4)]
                for half in range((tiles + 1) // 2):
                    parts = [r[8 * half : 8 * half + 8] for r in rest]
                    shifted = [pltpu.roll(part, REM, 0) for part in parts]
                    for q in range(2 * half, min(2 * half + 2, tiles)):
                        first, second = (parts, shifted) if q % 2 == 0 else (shifted, parts)
                        low = jnp.where(upper, first[0], second[1])
                        high = jnp.where(upper, first[2], second[3])
                        both = jnp.concatenate([low, high], axis=0).astype(jnp.bfloat16)
                        tile = slice(begin + q * LANES, begin + (q + 1) * LANES)
                        blk[slot, base + REM * k : base + REM * (k + 4), tile] = both
            begin += tiles * LANES
        return begin

    def multiply(pair, slot, cols):
        weights = coeff_t[pair]
        result = jnp.zeros((MAXPNO, MAXPNO), jnp.float32)
        for at in range(0, cols, 256):
            vec = jnp.dot(weights, blk[slot, :, at : at + 256], preferred_element_type=jnp.float32)
            vec = vec.astype(jnp.bfloat16)
            result += lax.dot_general(vec, vec, (((1,), (1,)), ((), ())), preferred_element_type=jnp.float32)
        return result

    def first_half(step, _):
        pair = 2 * step
        assemble(pair + 1, 1, (0, 1))
        total[pair] = multiply(pair, 0, early_cols)
        assemble(jnp.minimum(pair + 2, coeff.shape[0] - 1), 0, (0, 1))
        total[pair + 1] = multiply(pair + 1, 1, early_cols)
        return 0

    early_cols = LANES * (len(RESTS[0]) + len(RESTS[1]))
    late_cols = LANES * (len(RESTS[2]) + len(RESTS[3]))
    group = coeff.shape[0] // planes
    half_ring = planes // 2
    part = DUO // 2

    def chain(way, step, duo, piece):
        rows = pl.ds(piece * part, part)
        return pltpu.make_async_remote_copy(
            src_ref=sums.at[way, step, duo, rows],
            dst_ref=sums.at[way, step + 1, duo, rows],
            send_sem=sum_out.at[(way * half_ring + step) * 2 + duo, piece],
            recv_sem=sum_in.at[(way * half_ring + step) * 2 + duo, piece],
            device_id={"ri": jnp.where(way == 0, above, below)},
            device_id_type=MESH,
        )

    sends = 2 + 4 * (half_ring - 1)

    def locate(item):
        later = jnp.clip(item - 2, 0, sends - 3)
        turn = later % 4
        opening = item < 2
        step = jnp.where(opening, 0, 1 + later // 4)
        way = jnp.where(opening, item, turn % 2)
        early = jnp.logical_and(jnp.logical_not(opening), turn < 2)
        duo = jnp.where(early, 1 - way, way)
        away = jnp.where(way == 0, half_ring - step, half_ring + step)
        mine = item >= sends
        duo = jnp.where(mine, jnp.minimum(item - sends, 1), duo)
        owner = jnp.where(mine, at_z, lax.rem(at_z + away, planes))
        alone = jnp.logical_or(opening, jnp.logical_and(early, step == 1))
        return step, way, duo, owner * group + 2 * duo, alone

    def second_half(item):
        first, following = locate(item)[3], locate(item + 1)[3]
        assemble(first + 1, 1, (2, 3))
        whole = [total[first] + multiply(first, 0, late_cols)]
        assemble(following, 0, (2, 3))
        whole.append(total[first + 1] + multiply(first + 1, 1, late_cols))
        here, there = [w[:SPLIT, :SPLIT] for w in whole]
        fresh[:SPLIT, :] = jnp.where(pack_row >= pack_col, here, there)
        for n in range(2):
            fresh[SPLIT + n * REST : SPLIT + (n + 1) * REST, :] = whole[n][SPLIT:, :SPLIT]
        at = SPLIT + 2 * REST
        low_here, low_there = [w[SPLIT:, SPLIT:] for w in whole]
        fresh[at : at + REST, :REST] = jnp.where(rest_row >= rest_col, low_here, low_there)
        at += REST
        fresh[at : at + 1, :] = jnp.sum(jnp.where(pack_row == pack_col, there, 0.0), axis=0, keepdims=True)
        fresh[at + 1 : at + 2, :REST] = jnp.sum(
            jnp.where(rest_row == rest_col, low_there, 0.0), axis=0, keepdims=True
        )

    def send_on(item, _):
        step, way, duo, _, alone = locate(item)
        second_half(item)

        @pl.when(alone)
        def _():
            sums[way, step, duo] = fresh[...]
            for piece in range(2):
                chain(way, step, duo, piece).start()

        @pl.when(jnp.logical_not(alone))
        def _():
            for piece in range(2):
                rows = slice(piece * part, (piece + 1) * part)
                chain(way, step - 1, duo, piece).wait_recv()
                sums[way, step, duo, rows, :] = sums[way, step, duo, rows, :] + fresh[rows, :]
                chain(way, step, duo, piece).start()

        return 0

    def send_done(item, _):
        step, way, duo, _, _ = locate(item)
        for piece in range(2):
            chain(way, step, duo, piece).wait_send()
        return 0

    ports[0].finish_delivery()
    ports[1].finish_delivery()
    assemble(0, 0, (0, 1))
    lax.fori_loop(0, half_pairs // 4, first_half, 0)
    ports[2].forward_delivery()
    ports[3].forward_delivery()
    lax.fori_loop(half_pairs // 4, half_pairs, first_half, 0)
    for single in singles:
        single.finish_delivery()
    ports[2].finish_delivery()
    ports[3].finish_delivery()
    fresh[...] = jnp.zeros_like(fresh)
    assemble(locate(0)[3], 0, (2, 3))
    lax.fori_loop(0, sends, send_on, 0)
    for duo in range(2):
        second_half(sends + duo)
        for piece in range(2):
            rows = slice(piece * part, (piece + 1) * part)
            for way in range(2):
                chain(way, half_ring - 1, duo, piece).wait_recv()
            arrived = sums[0, half_ring, duo, rows, :] + sums[1, half_ring, duo, rows, :]
            out[duo, rows, :] = arrived + fresh[rows, :]
        for n in range(2):
            count = counts[at_z * group + 2 * duo + n].astype(jnp.float32)
            out[duo, COUNTS + n : COUNTS + n + 1, :] = jnp.full((1, LANES), count)
    lax.fori_loop(0, sends, send_done, 0)
    for n in range(len(peers)):
        ask(n).wait_send()
    for port in ports:
        port.finish_sends()
    for single in singles:
        single.finish_served()
        single.finish_sends()


def pair_products(blocks, domains, counts, coeff, planes):
    pair_dev, depth, slots = coeff.shape
    lines = 2 * RING * CORES
    half_cols = RING * LANES * 2
    bf16 = jnp.bfloat16
    tile = (MAIN, LANES)
    scratch = []
    for shape in (
        (RING, ATOMS),
        (RING * RING * CORES * ATOMS,),
        (2, ATOMS // 2),
        (RING, CORES, SHARE),
        (2, CORES, HALF_SHARE),
        (RING, SLOTS),
    ):
        scratch += [pltpu.VMEM(shape + tile, bf16)] * 4
    for shape in (
        (ATOMS,),
        (RING - 1, ATOMS),
        (RING, CORES, PICKS),
        (2, CORES, HALF),
        (RING * CORES * PICKS,),
    ):
        scratch += [pltpu.VMEM(shape + tile, bf16)] * 2
    scratch += [
        pltpu.VMEM((lines, 8, LANES), jnp.int32),
        pltpu.SMEM((lines, 8, LANES), jnp.int32),
        pltpu.VMEM((3, 8, LANES), jnp.int32),
        pltpu.SMEM((3, 8, LANES), jnp.int32),
        pltpu.VMEM((8, LANES), jnp.int32),
        pltpu.VMEM((16, LANES), jnp.int32),
        pltpu.VMEM((ATOMS * MAIN, ATOMS * MAIN), bf16),
        pltpu.VMEM((ATOMS * MAIN, ATOMS * MAIN), bf16),
        pltpu.VMEM((pair_dev, depth, slots), bf16),
        pltpu.VMEM((pair_dev, MAXPNO, DEPTH), bf16),
        pltpu.VMEM((DEPTH, depth), bf16),
        pltpu.VMEM((2, DEPTH, half_cols), bf16),
        pltpu.VMEM((pair_dev, MAXPNO, MAXPNO), jnp.float32),
        pltpu.VMEM((2, planes // 2 + 1, 2, DUO, LANES), jnp.float32),
        pltpu.VMEM((DUO, LANES), jnp.float32),
        pltpu.VMEM((MAXPNO, slots), bf16),
        pltpu.SemaphoreType.DMA((4, 27)),
        pltpu.SemaphoreType.DMA((4, 27)),
        pltpu.SemaphoreType.DMA((2, 16)),
        pltpu.SemaphoreType.DMA((2, 16)),
        pltpu.SemaphoreType.DMA((lines,)),
        pltpu.SemaphoreType.DMA((lines,)),
        pltpu.SemaphoreType.DMA((4,)),
        pltpu.SemaphoreType.DMA((2 * planes, 2)),
        pltpu.SemaphoreType.DMA((2 * planes, 2)),
    ]
    return pl.pallas_call(
        main_kernel,
        out_shape=jax.ShapeDtypeStruct((2, DUO, LANES), jnp.float32),
        in_specs=[
            pl.BlockSpec(memory_space=pltpu.VMEM),
            pl.BlockSpec(memory_space=pltpu.VMEM),
            pl.BlockSpec(memory_space=pltpu.SMEM),
            pl.BlockSpec(memory_space=pl.ANY),
        ],
        out_specs=pl.BlockSpec(memory_space=pltpu.VMEM),
        scratch_shapes=scratch,
        compiler_params=params(60, collective_id=0, has_side_effects=True),
    )(blocks, domains, counts, coeff)


def tail_kernel(packed, amp, energy_row, energy_col, out, wide):
    slots = amp.shape[1]
    step = pl.program_id(0)
    row = lax.broadcasted_iota(jnp.int32, (SPLIT, LANES), 0)
    col = lax.broadcasted_iota(jnp.int32, (SPLIT, LANES), 1)
    low_row, low_col = row[:REST], col[:REST]
    full_row = lax.broadcasted_iota(jnp.int32, (slots, slots), 0)
    full_col = lax.broadcasted_iota(jnp.int32, (slots, slots), 1)
    for n in range(2):
        first = packed[0, :SPLIT, :]
        rest = packed[0, SPLIT + 2 * REST : SPLIT + 3 * REST, :]
        if n == 0:
            first = jnp.where(row >= col, first, 0.0)
            rest = jnp.where(low_row >= low_col, rest, 0.0)
        else:
            at = SPLIT + 3 * REST
            first = jnp.where(row < col, first, jnp.where(row == col, packed[0, at : at + 1, :], 0.0))
            rest = jnp.where((low_row < low_col) & (low_col < REST), rest, 0.0)
            rest = jnp.where(low_row == low_col, packed[0, at + 1 : at + 2, :], rest)
        wide[n, :SPLIT, :LANES] = first
        wide[n, :SPLIT, LANES:] = jnp.zeros((SPLIT, slots - LANES), jnp.float32)
        wide[n, SPLIT : SPLIT + REST, :LANES] = packed[0, SPLIT + n * REST : SPLIT + (n + 1) * REST, :]
        wide[n, SPLIT : SPLIT + REST, LANES:] = rest
        wide[n, MAXPNO:, :] = jnp.zeros((slots - MAXPNO, slots), jnp.float32)
    for n in range(2):
        count = packed[0, COUNTS + n : COUNTS + n + 1, :1].astype(jnp.int32)
        held = wide[n]
        products = held + jnp.where(full_row == full_col, 0.0, held.T)
        valid = (full_row < count) & (full_col < count)
        products = jnp.where(valid, products / NAUX, 0.0)
        amps = amp[n]
        contract = (((1,), (1,)), ((), ()))
        high = products.astype(jnp.bfloat16)
        left = products - high.astype(jnp.float32)
        mid = left.astype(jnp.bfloat16)
        low = (left - mid.astype(jnp.float32)).astype(jnp.bfloat16)
        coupled = lax.dot_general(low, amps, contract, preferred_element_type=jnp.float32)
        coupled += lax.dot_general(mid, amps, contract, preferred_element_type=jnp.float32)
        coupled += lax.dot_general(high, amps, contract, preferred_element_type=jnp.float32)
        energies = energy_col[n] + energy_row[pl.ds(2 * step + n, 1), :]
        result = products + coupled + energies * amps.astype(jnp.float32)
        out[n] = jnp.where(valid, result, 0.0)


def tail(packed, amp, energy):
    subs, slots, _ = amp.shape
    return pl.pallas_call(
        tail_kernel,
        out_shape=jax.ShapeDtypeStruct((subs, slots, slots), jnp.float32),
        grid=(subs // 2,),
        in_specs=[
            pl.BlockSpec((1, DUO, LANES), lambda i: (i, 0, 0)),
            pl.BlockSpec((2, slots, slots), lambda i: (i, 0, 0)),
            pl.BlockSpec((subs, slots), lambda i: (0, 0)),
            pl.BlockSpec((2, slots, 1), lambda i: (i, 0, 0)),
        ],
        out_specs=pl.BlockSpec((2, slots, slots), lambda i: (i, 0, 0)),
        scratch_shapes=[pltpu.VMEM((2, slots, slots), jnp.float32)],
        compiler_params=params(32),
    )(packed, amp, energy, energy[:, :, None])


def on_device(atom_blocks, domains, pno_counts, pno_coeffs, amplitudes, pno_energies):
    planes = lax.axis_size("ri")
    mine = pair_products(atom_blocks.transpose(1, 0, 2), domains.T, pno_counts, pno_coeffs, planes)
    return tail(mine, amplitudes, pno_energies)


def solution(mesh):
    placed = (
        P("pairs", None, "ri"),
        P("pairs", None),
        P("pairs"),
        P("pairs", None, None),
        P(("pairs", "ri"), None, None),
        P(("pairs", "ri"), None),
    )
    return jax.shard_map(
        on_device,
        mesh=mesh,
        in_specs=placed,
        out_specs=P(("pairs", "ri"), None, None),
        check_vma=False,
    )
```

```python
import functools

import jax
import jax.numpy as jnp
from jax import lax
from jax.experimental import pallas as pl
from jax.experimental.pallas import tpu as pltpu
from jax.sharding import PartitionSpec as P

NAUX = 14336
CAP = 3
MAXPNO = 200
MAIN = 16
REM = 4
SPLIT = 128
REST = MAXPNO - SPLIT
LANES = 128
MIB = 1 << 20
RING = 4
CORES = 2
ATOMS = 16
DOM = 12
BAND = MAIN + REM
PICKS = RING * CAP
HALF = PICKS // 2
DEPTH = 256
SPARE = LANES - REST
LEFT = REST - SPARE
FOLD_ROWS = 32
HALF_PACK = 320
PACK = 2 * HALF_PACK
TOP = HALF_PACK - MAXPNO
FOLD_AT = PACK - FOLD_ROWS - 8
DIAG_AT = PACK - 8
COUNTS = PACK - 4
SQUARE_ROWS = 224
SLOTS = 48
SHARE = SLOTS // CORES
HALF_SHARE = SHARE // 2
ROW_LINES = RING * CORES
MAINS = ((0, 1, 2), (3, 4, 5), (6, 7, 8), (10, 11, 12))
RESTS = ((0, 1, 2), (3, 4, 5), (6, 7, 8, 9), (10, 11, 12, 13))
SINGLES = (9, 13)
MESH = pl.DeviceIdType.MESH


def params(mib, **kw):
    return pltpu.CompilerParams(vmem_limit_bytes=mib * MIB, **kw)


class Ports:
    def __init__(self, chunk, gather_to, deliver_to, wire, ring, send, relay, recv, out_sems, in_sems, core):
        self.gather_to, self.deliver_to, self.core = gather_to, deliver_to, core
        self.wire, self.ring, self.send, self.relay, self.recv = wire, ring, send, relay, recv
        self.out_sems, self.in_sems, self.chunk = out_sems, in_sems, chunk

    def copy(self, src, dst, out_at, in_at, to):
        return pltpu.make_async_remote_copy(
            src_ref=src,
            dst_ref=dst,
            send_sem=self.out_sems.at[self.chunk, out_at],
            recv_sem=self.in_sems.at[self.chunk, in_at],
            device_id={"pairs": to},
            device_id_type=MESH,
        )

    def gather_first(self):
        up = self.copy(self.wire, self.ring.at[2], 0, 1, self.gather_to(1, self.core))
        down = self.copy(self.wire, self.ring.at[0], 1, 0, self.gather_to(3, self.core))
        return up, down

    def gather_second(self):
        half = ATOMS // 2
        low, high = pl.ds(0, half), pl.ds(half, half)
        up = self.copy(self.ring.at[2, low], self.ring.at[1, low], 2, 2, self.gather_to(1, self.core))
        down = self.copy(self.ring.at[0, high], self.ring.at[1, high], 3, 3, self.gather_to(3, self.core))
        return up, down

    def place(self, rel, core):
        return (rel * CORES + core) * PICKS

    def far(self):
        up = self.copy(self.send.at[2, :, pl.ds(0, HALF)], self.relay.at[0], 4, 4, self.deliver_to(1, self.core))
        down = self.copy(self.send.at[2, :, pl.ds(HALF, HALF)], self.relay.at[1], 5, 5, self.deliver_to(3, self.core))
        return up, down

    def near(self):
        copies = []
        for n, step in enumerate((1, 3)):
            for core in range(CORES):
                dst = self.recv.at[pl.ds(self.place(RING - step, self.core), PICKS)]
                at = 6 + 2 * n
                copies.append(self.copy(self.send.at[step, core], dst, at + core, at + self.core, self.deliver_to(step, core)))
        other = 1 - self.core
        dst = self.recv.at[pl.ds(self.place(0, self.core), PICKS)]
        copies.append(self.copy(self.send.at[0, other], dst, 10, 10, self.deliver_to(0, other)))
        return copies

    def own(self):
        return pltpu.make_async_copy(
            self.send.at[0, self.core],
            self.recv.at[pl.ds(self.place(0, self.core), PICKS)],
            self.in_sems.at[self.chunk, 11],
        )

    def onward(self):
        copies = []
        for way, step in enumerate((1, 3)):
            for core in range(CORES):
                dst = self.recv.at[pl.ds(self.place(2, self.core) + way * HALF, HALF)]
                at = 12 + 2 * way
                copies.append(self.copy(self.relay.at[way, core], dst, at + core, at + self.core, self.deliver_to(step, core)))
        return copies

    def start_gather(self):
        for copy in self.gather_first():
            copy.start()

    def forward_gather(self):
        up, down = self.gather_second()
        first_up, first_down = self.gather_first()
        first_up.wait_recv()
        up.start()
        first_down.wait_recv()
        down.start()

    def finish_gather(self):
        for copy in self.gather_second():
            copy.wait_recv()

    def start_far(self):
        for copy in self.far():
            copy.start()

    def start_near(self):
        for copy in self.near():
            copy.start()
        self.own().start()

    def forward_delivery(self):
        far, onward = self.far(), self.onward()
        for way in range(2):
            far[way].wait_recv()
            for copy in onward[2 * way : 2 * way + 2]:
                copy.start()

    def finish_delivery(self):
        for n, step in enumerate((1, 3)):
            for core in range(CORES):
                dst = self.recv.at[pl.ds(self.place(step, core), PICKS)]
                at = 6 + 2 * (1 - n)
                self.copy(dst, dst, at + core, at + core, self.deliver_to(1, self.core)).wait_recv()
        other = 1 - self.core
        dst = self.recv.at[pl.ds(self.place(0, other), PICKS)]
        self.copy(dst, dst, 10, 10, self.deliver_to(1, self.core)).wait_recv()
        self.own().wait()
        for way in range(2):
            for core in range(CORES):
                dst = self.recv.at[pl.ds(self.place(2, core) + way * HALF, HALF)]
                at = 12 + 2 * way
                self.copy(dst, dst, at + core, at + core, self.deliver_to(1, self.core)).wait_recv()

    def finish_served(self):
        for copy in self.far() + tuple(self.near()):
            copy.wait_send()

    def finish_sends(self):
        for copy in self.gather_first() + self.gather_second() + tuple(self.onward()):
            copy.wait_send()


class Relay:
    def __init__(self, chunk, first_to, other_to, u, v, core, bufs, out_sems, in_sems):
        self.chunk, self.first_to, self.other_to = chunk, first_to, other_to
        self.u, self.v, self.core = u, v, core
        self.wire, self.table, self.passing, self.send, self.relay, self.recv = bufs
        self.out_sems, self.in_sems = out_sems, in_sems

    def copy(self, src, dst, out_at, in_at, to):
        return pltpu.make_async_remote_copy(
            src_ref=src,
            dst_ref=dst,
            send_sem=self.out_sems.at[self.chunk, out_at],
            recv_sem=self.in_sems.at[self.chunk, in_at],
            device_id={"pairs": to},
            device_id_type=MESH,
        )

    def arrival(self, dst, at):
        return self.copy(dst, dst, at, at, self.first_to(1, self.core))

    def near_u(self, step):
        return lax.rem(self.u + step, RING)

    def near_v(self, step):
        return lax.rem(self.v + step, RING)

    def atoms(self, step, at=0, count=ATOMS):
        base = ((self.v * CORES + self.core) * RING + self.near_u(step)) * ATOMS
        return self.table.at[pl.ds(base + at, count)]

    def block(self, step, core, at=0, count=RING * ATOMS):
        return self.table.at[pl.ds((self.near_v(step) * CORES + core) * RING * ATOMS + at, count)]

    def spread_sends(self):
        half = ATOMS // 2
        far = self.near_u(2)
        up, down = self.first_to(1, self.core), self.first_to(3, self.core)
        return [
            self.copy(self.wire.at[far, pl.ds(0, half)], self.passing.at[0], 2, 2, up),
            self.copy(self.wire.at[far, pl.ds(half, half)], self.passing.at[1], 3, 3, down),
            self.copy(self.wire.at[self.near_u(1)], self.atoms(0), 0, 1, up),
            self.copy(self.wire.at[self.near_u(3)], self.atoms(0), 1, 0, down),
        ]

    def spread_own(self):
        return pltpu.make_async_copy(self.wire.at[self.u], self.atoms(0), self.in_sems.at[self.chunk, 25])

    def spread_onward(self):
        half = ATOMS // 2
        return [
            self.copy(self.passing.at[0], self.atoms(3, 0, half), 4, 4, self.first_to(1, self.core)),
            self.copy(self.passing.at[1], self.atoms(1, half, half), 5, 5, self.first_to(3, self.core)),
        ]

    def start_spread(self):
        for copy in self.spread_sends():
            copy.start()
        self.spread_own().start()

    def forward_spread(self):
        for way, copy in enumerate(self.spread_onward()):
            self.arrival(self.passing.at[way], 2 + way).wait_recv()
            copy.start()

    def finish_spread(self):
        half = ATOMS // 2
        self.spread_own().wait()
        self.arrival(self.atoms(1), 0).wait_recv()
        self.arrival(self.atoms(3), 1).wait_recv()
        self.arrival(self.atoms(2, 0, half), 4).wait_recv()
        self.arrival(self.atoms(2, half, half), 5).wait_recv()

    def gather_first(self):
        own = self.block(0, self.core)
        return [
            self.copy(own, own, 6, 7, self.other_to(1, self.core)),
            self.copy(own, own, 7, 6, self.other_to(3, self.core)),
        ]

    def gather_second(self):
        half = RING * ATOMS // 2
        low, high = self.block(3, self.core, 0, half), self.block(1, self.core, half, half)
        return [
            self.copy(low, low, 8, 8, self.other_to(1, self.core)),
            self.copy(high, high, 9, 9, self.other_to(3, self.core)),
        ]

    def share(self, step):
        mine = self.block(step, self.core)
        return self.copy(mine, mine, 10 + step, 10 + step, self.first_to(0, 1 - self.core))

    def start_gather(self):
        for copy in self.gather_first():
            copy.start()
        self.share(0).start()

    def forward_gather(self):
        low, high = self.gather_second()
        self.arrival(self.block(3, self.core), 7).wait_recv()
        low.start()
        self.share(3).start()
        self.arrival(self.block(1, self.core), 6).wait_recv()
        high.start()
        self.share(1).start()

    def finish_gather(self):
        half = RING * ATOMS // 2
        self.arrival(self.block(2, self.core, 0, half), 8).wait_recv()
        self.arrival(self.block(2, self.core, half, half), 9).wait_recv()
        self.share(2).start()

    def finish_share(self):
        for step in range(RING):
            self.arrival(self.block(step, 1 - self.core), 10 + step).wait_recv()

    def place(self, step, core, at=0, count=SHARE):
        return self.recv.at[self.near_u(step), pl.ds(core * SHARE + at, count)]

    def far(self):
        return [
            self.copy(self.send.at[2, :, pl.ds(0, HALF_SHARE)], self.relay.at[0], 19, 19, self.first_to(1, self.core)),
            self.copy(
                self.send.at[2, :, pl.ds(HALF_SHARE, HALF_SHARE)], self.relay.at[1], 20, 20, self.first_to(3, self.core)
            ),
        ]

    def near(self):
        copies = []
        dst = self.place(0, self.core)
        for n, step in enumerate((1, 3)):
            for core in range(CORES):
                at = 14 + 2 * n
                copies.append(self.copy(self.send.at[step, core], dst, at + core, at + self.core, self.first_to(step, core)))
        other = 1 - self.core
        copies.append(self.copy(self.send.at[0, other], dst, 18, 18, self.first_to(0, other)))
        return copies

    def own(self):
        return pltpu.make_async_copy(
            self.send.at[0, self.core], self.place(0, self.core), self.in_sems.at[self.chunk, 26]
        )

    def onward(self):
        copies = []
        for way, step in enumerate((1, 3)):
            dst = self.place(RING - step, self.core, way * HALF_SHARE, HALF_SHARE)
            for core in range(CORES):
                at = 21 + 2 * way
                copies.append(self.copy(self.relay.at[way, core], dst, at + core, at + self.core, self.first_to(step, core)))
        return copies

    def start_far(self):
        for copy in self.far():
            copy.start()

    def start_near(self):
        for copy in self.near():
            copy.start()
        self.own().start()

    def forward_delivery(self):
        onward = self.onward()
        for way in range(2):
            self.arrival(self.relay.at[way], 19 + way).wait_recv()
            for copy in onward[2 * way : 2 * way + 2]:
                copy.start()

    def finish_delivery(self):
        for core in range(CORES):
            self.arrival(self.place(3, core), 14 + core).wait_recv()
            self.arrival(self.place(1, core), 16 + core).wait_recv()
            for way in range(2):
                at = 21 + 2 * way + core
                self.arrival(self.place(2, core, way * HALF_SHARE, HALF_SHARE), at).wait_recv()
        self.arrival(self.place(0, 1 - self.core), 18).wait_recv()
        self.own().wait()

    def finish_sends(self):
        copies = self.spread_sends() + self.spread_onward() + self.gather_first() + self.gather_second()
        copies += [self.share(step) for step in range(RING)] + self.far() + self.near() + self.onward()
        for copy in copies:
            copy.wait_send()


def main_kernel(
    blocks, domains, counts, coeff_hbm, out, *scratch
):
    relay_bufs = [scratch[4 * n : 4 * n + 4] for n in range(6)]
    single_bufs = [scratch[24 + 2 * n : 26 + 2 * n] for n in range(5)]
    wires, recvs = relay_bufs[0], relay_bufs[5]
    single_wires, single_recvs = single_bufs[0], single_bufs[4]
    asked, asked_smem, tables, places, request, ids, perm_main, perm_rest = scratch[34:42]
    coeff, coeff_t, perm, blk, total, sums, fresh, same, squares = scratch[42:51]
    out_sems, in_sems, single_out, single_in, ask_out, ask_in, local_sems, sum_out, sum_in = scratch[51:60]
    me = lax.axis_index("pairs")
    at_z = lax.axis_index("ri")
    planes = 2 * (sums.shape[1] - 1)
    above, below = lax.rem(at_z + 1, planes), lax.rem(at_z + planes - 1, planes)
    core = lax.rem(me, CORES)
    chip = lax.div(me, CORES)
    at_x = lax.rem(chip, RING)
    at_y = lax.div(chip, RING)

    def along_x(step, to_core):
        return (at_y * RING + lax.rem(at_x + step, RING)) * CORES + to_core

    def along_y(step, to_core):
        return (lax.rem(at_y + step, RING) * RING + at_x) * CORES + to_core

    peers = []
    for to_core in range(2):
        for step in range(1, RING):
            peers.append((along_y(step, to_core), step * CORES + to_core, (RING - step) * CORES + core))
            peers.append(
                (along_x(step, to_core), (RING + step) * CORES + to_core, (2 * RING - step) * CORES + core)
            )
    peers.append((along_x(0, 1 - core), 1 - core, core))

    fetch = pltpu.make_async_copy(coeff_hbm, coeff, local_sems.at[0])
    fetch.start()
    barrier = pltpu.get_barrier_semaphore()
    for peer, _, _ in peers:
        pl.semaphore_signal(barrier, inc=1, device_id={"pairs": peer}, device_id_type=MESH)
    for plane in (above, below):
        pl.semaphore_signal(barrier, inc=1, device_id={"ri": plane}, device_id_type=MESH)

    def ask(n):
        peer, _, there = peers[n]
        return pltpu.make_async_remote_copy(
            src_ref=request,
            dst_ref=asked.at[there],
            send_sem=ask_out.at[n],
            recv_sem=ask_in.at[there],
            device_id={"pairs": peer},
            device_id_type=MESH,
        )

    ports = []
    for chunk in range(4):
        by_x = chunk % 2 == 0
        first_to, other_to = (along_x, along_y) if by_x else (along_y, along_x)
        u, v = (at_x, at_y) if by_x else (at_y, at_x)
        bufs = [group_bufs[chunk] for group_bufs in relay_bufs]
        ports.append(Relay(chunk, first_to, other_to, u, v, core, bufs, out_sems, in_sems))
    singles = []
    for n in range(2):
        gather_to, deliver_to = (along_x, along_y) if n == 0 else (along_y, along_x)
        bufs = [group_bufs[n] for group_bufs in single_bufs]
        singles.append(Ports(n, gather_to, deliver_to, *bufs, single_out, single_in, core))

    square = (ATOMS * MAIN, ATOMS * MAIN)
    out_at = lax.broadcasted_iota(jnp.int32, square, 0)
    from_at = lax.broadcasted_iota(jnp.int32, square, 1)
    band_at, atom_at = out_at & (MAIN - 1), lax.shift_right_logical(out_at, 4)
    perm_main[...] = jnp.where(band_at * ATOMS + atom_at == from_at, 1.0, 0.0).astype(jnp.bfloat16)
    rest_at = lax.shift_right_logical(band_at, 2) * (REM * ATOMS) + (band_at & (REM - 1)) * ATOMS + atom_at
    perm_rest[...] = jnp.where(rest_at == from_at, 1.0, 0.0).astype(jnp.bfloat16)

    def main_rows(tiles):
        flat = blocks[:MAIN, :, tiles[0] * LANES : (tiles[-1] + 1) * LANES]
        flat = flat.reshape(MAIN * ATOMS, len(tiles) * LANES)
        return jnp.dot(perm_main[...], flat, preferred_element_type=jnp.float32).astype(jnp.bfloat16)

    def form(chunk):
        main = main_rows(MAINS[chunk])
        for n in range(len(MAINS[chunk])):
            wires[chunk][n] = main[:, n * LANES : (n + 1) * LANES].reshape(ATOMS, MAIN, LANES)
        parts = [blocks[MAIN:, :, t * LANES : (t + 1) * LANES].reshape(REM * ATOMS, LANES) for t in RESTS[chunk]]
        stacked = jnp.concatenate(parts, axis=0)
        depth = stacked.shape[0]
        late = jnp.dot(perm_rest[:, :depth], stacked, preferred_element_type=jnp.float32).astype(jnp.bfloat16)
        wires[chunk][RING - 1] = late.reshape(ATOMS, MAIN, LANES)

    form(0)
    pl.semaphore_wait(barrier, len(peers) + 2)
    ports[0].start_spread()
    for chunk in range(1, 4):
        form(chunk)
        ports[chunk].start_spread()
    for n in range(2):
        single_wires[n][...] = main_rows(SINGLES[n : n + 1]).reshape(ATOMS, MAIN, LANES)
    for chunk in (0, 1):
        ports[chunk].forward_spread()
    for chunk in (0, 1):
        ports[chunk].finish_spread()
        ports[chunk].start_gather()

    ids[...] = jnp.zeros_like(ids)
    pairs = domains.shape[1]
    fold = LANES // pairs
    ids[: domains.shape[0], :pairs] = domains[...]
    held = ids[...]
    lane = lax.broadcasted_iota(jnp.int32, held.shape, 1)
    turned = [held if n == 0 else pltpu.roll(held, n * pairs, 1) for n in range(fold)]
    lines = []
    for line in range(DOM // fold):
        row = jnp.zeros((1, LANES), jnp.int32)
        for n in range(fold):
            k = line * fold + n
            row = jnp.where(lane[:1] // pairs == n, turned[n][k : k + 1], row)
        lines.append(row)
    flat_shape = (ATOMS * RING * RING * CORES, LANES)
    atom = lax.broadcasted_iota(jnp.int32, flat_shape, 0)
    lane_at = lax.broadcasted_iota(jnp.int32, flat_shape, 1)
    named = jnp.zeros(flat_shape, jnp.int32)
    for line in lines:
        named = jnp.where(atom == line, 1, named)
    named = jnp.broadcast_to(jnp.max(named, axis=1, keepdims=True), flat_shape)
    local = atom & (ATOMS - 1)
    owner = lax.shift_right_logical(atom, 4)
    rank = named
    for shift in (1, 2, 4, 8):
        rank = rank + jnp.where(local >= shift, pltpu.roll(rank, shift, 0), 0)
    order = named
    for shift in (1, 2, 4, 8, 16, 32, 64, 128, 256):
        order = order + jnp.where(atom >= shift, pltpu.roll(order, shift, 0), 0)
    own_lane = jnp.where((owner == lane_at) & (named > 0), local, 0)
    for j in range(CAP):
        request[j : j + 1, :] = jnp.sum(jnp.where(rank == j + 1, own_lane, 0), axis=0, keepdims=True)
    owner_chip = lax.shift_right_logical(owner, 1)
    owner_core = owner & (CORES - 1)
    owner_x, owner_y = owner_chip & (RING - 1), lax.shift_right_logical(owner_chip, 2)
    taken = (order == lane_at + 1) & (named > 0)
    for n, (u, v) in enumerate(((owner_x, owner_y), (owner_y, owner_x))):
        held_at = ((v * CORES + owner_core) * RING + u) * ATOMS + local
        request[CAP + n : CAP + n + 1, :] = jnp.sum(jnp.where(taken, held_at, 0), axis=0, keepdims=True)
    request[CAP + 2 :, :] = jnp.zeros((6 - CAP, LANES), jnp.int32)

    for n in range(len(peers)):
        ask(n).start()
    own_ask = pltpu.make_async_copy(request, asked.at[core], local_sems.at[1])
    own_ask.start()

    for chunk in (2, 3):
        ports[chunk].forward_spread()
    shape = (DEPTH, DOM * BAND)
    row = lax.broadcasted_iota(jnp.int32, shape, 0)
    col = lax.broadcasted_iota(jnp.int32, shape, 1)
    split = DOM * MAIN
    late = row - split
    source = jnp.where(
        row < split,
        lax.shift_right_logical(row, 4) * BAND + (row & (MAIN - 1)),
        lax.shift_right_arithmetic(late, 2) * BAND + MAIN + (late & (REM - 1)),
    )
    perm[...] = jnp.where((source == col) & (row < DOM * BAND), 1.0, 0.0).astype(jnp.bfloat16)
    same[...] = jnp.where(
        lax.broadcasted_iota(jnp.int32, same.shape, 0) == lax.broadcasted_iota(jnp.int32, same.shape, 1), 1.0, 0.0
    ).astype(jnp.bfloat16)
    for n in range(2):
        blk[n, DOM * BAND :, :] = jnp.zeros((DEPTH - DOM * BAND, blk.shape[2]), jnp.bfloat16)
    fetch.wait()

    def prepare(begin, end):
        def turn(pair, _):
            ordered = [
                jnp.dot(perm[...], coeff[4 * pair + n], preferred_element_type=jnp.float32).astype(jnp.bfloat16)
                for n in range(4)
            ]
            for n in range(4):
                turned = lax.dot_general(
                    same[...], ordered[n], (((1,), (1,)), ((), ())), preferred_element_type=jnp.float32
                )
                coeff_t[4 * pair + n] = turned.astype(jnp.bfloat16)
            return 0

        lax.fori_loop(begin // 4, end // 4, turn, 0)

    prepare(0, 4)
    for chunk in (2, 3):
        ports[chunk].finish_spread()
    for chunk in (0, 1):
        ports[chunk].forward_gather()
    for chunk in (2, 3):
        ports[chunk].start_gather()

    rel_x = (owner_x + RING - at_x) & (RING - 1)
    rel_y = (owner_y + RING - at_y) & (RING - 1)
    place_x = ((rel_y * CORES + owner_core) * RING + rel_x) * CAP + rank - 1
    place_y = ((rel_x * CORES + owner_core) * RING + rel_y) * CAP + rank - 1
    tables[...] = jnp.zeros_like(tables)
    for n, line in enumerate(lines):
        for table, place in enumerate((order - 1, place_x, place_y)):
            tables[table, n : n + 1, :] = jnp.sum(jnp.where(atom == line, place, 0), axis=0, keepdims=True)
    table_copy = pltpu.make_async_copy(tables, places, local_sems.at[3])
    table_copy.start()
    table_copy.wait()

    for single in singles:
        single.start_gather()
    prepare(4, 12)

    own_ask.wait()
    for n in range(len(peers)):
        _, here, _ = peers[n]
        pltpu.make_async_remote_copy(
            src_ref=request,
            dst_ref=asked.at[here],
            send_sem=ask_out.at[n],
            recv_sem=ask_in.at[here],
            device_id={"pairs": peers[n][0]},
            device_id_type=MESH,
        ).wait_recv()
    to_smem = pltpu.make_async_copy(asked, asked_smem, local_sems.at[2])
    to_smem.start()
    to_smem.wait()

    def line_of(dest, on_row):
        return jnp.where(dest < CORES, dest, dest + ROW_LINES) if on_row else dest

    def pick_single(n):
        port = singles[n]
        owner_of = along_x if n == 0 else along_y

        def serve(dest, _):
            line = line_of(dest, n == 1)
            step, to_core = dest // CORES, dest % CORES
            for r in range(RING):
                for j in range(CAP):
                    atom = asked_smem[line, j, owner_of(r, core)]
                    found = port.wire[atom] if r == 0 else port.ring[r - 1, atom]
                    port.send[step, to_core, r * CAP + j] = found
            return 0

        lax.fori_loop(2 * CORES, 3 * CORES, serve, 0)
        port.start_far()

        def serve_near(dest, _):
            return serve(jnp.where(dest < 2 * CORES, dest, dest + CORES), 0)

        lax.fori_loop(0, 3 * CORES, serve_near, 0)
        port.start_near()

    def pick(chunk):
        port = ports[chunk]

        def serve(dest, _):
            line = line_of(dest, chunk % 2 == 0)
            step, to_core = dest // CORES, dest % CORES
            for n in range(SHARE):
                port.send[step, to_core, n] = port.table[asked_smem[line, CAP + chunk % 2, core * SHARE + n]]
            return 0

        lax.fori_loop(2 * CORES, 3 * CORES, serve, 0)
        port.start_far()

        def serve_near(dest, _):
            return serve(jnp.where(dest < 2 * CORES, dest, dest + CORES), 0)

        lax.fori_loop(0, 3 * CORES, serve_near, 0)
        port.start_near()

    for chunk in (0, 1):
        ports[chunk].finish_gather()
    for chunk in (0, 1):
        ports[chunk].finish_share()
        pick(chunk)
    for chunk in (2, 3):
        ports[chunk].forward_gather()
    for single in singles:
        single.forward_gather()
    prepare(12, 20)
    for chunk in (0, 1):
        ports[chunk].forward_delivery()
    prepare(20, 24)
    for chunk in (2, 3):
        ports[chunk].finish_gather()
    for n in range(2):
        singles[n].finish_gather()
        pick_single(n)
    for chunk in (2, 3):
        ports[chunk].finish_share()
        pick(chunk)
    prepare(24, 32)
    for single in singles:
        single.forward_delivery()
    for chunk in (2, 3):
        ports[chunk].forward_delivery()

    pack_row = lax.broadcasted_iota(jnp.int32, (MAXPNO, MAXPNO), 0)
    pack_col = lax.broadcasted_iota(jnp.int32, (MAXPNO, MAXPNO), 1)
    pack_lane = lax.broadcasted_iota(jnp.int32, (MAXPNO, LANES), 1)
    fold_lane = lax.broadcasted_iota(jnp.int32, (FOLD_ROWS, LANES), 1)

    def assemble(pair, slot, chunks):
        base = MAIN * DOM
        begin = 0
        upper = lax.broadcasted_iota(jnp.int32, (8, LANES), 0) < REM

        def named_at(table):
            return [places[table, k // fold, (k % fold) * pairs + pair] for k in range(DOM)]

        at = named_at(0)
        for chunk in chunks:
            tiles = len(RESTS[chunk])
            for n in range(RING - 1):
                span = slice(begin + n * LANES, begin + (n + 1) * LANES)
                for k in range(DOM):
                    blk[slot, MAIN * k : MAIN * (k + 1), span] = recvs[chunk][n, at[k]]
            if tiles == RING:
                span = slice(begin + (RING - 1) * LANES, begin + RING * LANES)
                single_at = named_at(1 + chunk % 2)
                for k in range(DOM):
                    blk[slot, MAIN * k : MAIN * (k + 1), span] = single_recvs[chunk % 2][single_at[k]]
            for k in range(0, DOM, 4):
                rest = [recvs[chunk][RING - 1, at[k + n]].astype(jnp.float32) for n in range(4)]
                for half in range((tiles + 1) // 2):
                    parts = [r[8 * half : 8 * half + 8] for r in rest]
                    shifted = [pltpu.roll(part, REM, 0) for part in parts]
                    for q in range(2 * half, min(2 * half + 2, tiles)):
                        first, second = (parts, shifted) if q % 2 == 0 else (shifted, parts)
                        low = jnp.where(upper, first[0], second[1])
                        high = jnp.where(upper, first[2], second[3])
                        both = jnp.concatenate([low, high], axis=0).astype(jnp.bfloat16)
                        tile = slice(begin + q * LANES, begin + (q + 1) * LANES)
                        blk[slot, base + REM * k : base + REM * (k + 4), tile] = both
            begin += tiles * LANES
        return begin

    def multiply(pair, slot, cols):
        weights = coeff_t[pair]
        result = jnp.zeros((MAXPNO, MAXPNO), jnp.float32)
        for at in range(0, cols, 256):
            vec = jnp.dot(weights, blk[slot, :, at : at + 256], preferred_element_type=jnp.float32)
            vec = vec.astype(jnp.bfloat16)
            result += lax.dot_general(vec, vec, (((1,), (1,)), ((), ())), preferred_element_type=jnp.float32)
        return result

    early_cols = LANES * (len(RESTS[0]) + len(RESTS[1]))
    late_cols = LANES * (len(RESTS[2]) + len(RESTS[3]))
    group = coeff.shape[0] // planes
    half_ring = planes // 2
    part = HALF_PACK // 2

    def rows_of(half, piece):
        return pl.ds(pl.multiple_of(half * HALF_PACK + piece * part, 8), part)

    def chain(way, step, half, piece):
        rows = rows_of(half, piece)
        return pltpu.make_async_remote_copy(
            src_ref=sums.at[way, step, rows],
            dst_ref=sums.at[way, step + 1, rows],
            send_sem=sum_out.at[(way * half_ring + step) * 2 + half, piece],
            recv_sem=sum_in.at[(way * half_ring + step) * 2 + half, piece],
            device_id={"ri": jnp.where(way == 0, above, below)},
            device_id_type=MESH,
        )

    def locate(item):
        step = (item + 1) // 2
        way = jnp.where(item == 0, 0, (item + 1) % 2)
        away = jnp.where(way == 0, half_ring - step, half_ring + step)
        return way, step, lax.rem(at_z + away, planes) * group

    def first_half(step, _):
        pair = locate(step // 2)[2] + 2 * (step % 2)
        following = locate((step + 1) // 2)[2] + 2 * ((step + 1) % 2)
        assemble(pair + 1, 1, (0, 1))
        total[pair] = multiply(pair, 0, early_cols)
        assemble(following, 0, (0, 1))
        total[pair + 1] = multiply(pair + 1, 1, early_cols)
        return 0

    def block_products(slot, first, following, whole):
        chunks = (0, 1, 2, 3) if whole else (2, 3)
        cols = early_cols + late_cols if whole else late_cols

        def one(duo, _):
            pair = first + 2 * duo
            assemble(pair + 1, 1, chunks)
            here = multiply(pair, 0, cols)
            assemble(jnp.where(duo == 0, pair + 2, following), 0, chunks)
            there = multiply(pair + 1, 1, cols)
            if not whole:
                here += total[pair]
                there += total[pair + 1]
            squares[duo, :MAXPNO, :MAXPNO] = jnp.where(pack_row >= pack_col, here, there)
            diagonal = jnp.sum(jnp.where(pack_row == pack_col, there, 0.0), axis=0, keepdims=True)
            at = DIAG_AT + 2 * duo
            fresh[slot, pl.ds(at, 1), :] = diagonal[:, :LANES]
            fresh[slot, pl.ds(at + 1, 1), :REST] = diagonal[:, LANES:]
            return 0

        lax.fori_loop(0, 2, one, 0)
        fresh[slot, :MAXPNO, :] = squares[0, :MAXPNO, :LANES]
        fresh[slot, HALF_PACK : HALF_PACK + MAXPNO, :] = squares[1, :MAXPNO, :LANES]
        shared = jnp.where(
            pack_lane < REST, squares[0, :MAXPNO, LANES:], pltpu.roll(squares[1, :MAXPNO, LANES:], REST, 1)
        )
        fresh[slot, MAXPNO:HALF_PACK, :] = shared[:TOP]
        fresh[slot, HALF_PACK + MAXPNO : FOLD_AT, :] = shared[TOP:]
        folded = jnp.zeros((FOLD_ROWS, LANES), jnp.float32)
        for n in range(SQUARE_ROWS // FOLD_ROWS):
            rows = squares[1, n * FOLD_ROWS : (n + 1) * FOLD_ROWS, LANES:]
            moved = pltpu.roll(rows, (n * LEFT - SPARE) % LANES, 1)
            folded = jnp.where((fold_lane >= n * LEFT) & (fold_lane < (n + 1) * LEFT), moved, folded)
        fresh[slot, FOLD_AT:DIAG_AT, :] = folded

    def begin_half(slot, way, step, half):
        for piece in range(2):
            rows = rows_of(half, piece)
            sums[way, step, rows, :] = fresh[slot, rows, :]
            chain(way, step, half, piece).start()

    def add_half(way, step, half):
        for piece in range(2):
            rows = rows_of(half, piece)
            chain(way, step - 1, half, piece).wait_recv()
            sums[way, step, rows, :] = sums[way, step, rows, :] + fresh[way, rows, :]
            chain(way, step, half, piece).start()

    def ring_item(whole, item, _):
        way, step, first = locate(item)
        block_products(way, first, locate(item + 1)[2], whole)

        @pl.when(item == 0)
        def _():
            begin_half(0, 0, 0, 0)
            begin_half(0, 1, 0, 1)

        @pl.when(step == 1)
        def _():
            begin_half(way, way, step, 1 - way)

        @pl.when((step > 1) & (step < half_ring))
        def _():
            add_half(way, step, 1 - way)

        @pl.when((way == 1) & (step < half_ring))
        def _():
            add_half(0, step, 0)
            add_half(1, step, 1)

        @pl.when(item == 2)
        def _():
            for n in range(len(peers)):
                ask(n).wait_send()
            for port in ports:
                port.finish_sends()
            for single in singles:
                single.finish_served()
                single.finish_sends()

        return 0

    fresh[...] = jnp.zeros_like(fresh)
    squares[...] = jnp.zeros_like(squares)
    ahead = 5
    ports[0].finish_delivery()
    ports[1].finish_delivery()
    assemble(locate(0)[2], 0, (0, 1))
    lax.fori_loop(0, 2 * ahead, first_half, 0)
    for single in singles:
        single.finish_delivery()
    ports[2].finish_delivery()
    ports[3].finish_delivery()
    assemble(locate(0)[2], 0, (2, 3))
    lax.fori_loop(0, ahead, functools.partial(ring_item, False), 0)
    assemble(locate(ahead)[2], 0, (0, 1, 2, 3))
    lax.fori_loop(ahead, planes, functools.partial(ring_item, True), 0)
    for half in (1, 0):
        for piece in range(2):
            rows = rows_of(half, piece)
            for way in range(2):
                chain(way, half_ring - 1, half, piece).wait_recv()
            arrived = sums[0, half_ring, rows, :] + sums[1, half_ring, rows, :]
            out[rows, :] = arrived + fresh[0, rows, :]
    for n in range(group):
        count = counts[at_z * group + n].astype(jnp.float32)
        out[COUNTS + n : COUNTS + n + 1, :] = jnp.full((1, LANES), count)
    for step in range(half_ring):
        for way in range(2):
            for half in range(2):
                if step or half == way:
                    for piece in range(2):
                        chain(way, step, half, piece).wait_send()


def pair_products(blocks, domains, counts, coeff, planes):
    pair_dev, depth, slots = coeff.shape
    lines = 2 * RING * CORES
    bf16 = jnp.bfloat16
    tile = (MAIN, LANES)
    scratch = []
    for shape in (
        (RING, ATOMS),
        (RING * RING * CORES * ATOMS,),
        (2, ATOMS // 2),
        (RING, CORES, SHARE),
        (2, CORES, HALF_SHARE),
        (RING, SLOTS),
    ):
        scratch += [pltpu.VMEM(shape + tile, bf16)] * 4
    for shape in (
        (ATOMS,),
        (RING - 1, ATOMS),
        (RING, CORES, PICKS),
        (2, CORES, HALF),
        (RING * CORES * PICKS,),
    ):
        scratch += [pltpu.VMEM(shape + tile, bf16)] * 2
    scratch += [
        pltpu.VMEM((lines, 8, LANES), jnp.int32),
        pltpu.SMEM((lines, 8, LANES), jnp.int32),
        pltpu.VMEM((3, 8, LANES), jnp.int32),
        pltpu.SMEM((3, 8, LANES), jnp.int32),
        pltpu.VMEM((8, LANES), jnp.int32),
        pltpu.VMEM((16, LANES), jnp.int32),
        pltpu.VMEM((ATOMS * MAIN, ATOMS * MAIN), bf16),
        pltpu.VMEM((ATOMS * MAIN, ATOMS * MAIN), bf16),
        pltpu.VMEM((pair_dev, depth, slots), bf16),
        pltpu.VMEM((pair_dev, MAXPNO, DEPTH), bf16),
        pltpu.VMEM((DEPTH, depth), bf16),
        pltpu.VMEM((2, DEPTH, blocks.shape[2]), bf16),
        pltpu.VMEM((pair_dev, MAXPNO, MAXPNO), jnp.float32),
        pltpu.VMEM((2, planes // 2 + 1, PACK, LANES), jnp.float32),
        pltpu.VMEM((2, PACK, LANES), jnp.float32),
        pltpu.VMEM((MAXPNO, slots), bf16),
        pltpu.VMEM((2, SQUARE_ROWS, 2 * LANES), jnp.float32),
        pltpu.SemaphoreType.DMA((4, 27)),
        pltpu.SemaphoreType.DMA((4, 27)),
        pltpu.SemaphoreType.DMA((2, 16)),
        pltpu.SemaphoreType.DMA((2, 16)),
        pltpu.SemaphoreType.DMA((lines,)),
        pltpu.SemaphoreType.DMA((lines,)),
        pltpu.SemaphoreType.DMA((4,)),
        pltpu.SemaphoreType.DMA((2 * planes, 2)),
        pltpu.SemaphoreType.DMA((2 * planes, 2)),
    ]
    return pl.pallas_call(
        main_kernel,
        out_shape=jax.ShapeDtypeStruct((PACK, LANES), jnp.float32),
        in_specs=[
            pl.BlockSpec(memory_space=pltpu.VMEM),
            pl.BlockSpec(memory_space=pltpu.VMEM),
            pl.BlockSpec(memory_space=pltpu.SMEM),
            pl.BlockSpec(memory_space=pl.ANY),
        ],
        out_specs=pl.BlockSpec(memory_space=pltpu.VMEM),
        scratch_shapes=scratch,
        compiler_params=params(60, collective_id=0, has_side_effects=True),
    )(blocks, domains, counts, coeff)


def tail_kernel(packed, amp, energy_row, energy_col, out, wide):
    slots = amp.shape[1]
    step = pl.program_id(0)
    full_row = lax.broadcasted_iota(jnp.int32, (slots, slots), 0)
    full_col = lax.broadcasted_iota(jnp.int32, (slots, slots), 1)
    lane = lax.broadcasted_iota(jnp.int32, (MAXPNO, LANES), 1)
    fold_lane = lax.broadcasted_iota(jnp.int32, (FOLD_ROWS, LANES), 1)
    wide[MAXPNO:, :] = jnp.zeros((slots - MAXPNO, slots), jnp.float32)

    def shared_at(begin, end):
        if end <= TOP:
            return packed[MAXPNO + begin : MAXPNO + end, :]
        return packed[HALF_PACK + MAXPNO + begin - TOP : HALF_PACK + MAXPNO + end - TOP, :]

    @pl.when(step == 0)
    def _():
        wide[:MAXPNO, :LANES] = packed[:MAXPNO, :]
        for begin, end in ((0, TOP), (TOP, MAXPNO)):
            wide[begin:end, LANES:] = jnp.where(lane[begin:end] < REST, shared_at(begin, end), 0.0)

    @pl.when(step == 1)
    def _():
        wide[:MAXPNO, :LANES] = packed[HALF_PACK : HALF_PACK + MAXPNO, :]
        for begin, end in ((0, TOP), (TOP, MAXPNO)):
            turned = pltpu.roll(shared_at(begin, end), SPARE, 1)
            wide[begin:end, LANES:] = jnp.where(lane[begin:end] < SPARE, turned, 0.0)
        folded = packed[FOLD_AT:DIAG_AT, :]
        for n in range(SQUARE_ROWS // FOLD_ROWS):
            begin, end = n * FOLD_ROWS, min((n + 1) * FOLD_ROWS, MAXPNO)
            moved = pltpu.roll(folded, (SPARE - n * LEFT) % LANES, 1)
            left = (fold_lane >= SPARE) & (fold_lane < REST)
            held = wide[begin:end, LANES:]
            wide[begin:end, LANES:] = jnp.where(left[: end - begin], moved[: end - begin], held)

    square = wide[...]
    at = DIAG_AT + 2 * step
    diagonal = jnp.concatenate([packed[pl.ds(at, 1), :], packed[pl.ds(at + 1, 1), :]], axis=1)
    on_diagonal = full_row == full_col
    for n in range(2):
        count = packed[pl.ds(COUNTS + 2 * step + n, 1), :][:, :1].astype(jnp.int32)
        if n == 0:
            held = jnp.where(full_row >= full_col, square, 0.0)
        else:
            held = jnp.where(full_row < full_col, square, jnp.where(on_diagonal, diagonal, 0.0))
        products = held + jnp.where(on_diagonal, 0.0, held.T)
        valid = (full_row < count) & (full_col < count)
        products = jnp.where(valid, products / NAUX, 0.0)
        amps = amp[n]
        contract = (((1,), (1,)), ((), ()))
        high = products.astype(jnp.bfloat16)
        left = products - high.astype(jnp.float32)
        mid = left.astype(jnp.bfloat16)
        low = (left - mid.astype(jnp.float32)).astype(jnp.bfloat16)
        coupled = lax.dot_general(low, amps, contract, preferred_element_type=jnp.float32)
        coupled += lax.dot_general(mid, amps, contract, preferred_element_type=jnp.float32)
        coupled += lax.dot_general(high, amps, contract, preferred_element_type=jnp.float32)
        energies = energy_col[n] + energy_row[pl.ds(2 * step + n, 1), :]
        result = products + coupled + energies * amps.astype(jnp.float32)
        out[n] = jnp.where(valid, result, 0.0)


def tail(packed, amp, energy):
    subs, slots, _ = amp.shape
    return pl.pallas_call(
        tail_kernel,
        out_shape=jax.ShapeDtypeStruct((subs, slots, slots), jnp.float32),
        grid=(subs // 2,),
        in_specs=[
            pl.BlockSpec((PACK, LANES), lambda i: (0, 0)),
            pl.BlockSpec((2, slots, slots), lambda i: (i, 0, 0)),
            pl.BlockSpec((subs, slots), lambda i: (0, 0)),
            pl.BlockSpec((2, slots, 1), lambda i: (i, 0, 0)),
        ],
        out_specs=pl.BlockSpec((2, slots, slots), lambda i: (i, 0, 0)),
        scratch_shapes=[pltpu.VMEM((slots, slots), jnp.float32)],
        compiler_params=params(32),
    )(packed, amp, energy, energy[:, :, None])


def on_device(atom_blocks, domains, pno_counts, pno_coeffs, amplitudes, pno_energies):
    planes = lax.axis_size("ri")
    mine = pair_products(atom_blocks.transpose(1, 0, 2), domains.T, pno_counts, pno_coeffs, planes)
    return tail(mine, amplitudes, pno_energies)


def solution(mesh):
    placed = (
        P("pairs", None, "ri"),
        P("pairs", None),
        P("pairs"),
        P("pairs", None, None),
        P(("pairs", "ri"), None, None),
        P(("pairs", "ri"), None),
    )
    return jax.shard_map(
        on_device,
        mesh=mesh,
        in_specs=placed,
        out_specs=P(("pairs", "ri"), None, None),
        check_vma=False,
    )
```

```python
import functools

import jax
import jax.numpy as jnp
from jax import lax
from jax.experimental import pallas as pl
from jax.experimental.pallas import tpu as pltpu
from jax.sharding import PartitionSpec as P

NAUX = 14336
CAP = 3
MAXPNO = 200
MAIN = 16
REM = 4
SPLIT = 128
REST = MAXPNO - SPLIT
LANES = 128
MIB = 1 << 20
RING = 4
CORES = 2
ATOMS = 16
DOM = 12
BAND = MAIN + REM
PICKS = RING * CAP
HALF = PICKS // 2
DEPTH = 256
SPARE = LANES - REST
LEFT = REST - SPARE
FOLD_ROWS = 32
HALF_PACK = 320
PACK = 2 * HALF_PACK
TOP = HALF_PACK - MAXPNO
FOLD_AT = PACK - FOLD_ROWS - 8
DIAG_AT = PACK - 8
COUNTS = PACK - 4
SQUARE_ROWS = 224
SLOTS = 48
SHARE = SLOTS // CORES
HALF_SHARE = SHARE // 2
ROW_LINES = RING * CORES
MAINS = ((0, 1, 2), (3, 4, 5), (6, 7, 8), (10, 11, 12))
RESTS = ((0, 1, 2), (3, 4, 5), (6, 7, 8, 9), (10, 11, 12, 13))
SINGLES = (9, 13)
MESH = pl.DeviceIdType.MESH


def params(mib, **kw):
    return pltpu.CompilerParams(vmem_limit_bytes=mib * MIB, **kw)


class Ports:
    def __init__(self, chunk, gather_to, deliver_to, wire, ring, send, relay, recv, out_sems, in_sems, core):
        self.gather_to, self.deliver_to, self.core = gather_to, deliver_to, core
        self.wire, self.ring, self.send, self.relay, self.recv = wire, ring, send, relay, recv
        self.out_sems, self.in_sems, self.chunk = out_sems, in_sems, chunk

    def copy(self, src, dst, out_at, in_at, to):
        return pltpu.make_async_remote_copy(
            src_ref=src,
            dst_ref=dst,
            send_sem=self.out_sems.at[self.chunk, out_at],
            recv_sem=self.in_sems.at[self.chunk, in_at],
            device_id={"pairs": to},
            device_id_type=MESH,
        )

    def gather_first(self):
        up = self.copy(self.wire, self.ring.at[2], 0, 1, self.gather_to(1, self.core))
        down = self.copy(self.wire, self.ring.at[0], 1, 0, self.gather_to(3, self.core))
        return up, down

    def gather_second(self):
        half = ATOMS // 2
        low, high = pl.ds(0, half), pl.ds(half, half)
        up = self.copy(self.ring.at[2, low], self.ring.at[1, low], 2, 2, self.gather_to(1, self.core))
        down = self.copy(self.ring.at[0, high], self.ring.at[1, high], 3, 3, self.gather_to(3, self.core))
        return up, down

    def place(self, rel, core):
        return (rel * CORES + core) * PICKS

    def far(self):
        up = self.copy(self.send.at[2, :, pl.ds(0, HALF)], self.relay.at[0], 4, 4, self.deliver_to(1, self.core))
        down = self.copy(self.send.at[2, :, pl.ds(HALF, HALF)], self.relay.at[1], 5, 5, self.deliver_to(3, self.core))
        return up, down

    def near(self):
        copies = []
        for n, step in enumerate((1, 3)):
            for core in range(CORES):
                dst = self.recv.at[pl.ds(self.place(RING - step, self.core), PICKS)]
                at = 6 + 2 * n
                copies.append(self.copy(self.send.at[step, core], dst, at + core, at + self.core, self.deliver_to(step, core)))
        other = 1 - self.core
        dst = self.recv.at[pl.ds(self.place(0, self.core), PICKS)]
        copies.append(self.copy(self.send.at[0, other], dst, 10, 10, self.deliver_to(0, other)))
        return copies

    def own(self):
        return pltpu.make_async_copy(
            self.send.at[0, self.core],
            self.recv.at[pl.ds(self.place(0, self.core), PICKS)],
            self.in_sems.at[self.chunk, 11],
        )

    def onward(self):
        copies = []
        for way, step in enumerate((1, 3)):
            for core in range(CORES):
                dst = self.recv.at[pl.ds(self.place(2, self.core) + way * HALF, HALF)]
                at = 12 + 2 * way
                copies.append(self.copy(self.relay.at[way, core], dst, at + core, at + self.core, self.deliver_to(step, core)))
        return copies

    def start_gather(self):
        for copy in self.gather_first():
            copy.start()

    def forward_gather(self):
        up, down = self.gather_second()
        first_up, first_down = self.gather_first()
        first_up.wait_recv()
        up.start()
        first_down.wait_recv()
        down.start()

    def finish_gather(self):
        for copy in self.gather_second():
            copy.wait_recv()

    def start_far(self):
        for copy in self.far():
            copy.start()

    def start_near(self):
        for copy in self.near():
            copy.start()
        self.own().start()

    def forward_delivery(self):
        far, onward = self.far(), self.onward()
        for way in range(2):
            far[way].wait_recv()
            for copy in onward[2 * way : 2 * way + 2]:
                copy.start()

    def finish_delivery(self):
        for n, step in enumerate((1, 3)):
            for core in range(CORES):
                dst = self.recv.at[pl.ds(self.place(step, core), PICKS)]
                at = 6 + 2 * (1 - n)
                self.copy(dst, dst, at + core, at + core, self.deliver_to(1, self.core)).wait_recv()
        other = 1 - self.core
        dst = self.recv.at[pl.ds(self.place(0, other), PICKS)]
        self.copy(dst, dst, 10, 10, self.deliver_to(1, self.core)).wait_recv()
        self.own().wait()
        for way in range(2):
            for core in range(CORES):
                dst = self.recv.at[pl.ds(self.place(2, core) + way * HALF, HALF)]
                at = 12 + 2 * way
                self.copy(dst, dst, at + core, at + core, self.deliver_to(1, self.core)).wait_recv()

    def finish_served(self):
        for copy in self.far() + tuple(self.near()):
            copy.wait_send()

    def finish_sends(self):
        for copy in self.gather_first() + self.gather_second() + tuple(self.onward()):
            copy.wait_send()


class Relay:
    def __init__(self, chunk, first_to, other_to, u, v, core, bufs, out_sems, in_sems):
        self.chunk, self.first_to, self.other_to = chunk, first_to, other_to
        self.u, self.v, self.core = u, v, core
        self.wire, self.table, self.passing, self.send, self.relay, self.recv = bufs
        self.out_sems, self.in_sems = out_sems, in_sems

    def copy(self, src, dst, out_at, in_at, to):
        return pltpu.make_async_remote_copy(
            src_ref=src,
            dst_ref=dst,
            send_sem=self.out_sems.at[self.chunk, out_at],
            recv_sem=self.in_sems.at[self.chunk, in_at],
            device_id={"pairs": to},
            device_id_type=MESH,
        )

    def arrival(self, dst, at):
        return self.copy(dst, dst, at, at, self.first_to(1, self.core))

    def near_u(self, step):
        return lax.rem(self.u + step, RING)

    def near_v(self, step):
        return lax.rem(self.v + step, RING)

    def atoms(self, step, at=0, count=ATOMS):
        base = ((self.v * CORES + self.core) * RING + self.near_u(step)) * ATOMS
        return self.table.at[pl.ds(base + at, count)]

    def block(self, step, core, at=0, count=RING * ATOMS):
        return self.table.at[pl.ds((self.near_v(step) * CORES + core) * RING * ATOMS + at, count)]

    def spread_sends(self):
        half = ATOMS // 2
        far = self.near_u(2)
        up, down = self.first_to(1, self.core), self.first_to(3, self.core)
        return [
            self.copy(self.wire.at[far, pl.ds(0, half)], self.passing.at[0], 2, 2, up),
            self.copy(self.wire.at[far, pl.ds(half, half)], self.passing.at[1], 3, 3, down),
            self.copy(self.wire.at[self.near_u(1)], self.atoms(0), 0, 1, up),
            self.copy(self.wire.at[self.near_u(3)], self.atoms(0), 1, 0, down),
        ]

    def spread_own(self):
        return pltpu.make_async_copy(self.wire.at[self.u], self.atoms(0), self.in_sems.at[self.chunk, 25])

    def spread_onward(self):
        half = ATOMS // 2
        return [
            self.copy(self.passing.at[0], self.atoms(3, 0, half), 4, 4, self.first_to(1, self.core)),
            self.copy(self.passing.at[1], self.atoms(1, half, half), 5, 5, self.first_to(3, self.core)),
        ]

    def start_spread(self):
        for copy in self.spread_sends():
            copy.start()
        self.spread_own().start()

    def forward_spread(self):
        for way, copy in enumerate(self.spread_onward()):
            self.arrival(self.passing.at[way], 2 + way).wait_recv()
            copy.start()

    def finish_spread(self):
        half = ATOMS // 2
        self.spread_own().wait()
        self.arrival(self.atoms(1), 0).wait_recv()
        self.arrival(self.atoms(3), 1).wait_recv()
        self.arrival(self.atoms(2, 0, half), 4).wait_recv()
        self.arrival(self.atoms(2, half, half), 5).wait_recv()

    def gather_first(self):
        own = self.block(0, self.core)
        return [
            self.copy(own, own, 6, 7, self.other_to(1, self.core)),
            self.copy(own, own, 7, 6, self.other_to(3, self.core)),
        ]

    def gather_second(self):
        half = RING * ATOMS // 2
        low, high = self.block(3, self.core, 0, half), self.block(1, self.core, half, half)
        return [
            self.copy(low, low, 8, 8, self.other_to(1, self.core)),
            self.copy(high, high, 9, 9, self.other_to(3, self.core)),
        ]

    def share(self, step):
        mine = self.block(step, self.core)
        return self.copy(mine, mine, 10 + step, 10 + step, self.first_to(0, 1 - self.core))

    def start_gather(self):
        for copy in self.gather_first():
            copy.start()
        self.share(0).start()

    def forward_gather(self):
        low, high = self.gather_second()
        self.arrival(self.block(3, self.core), 7).wait_recv()
        low.start()
        self.share(3).start()
        self.arrival(self.block(1, self.core), 6).wait_recv()
        high.start()
        self.share(1).start()

    def finish_gather(self):
        half = RING * ATOMS // 2
        self.arrival(self.block(2, self.core, 0, half), 8).wait_recv()
        self.arrival(self.block(2, self.core, half, half), 9).wait_recv()
        self.share(2).start()

    def finish_share(self):
        for step in range(RING):
            self.arrival(self.block(step, 1 - self.core), 10 + step).wait_recv()

    def place(self, step, core, at=0, count=SHARE):
        return self.recv.at[self.near_u(step), pl.ds(core * SHARE + at, count)]

    def far(self):
        return [
            self.copy(self.send.at[2, :, pl.ds(0, HALF_SHARE)], self.relay.at[0], 19, 19, self.first_to(1, self.core)),
            self.copy(
                self.send.at[2, :, pl.ds(HALF_SHARE, HALF_SHARE)], self.relay.at[1], 20, 20, self.first_to(3, self.core)
            ),
        ]

    def near(self):
        copies = []
        dst = self.place(0, self.core)
        for n, step in enumerate((1, 3)):
            for core in range(CORES):
                at = 14 + 2 * n
                copies.append(self.copy(self.send.at[step, core], dst, at + core, at + self.core, self.first_to(step, core)))
        other = 1 - self.core
        copies.append(self.copy(self.send.at[0, other], dst, 18, 18, self.first_to(0, other)))
        return copies

    def own(self):
        return pltpu.make_async_copy(
            self.send.at[0, self.core], self.place(0, self.core), self.in_sems.at[self.chunk, 26]
        )

    def onward(self):
        copies = []
        for way, step in enumerate((1, 3)):
            dst = self.place(RING - step, self.core, way * HALF_SHARE, HALF_SHARE)
            for core in range(CORES):
                at = 21 + 2 * way
                copies.append(self.copy(self.relay.at[way, core], dst, at + core, at + self.core, self.first_to(step, core)))
        return copies

    def start_far(self):
        for copy in self.far():
            copy.start()

    def start_near(self):
        for copy in self.near():
            copy.start()
        self.own().start()

    def forward_delivery(self):
        onward = self.onward()
        for way in range(2):
            self.arrival(self.relay.at[way], 19 + way).wait_recv()
            for copy in onward[2 * way : 2 * way + 2]:
                copy.start()

    def finish_delivery(self):
        for core in range(CORES):
            self.arrival(self.place(3, core), 14 + core).wait_recv()
            self.arrival(self.place(1, core), 16 + core).wait_recv()
            for way in range(2):
                at = 21 + 2 * way + core
                self.arrival(self.place(2, core, way * HALF_SHARE, HALF_SHARE), at).wait_recv()
        self.arrival(self.place(0, 1 - self.core), 18).wait_recv()
        self.own().wait()

    def finish_sends(self):
        copies = self.spread_sends() + self.spread_onward() + self.gather_first() + self.gather_second()
        copies += [self.share(step) for step in range(RING)] + self.far() + self.near() + self.onward()
        for copy in copies:
            copy.wait_send()


def main_kernel(
    blocks, domains, counts, coeff_hbm, out, *scratch
):
    relay_bufs = [scratch[4 * n : 4 * n + 4] for n in range(6)]
    single_bufs = [scratch[24 + 2 * n : 26 + 2 * n] for n in range(5)]
    wires, recvs = relay_bufs[0], relay_bufs[5]
    single_wires, single_recvs = single_bufs[0], single_bufs[4]
    asked, asked_smem, tables, places, request, ids, perm_main, perm_rest = scratch[34:42]
    coeff, coeff_t, perm, blk, total, sums, fresh, same, squares = scratch[42:51]
    out_sems, in_sems, single_out, single_in, ask_out, ask_in, local_sems, sum_out, sum_in = scratch[51:60]
    me = lax.axis_index("pairs")
    at_z = lax.axis_index("ri")
    planes = 2 * (sums.shape[1] - 1)
    above, below = lax.rem(at_z + 1, planes), lax.rem(at_z + planes - 1, planes)
    core = lax.rem(me, CORES)
    chip = lax.div(me, CORES)
    at_x = lax.rem(chip, RING)
    at_y = lax.div(chip, RING)

    def along_x(step, to_core):
        return (at_y * RING + lax.rem(at_x + step, RING)) * CORES + to_core

    def along_y(step, to_core):
        return (lax.rem(at_y + step, RING) * RING + at_x) * CORES + to_core

    peers = []
    for to_core in range(2):
        for step in range(1, RING):
            peers.append((along_y(step, to_core), step * CORES + to_core, (RING - step) * CORES + core))
            peers.append(
                (along_x(step, to_core), (RING + step) * CORES + to_core, (2 * RING - step) * CORES + core)
            )
    peers.append((along_x(0, 1 - core), 1 - core, core))

    fetch = pltpu.make_async_copy(coeff_hbm, coeff, local_sems.at[0])
    fetch.start()
    barrier = pltpu.get_barrier_semaphore()
    for peer, _, _ in peers:
        pl.semaphore_signal(barrier, inc=1, device_id={"pairs": peer}, device_id_type=MESH)
    for plane in (above, below):
        pl.semaphore_signal(barrier, inc=1, device_id={"ri": plane}, device_id_type=MESH)

    def ask(n):
        peer, _, there = peers[n]
        return pltpu.make_async_remote_copy(
            src_ref=request,
            dst_ref=asked.at[there],
            send_sem=ask_out.at[n],
            recv_sem=ask_in.at[there],
            device_id={"pairs": peer},
            device_id_type=MESH,
        )

    ports = []
    for chunk in range(4):
        by_x = chunk % 2 == 0
        first_to, other_to = (along_x, along_y) if by_x else (along_y, along_x)
        u, v = (at_x, at_y) if by_x else (at_y, at_x)
        bufs = [group_bufs[chunk] for group_bufs in relay_bufs]
        ports.append(Relay(chunk, first_to, other_to, u, v, core, bufs, out_sems, in_sems))
    singles = []
    for n in range(2):
        gather_to, deliver_to = (along_x, along_y) if n == 0 else (along_y, along_x)
        bufs = [group_bufs[n] for group_bufs in single_bufs]
        singles.append(Ports(n, gather_to, deliver_to, *bufs, single_out, single_in, core))

    square = (ATOMS * MAIN, ATOMS * MAIN)
    out_at = lax.broadcasted_iota(jnp.int32, square, 0)
    from_at = lax.broadcasted_iota(jnp.int32, square, 1)
    band_at, atom_at = out_at & (MAIN - 1), lax.shift_right_logical(out_at, 4)
    perm_main[...] = jnp.where(band_at * ATOMS + atom_at == from_at, 1.0, 0.0).astype(jnp.bfloat16)
    rest_at = lax.shift_right_logical(band_at, 2) * (REM * ATOMS) + (band_at & (REM - 1)) * ATOMS + atom_at
    perm_rest[...] = jnp.where(rest_at == from_at, 1.0, 0.0).astype(jnp.bfloat16)

    def main_rows(tiles):
        flat = blocks[:MAIN, :, tiles[0] * LANES : (tiles[-1] + 1) * LANES]
        flat = flat.reshape(MAIN * ATOMS, len(tiles) * LANES)
        return jnp.dot(perm_main[...], flat, preferred_element_type=jnp.float32).astype(jnp.bfloat16)

    def form(chunk):
        main = main_rows(MAINS[chunk])
        for n in range(len(MAINS[chunk])):
            wires[chunk][n] = main[:, n * LANES : (n + 1) * LANES].reshape(ATOMS, MAIN, LANES)
        parts = [blocks[MAIN:, :, t * LANES : (t + 1) * LANES].reshape(REM * ATOMS, LANES) for t in RESTS[chunk]]
        stacked = jnp.concatenate(parts, axis=0)
        depth = stacked.shape[0]
        late = jnp.dot(perm_rest[:, :depth], stacked, preferred_element_type=jnp.float32).astype(jnp.bfloat16)
        wires[chunk][RING - 1] = late.reshape(ATOMS, MAIN, LANES)

    form(0)
    pl.semaphore_wait(barrier, len(peers) + 2)
    ports[0].start_spread()
    for chunk in range(1, 4):
        form(chunk)
        ports[chunk].start_spread()
    for n in range(2):
        single_wires[n][...] = main_rows(SINGLES[n : n + 1]).reshape(ATOMS, MAIN, LANES)
    for chunk in (0, 1):
        ports[chunk].forward_spread()
    for chunk in (0, 1):
        ports[chunk].finish_spread()
        ports[chunk].start_gather()

    for chunk in (2, 3):
        ports[chunk].forward_spread()

    def parts_of(atom):
        owner = lax.shift_right_logical(atom, 4)
        chip = lax.shift_right_logical(owner, 1)
        return owner, owner & (CORES - 1), chip & (RING - 1), lax.shift_right_logical(chip, 2), atom & (ATOMS - 1)

    map_shape = (8, LANES)
    map_row = lax.broadcasted_iota(jnp.int32, map_shape, 0)
    map_lane = lax.broadcasted_iota(jnp.int32, map_shape, 1)
    atom_map = map_row * LANES + map_lane
    pairs = domains.shape[1]

    def mark(pair, seen):
        for k in range(DOM):
            seen = jnp.where(atom_map == domains[k, pair], 1, seen)
        return seen

    named = lax.fori_loop(0, pairs, mark, jnp.zeros(map_shape, jnp.int32))
    owner, owner_core, owner_x, owner_y, local = parts_of(atom_map)
    rank = named
    for shift in (1, 2, 4, 8):
        rank = rank + jnp.where(local >= shift, pltpu.roll(rank, shift, 1), 0)
    order = named
    for shift in (1, 2, 4, 8, 16, 32, 64):
        order = order + jnp.where(map_lane >= shift, pltpu.roll(order, shift, 1), 0)
    counted = order
    map_rows = ATOMS * RING * RING * CORES // LANES
    for n in range(map_rows - 1):
        order = order + jnp.where(map_row > n, counted[n : n + 1, LANES - 1 :], 0)
    rel_x = (owner_x + RING - at_x) & (RING - 1)
    rel_y = (owner_y + RING - at_y) & (RING - 1)
    tables[0] = order - 1
    tables[1] = ((rel_y * CORES + owner_core) * RING + rel_x) * CAP + rank - 1
    tables[2] = ((rel_x * CORES + owner_core) * RING + rel_y) * CAP + rank - 1
    table_copy = pltpu.make_async_copy(tables, places, local_sems.at[3])
    table_copy.start()

    ids[:map_rows, :] = jnp.where(named > 0, order, 0)[:map_rows]
    ids[map_rows:, :] = jnp.where(named > 0, rank, 0)[:map_rows]
    upright = ids[...].T
    list_shape = (LANES, LANES)
    list_row = lax.broadcasted_iota(jnp.int32, list_shape, 0)
    list_lane = lax.broadcasted_iota(jnp.int32, list_shape, 1)
    rows = [jnp.zeros((1, LANES), jnp.int32) for _ in range(CAP + 2)]
    for n in range(map_rows):
        owner, owner_core, owner_x, owner_y, local = parts_of(list_row + n * LANES)
        own_lane = jnp.where(owner == list_lane, local, 0)
        order_at = jnp.broadcast_to(upright[:, n : n + 1], list_shape)
        rank_at = jnp.broadcast_to(upright[:, map_rows + n : map_rows + n + 1], list_shape)
        for j in range(CAP):
            rows[j] += jnp.sum(jnp.where(rank_at == j + 1, own_lane, 0), axis=0, keepdims=True)
        for j, (u, v) in enumerate(((owner_x, owner_y), (owner_y, owner_x))):
            held_at = ((v * CORES + owner_core) * RING + u) * ATOMS + local
            rows[CAP + j] += jnp.sum(jnp.where(order_at == list_lane + 1, held_at, 0), axis=0, keepdims=True)
    for n in range(CAP + 2):
        request[n : n + 1, :] = rows[n]
    request[CAP + 2 :, :] = jnp.zeros((6 - CAP, LANES), jnp.int32)

    for n in range(len(peers)):
        ask(n).start()
    own_ask = pltpu.make_async_copy(request, asked.at[core], local_sems.at[1])
    own_ask.start()
    for chunk in (2, 3):
        ports[chunk].finish_spread()

    shape = (DEPTH, DOM * BAND)
    row = lax.broadcasted_iota(jnp.int32, shape, 0)
    col = lax.broadcasted_iota(jnp.int32, shape, 1)
    split = DOM * MAIN
    late = row - split
    source = jnp.where(
        row < split,
        lax.shift_right_logical(row, 4) * BAND + (row & (MAIN - 1)),
        lax.shift_right_arithmetic(late, 2) * BAND + MAIN + (late & (REM - 1)),
    )
    perm[...] = jnp.where((source == col) & (row < DOM * BAND), 1.0, 0.0).astype(jnp.bfloat16)
    same[...] = jnp.where(
        lax.broadcasted_iota(jnp.int32, same.shape, 0) == lax.broadcasted_iota(jnp.int32, same.shape, 1), 1.0, 0.0
    ).astype(jnp.bfloat16)
    for n in range(2):
        blk[n, DOM * BAND :, :] = jnp.zeros((DEPTH - DOM * BAND, blk.shape[2]), jnp.bfloat16)
    fetch.wait()

    def prepare(begin, end):
        def turn(pair, _):
            ordered = [
                jnp.dot(perm[...], coeff[4 * pair + n], preferred_element_type=jnp.float32).astype(jnp.bfloat16)
                for n in range(4)
            ]
            for n in range(4):
                turned = lax.dot_general(
                    same[...], ordered[n], (((1,), (1,)), ((), ())), preferred_element_type=jnp.float32
                )
                coeff_t[4 * pair + n] = turned.astype(jnp.bfloat16)
            return 0

        lax.fori_loop(begin // 4, end // 4, turn, 0)

    prepare(0, 4)
    for chunk in (0, 1):
        ports[chunk].forward_gather()
    for chunk in (2, 3):
        ports[chunk].start_gather()

    for single in singles:
        single.start_gather()
    prepare(4, 12)

    own_ask.wait()
    for n in range(len(peers)):
        _, here, _ = peers[n]
        pltpu.make_async_remote_copy(
            src_ref=request,
            dst_ref=asked.at[here],
            send_sem=ask_out.at[n],
            recv_sem=ask_in.at[here],
            device_id={"pairs": peers[n][0]},
            device_id_type=MESH,
        ).wait_recv()
    to_smem = pltpu.make_async_copy(asked, asked_smem, local_sems.at[2])
    to_smem.start()
    to_smem.wait()

    def line_of(dest, on_row):
        return jnp.where(dest < CORES, dest, dest + ROW_LINES) if on_row else dest

    def pick_single(n):
        port = singles[n]
        owner_of = along_x if n == 0 else along_y

        def serve(dest, _):
            line = line_of(dest, n == 1)
            step, to_core = dest // CORES, dest % CORES
            for r in range(RING):
                for j in range(CAP):
                    atom = asked_smem[line, j, owner_of(r, core)]
                    found = port.wire[atom] if r == 0 else port.ring[r - 1, atom]
                    port.send[step, to_core, r * CAP + j] = found
            return 0

        lax.fori_loop(2 * CORES, 3 * CORES, serve, 0)
        port.start_far()

        def serve_near(dest, _):
            return serve(jnp.where(dest < 2 * CORES, dest, dest + CORES), 0)

        lax.fori_loop(0, 3 * CORES, serve_near, 0)
        port.start_near()

    def pick(chunk):
        port = ports[chunk]

        def serve(dest, _):
            line = line_of(dest, chunk % 2 == 0)
            step, to_core = dest // CORES, dest % CORES
            for n in range(SHARE):
                port.send[step, to_core, n] = port.table[asked_smem[line, CAP + chunk % 2, core * SHARE + n]]
            return 0

        lax.fori_loop(2 * CORES, 3 * CORES, serve, 0)
        port.start_far()

        def serve_near(dest, _):
            return serve(jnp.where(dest < 2 * CORES, dest, dest + CORES), 0)

        lax.fori_loop(0, 3 * CORES, serve_near, 0)
        port.start_near()

    for chunk in (0, 1):
        ports[chunk].finish_gather()
    for chunk in (0, 1):
        ports[chunk].finish_share()
        pick(chunk)
    for chunk in (2, 3):
        ports[chunk].forward_gather()
    for single in singles:
        single.forward_gather()
    prepare(12, 20)
    for chunk in (0, 1):
        ports[chunk].forward_delivery()
    prepare(20, 24)
    for chunk in (2, 3):
        ports[chunk].finish_gather()
    for n in range(2):
        singles[n].finish_gather()
        pick_single(n)
    for chunk in (2, 3):
        ports[chunk].finish_share()
        pick(chunk)
    prepare(24, 32)
    for single in singles:
        single.forward_delivery()
    for chunk in (2, 3):
        ports[chunk].forward_delivery()

    pack_row = lax.broadcasted_iota(jnp.int32, (MAXPNO, MAXPNO), 0)
    pack_col = lax.broadcasted_iota(jnp.int32, (MAXPNO, MAXPNO), 1)
    pack_lane = lax.broadcasted_iota(jnp.int32, (MAXPNO, LANES), 1)
    fold_lane = lax.broadcasted_iota(jnp.int32, (FOLD_ROWS, LANES), 1)

    def assemble(pair, slot, chunks):
        base = MAIN * DOM
        begin = 0
        upper = lax.broadcasted_iota(jnp.int32, (8, LANES), 0) < REM

        names = [domains[k, pair] for k in range(DOM)]

        def named_at(table):
            return [places[table, lax.shift_right_logical(a, 7), a & (LANES - 1)] for a in names]

        at = named_at(0)
        for chunk in chunks:
            tiles = len(RESTS[chunk])
            for n in range(RING - 1):
                span = slice(begin + n * LANES, begin + (n + 1) * LANES)
                for k in range(DOM):
                    blk[slot, MAIN * k : MAIN * (k + 1), span] = recvs[chunk][n, at[k]]
            if tiles == RING:
                span = slice(begin + (RING - 1) * LANES, begin + RING * LANES)
                single_at = named_at(1 + chunk % 2)
                for k in range(DOM):
                    blk[slot, MAIN * k : MAIN * (k + 1), span] = single_recvs[chunk % 2][single_at[k]]
            for k in range(0, DOM, 4):
                rest = [recvs[chunk][RING - 1, at[k + n]].astype(jnp.float32) for n in range(4)]
                for half in range((tiles + 1) // 2):
                    parts = [r[8 * half : 8 * half + 8] for r in rest]
                    shifted = [pltpu.roll(part, REM, 0) for part in parts]
                    for q in range(2 * half, min(2 * half + 2, tiles)):
                        first, second = (parts, shifted) if q % 2 == 0 else (shifted, parts)
                        low = jnp.where(upper, first[0], second[1])
                        high = jnp.where(upper, first[2], second[3])
                        both = jnp.concatenate([low, high], axis=0).astype(jnp.bfloat16)
                        tile = slice(begin + q * LANES, begin + (q + 1) * LANES)
                        blk[slot, base + REM * k : base + REM * (k + 4), tile] = both
            begin += tiles * LANES
        return begin

    def multiply(pair, slot, cols):
        weights = coeff_t[pair]
        result = jnp.zeros((MAXPNO, MAXPNO), jnp.float32)
        for at in range(0, cols, 256):
            vec = jnp.dot(weights, blk[slot, :, at : at + 256], preferred_element_type=jnp.float32)
            vec = vec.astype(jnp.bfloat16)
            result += lax.dot_general(vec, vec, (((1,), (1,)), ((), ())), preferred_element_type=jnp.float32)
        return result

    early_cols = LANES * (len(RESTS[0]) + len(RESTS[1]))
    late_cols = LANES * (len(RESTS[2]) + len(RESTS[3]))
    group = coeff.shape[0] // planes
    half_ring = planes // 2
    part = HALF_PACK // 2

    def rows_of(half, piece):
        return pl.ds(pl.multiple_of(half * HALF_PACK + piece * part, 8), part)

    def chain(way, step, half, piece):
        rows = rows_of(half, piece)
        return pltpu.make_async_remote_copy(
            src_ref=sums.at[way, step, rows],
            dst_ref=sums.at[way, step + 1, rows],
            send_sem=sum_out.at[(way * half_ring + step) * 2 + half, piece],
            recv_sem=sum_in.at[(way * half_ring + step) * 2 + half, piece],
            device_id={"ri": jnp.where(way == 0, above, below)},
            device_id_type=MESH,
        )

    def locate(item):
        step = (item + 1) // 2
        way = jnp.where(item == 0, 0, (item + 1) % 2)
        away = jnp.where(way == 0, half_ring - step, half_ring + step)
        return way, step, lax.rem(at_z + away, planes) * group

    def first_half(step, _):
        pair = locate(step // 2)[2] + 2 * (step % 2)
        following = locate((step + 1) // 2)[2] + 2 * ((step + 1) % 2)
        assemble(pair + 1, 1, (0, 1))
        total[pair] = multiply(pair, 0, early_cols)
        assemble(following, 0, (0, 1))
        total[pair + 1] = multiply(pair + 1, 1, early_cols)
        return 0

    def block_products(slot, first, following, whole):
        chunks = (0, 1, 2, 3) if whole else (2, 3)
        cols = early_cols + late_cols if whole else late_cols

        def one(duo, _):
            pair = first + 2 * duo
            assemble(pair + 1, 1, chunks)
            here = multiply(pair, 0, cols)
            assemble(jnp.where(duo == 0, pair + 2, following), 0, chunks)
            there = multiply(pair + 1, 1, cols)
            if not whole:
                here += total[pair]
                there += total[pair + 1]
            squares[duo, :MAXPNO, :MAXPNO] = jnp.where(pack_row >= pack_col, here, there)
            diagonal = jnp.sum(jnp.where(pack_row == pack_col, there, 0.0), axis=0, keepdims=True)
            at = DIAG_AT + 2 * duo
            fresh[slot, pl.ds(at, 1), :] = diagonal[:, :LANES]
            fresh[slot, pl.ds(at + 1, 1), :REST] = diagonal[:, LANES:]
            return 0

        lax.fori_loop(0, 2, one, 0)
        fresh[slot, :MAXPNO, :] = squares[0, :MAXPNO, :LANES]
        fresh[slot, HALF_PACK : HALF_PACK + MAXPNO, :] = squares[1, :MAXPNO, :LANES]
        shared = jnp.where(
            pack_lane < REST, squares[0, :MAXPNO, LANES:], pltpu.roll(squares[1, :MAXPNO, LANES:], REST, 1)
        )
        fresh[slot, MAXPNO:HALF_PACK, :] = shared[:TOP]
        fresh[slot, HALF_PACK + MAXPNO : FOLD_AT, :] = shared[TOP:]
        folded = jnp.zeros((FOLD_ROWS, LANES), jnp.float32)
        for n in range(SQUARE_ROWS // FOLD_ROWS):
            rows = squares[1, n * FOLD_ROWS : (n + 1) * FOLD_ROWS, LANES:]
            moved = pltpu.roll(rows, (n * LEFT - SPARE) % LANES, 1)
            folded = jnp.where((fold_lane >= n * LEFT) & (fold_lane < (n + 1) * LEFT), moved, folded)
        fresh[slot, FOLD_AT:DIAG_AT, :] = folded

    def begin_half(slot, way, step, half):
        for piece in range(2):
            rows = rows_of(half, piece)
            sums[way, step, rows, :] = fresh[slot, rows, :]
            chain(way, step, half, piece).start()

    def add_half(way, step, half):
        for piece in range(2):
            rows = rows_of(half, piece)
            chain(way, step - 1, half, piece).wait_recv()
            sums[way, step, rows, :] = sums[way, step, rows, :] + fresh[way, rows, :]
            chain(way, step, half, piece).start()

    def ring_item(whole, item, _):
        way, step, first = locate(item)
        block_products(way, first, locate(item + 1)[2], whole)

        @pl.when(item == 0)
        def _():
            begin_half(0, 0, 0, 0)
            begin_half(0, 1, 0, 1)

        @pl.when(step == 1)
        def _():
            begin_half(way, way, step, 1 - way)

        @pl.when((step > 1) & (step < half_ring))
        def _():
            add_half(way, step, 1 - way)

        @pl.when((way == 1) & (step < half_ring))
        def _():
            add_half(0, step, 0)
            add_half(1, step, 1)

        @pl.when(item == 2)
        def _():
            for n in range(len(peers)):
                ask(n).wait_send()
            for port in ports:
                port.finish_sends()
            for single in singles:
                single.finish_served()
                single.finish_sends()

        return 0

    fresh[...] = jnp.zeros_like(fresh)
    squares[...] = jnp.zeros_like(squares)
    ahead = 4
    table_copy.wait()
    ports[0].finish_delivery()
    ports[1].finish_delivery()
    assemble(locate(0)[2], 0, (0, 1))
    lax.fori_loop(0, 2 * ahead, first_half, 0)
    for single in singles:
        single.finish_delivery()
    ports[2].finish_delivery()
    ports[3].finish_delivery()
    assemble(locate(0)[2], 0, (2, 3))
    lax.fori_loop(0, ahead, functools.partial(ring_item, False), 0)
    assemble(locate(ahead)[2], 0, (0, 1, 2, 3))
    lax.fori_loop(ahead, planes, functools.partial(ring_item, True), 0)
    for half in (1, 0):
        for piece in range(2):
            rows = rows_of(half, piece)
            for way in range(2):
                chain(way, half_ring - 1, half, piece).wait_recv()
            arrived = sums[0, half_ring, rows, :] + sums[1, half_ring, rows, :]
            out[rows, :] = arrived + fresh[0, rows, :]
    for n in range(group):
        count = counts[at_z * group + n].astype(jnp.float32)
        out[COUNTS + n : COUNTS + n + 1, :] = jnp.full((1, LANES), count)
    for step in range(half_ring):
        for way in range(2):
            for half in range(2):
                if step or half == way:
                    for piece in range(2):
                        chain(way, step, half, piece).wait_send()


def pair_products(blocks, domains, counts, coeff, planes):
    pair_dev, depth, slots = coeff.shape
    lines = 2 * RING * CORES
    bf16 = jnp.bfloat16
    tile = (MAIN, LANES)
    scratch = []
    for shape in (
        (RING, ATOMS),
        (RING * RING * CORES * ATOMS,),
        (2, ATOMS // 2),
        (RING, CORES, SHARE),
        (2, CORES, HALF_SHARE),
        (RING, SLOTS),
    ):
        scratch += [pltpu.VMEM(shape + tile, bf16)] * 4
    for shape in (
        (ATOMS,),
        (RING - 1, ATOMS),
        (RING, CORES, PICKS),
        (2, CORES, HALF),
        (RING * CORES * PICKS,),
    ):
        scratch += [pltpu.VMEM(shape + tile, bf16)] * 2
    scratch += [
        pltpu.VMEM((lines, 8, LANES), jnp.int32),
        pltpu.SMEM((lines, 8, LANES), jnp.int32),
        pltpu.VMEM((3, 8, LANES), jnp.int32),
        pltpu.SMEM((3, 8, LANES), jnp.int32),
        pltpu.VMEM((8, LANES), jnp.int32),
        pltpu.VMEM((8, LANES), jnp.int32),
        pltpu.VMEM((ATOMS * MAIN, ATOMS * MAIN), bf16),
        pltpu.VMEM((ATOMS * MAIN, ATOMS * MAIN), bf16),
        pltpu.VMEM((pair_dev, depth, slots), bf16),
        pltpu.VMEM((pair_dev, MAXPNO, DEPTH), bf16),
        pltpu.VMEM((DEPTH, depth), bf16),
        pltpu.VMEM((2, DEPTH, blocks.shape[2]), bf16),
        pltpu.VMEM((pair_dev, MAXPNO, MAXPNO), jnp.float32),
        pltpu.VMEM((2, planes // 2 + 1, PACK, LANES), jnp.float32),
        pltpu.VMEM((2, PACK, LANES), jnp.float32),
        pltpu.VMEM((MAXPNO, slots), bf16),
        pltpu.VMEM((2, SQUARE_ROWS, 2 * LANES), jnp.float32),
        pltpu.SemaphoreType.DMA((4, 27)),
        pltpu.SemaphoreType.DMA((4, 27)),
        pltpu.SemaphoreType.DMA((2, 16)),
        pltpu.SemaphoreType.DMA((2, 16)),
        pltpu.SemaphoreType.DMA((lines,)),
        pltpu.SemaphoreType.DMA((lines,)),
        pltpu.SemaphoreType.DMA((4,)),
        pltpu.SemaphoreType.DMA((2 * planes, 2)),
        pltpu.SemaphoreType.DMA((2 * planes, 2)),
    ]
    return pl.pallas_call(
        main_kernel,
        out_shape=pltpu.VMEM((PACK, LANES), jnp.float32),
        in_specs=[
            pl.BlockSpec(memory_space=pltpu.VMEM),
            pl.BlockSpec(memory_space=pltpu.SMEM),
            pl.BlockSpec(memory_space=pltpu.SMEM),
            pl.BlockSpec(memory_space=pl.ANY),
        ],
        out_specs=pl.BlockSpec(memory_space=pltpu.VMEM),
        scratch_shapes=scratch,
        compiler_params=params(60, collective_id=0, has_side_effects=True),
    )(blocks, domains, counts, coeff)


def tail_kernel(packed, amp, energy_row, energy_col, out, wide):
    slots = amp.shape[1]
    step = pl.program_id(0)
    full_row = lax.broadcasted_iota(jnp.int32, (slots, slots), 0)
    full_col = lax.broadcasted_iota(jnp.int32, (slots, slots), 1)
    lane = lax.broadcasted_iota(jnp.int32, (MAXPNO, LANES), 1)
    fold_lane = lax.broadcasted_iota(jnp.int32, (FOLD_ROWS, LANES), 1)
    wide[MAXPNO:, :] = jnp.zeros((slots - MAXPNO, slots), jnp.float32)

    def shared_at(begin, end):
        if end <= TOP:
            return packed[MAXPNO + begin : MAXPNO + end, :]
        return packed[HALF_PACK + MAXPNO + begin - TOP : HALF_PACK + MAXPNO + end - TOP, :]

    @pl.when(step == 0)
    def _():
        wide[:MAXPNO, :LANES] = packed[:MAXPNO, :]
        for begin, end in ((0, TOP), (TOP, MAXPNO)):
            wide[begin:end, LANES:] = jnp.where(lane[begin:end] < REST, shared_at(begin, end), 0.0)

    @pl.when(step == 1)
    def _():
        wide[:MAXPNO, :LANES] = packed[HALF_PACK : HALF_PACK + MAXPNO, :]
        for begin, end in ((0, TOP), (TOP, MAXPNO)):
            turned = pltpu.roll(shared_at(begin, end), SPARE, 1)
            wide[begin:end, LANES:] = jnp.where(lane[begin:end] < SPARE, turned, 0.0)
        folded = packed[FOLD_AT:DIAG_AT, :]
        for n in range(SQUARE_ROWS // FOLD_ROWS):
            begin, end = n * FOLD_ROWS, min((n + 1) * FOLD_ROWS, MAXPNO)
            moved = pltpu.roll(folded, (SPARE - n * LEFT) % LANES, 1)
            left = (fold_lane >= SPARE) & (fold_lane < REST)
            held = wide[begin:end, LANES:]
            wide[begin:end, LANES:] = jnp.where(left[: end - begin], moved[: end - begin], held)

    square = wide[...]
    at = DIAG_AT + 2 * step
    diagonal = jnp.concatenate([packed[pl.ds(at, 1), :], packed[pl.ds(at + 1, 1), :]], axis=1)
    on_diagonal = full_row == full_col
    for n in range(2):
        count = packed[pl.ds(COUNTS + 2 * step + n, 1), :][:, :1].astype(jnp.int32)
        if n == 0:
            held = jnp.where(full_row >= full_col, square, 0.0)
        else:
            held = jnp.where(full_row < full_col, square, jnp.where(on_diagonal, diagonal, 0.0))
        products = held + jnp.where(on_diagonal, 0.0, held.T)
        valid = (full_row < count) & (full_col < count)
        products = jnp.where(valid, products / NAUX, 0.0)
        amps = amp[n]
        contract = (((1,), (1,)), ((), ()))
        high = products.astype(jnp.bfloat16)
        left = products - high.astype(jnp.float32)
        mid = left.astype(jnp.bfloat16)
        low = (left - mid.astype(jnp.float32)).astype(jnp.bfloat16)
        coupled = lax.dot_general(low, amps, contract, preferred_element_type=jnp.float32)
        coupled += lax.dot_general(mid, amps, contract, preferred_element_type=jnp.float32)
        coupled += lax.dot_general(high, amps, contract, preferred_element_type=jnp.float32)
        energies = energy_col[n] + energy_row[pl.ds(2 * step + n, 1), :]
        result = products + coupled + energies * amps.astype(jnp.float32)
        out[n] = jnp.where(valid, result, 0.0)


def tail(packed, amp, energy):
    subs, slots, _ = amp.shape
    return pl.pallas_call(
        tail_kernel,
        out_shape=jax.ShapeDtypeStruct((subs, slots, slots), jnp.float32),
        grid=(subs // 2,),
        in_specs=[
            pl.BlockSpec((PACK, LANES), lambda i: (0, 0)),
            pl.BlockSpec((2, slots, slots), lambda i: (i, 0, 0)),
            pl.BlockSpec((subs, slots), lambda i: (0, 0)),
            pl.BlockSpec((2, slots, 1), lambda i: (i, 0, 0)),
        ],
        out_specs=pl.BlockSpec((2, slots, slots), lambda i: (i, 0, 0)),
        scratch_shapes=[pltpu.VMEM((slots, slots), jnp.float32)],
        compiler_params=params(32),
    )(packed, amp, energy, energy[:, :, None])


def on_device(atom_blocks, domains, pno_counts, pno_coeffs, amplitudes, pno_energies):
    planes = lax.axis_size("ri")
    mine = pair_products(atom_blocks.transpose(1, 0, 2), domains.T, pno_counts, pno_coeffs, planes)
    return tail(mine, amplitudes, pno_energies)


def solution(mesh):
    placed = (
        P("pairs", None, "ri"),
        P("pairs", None),
        P("pairs"),
        P("pairs", None, None),
        P(("pairs", "ri"), None, None),
        P(("pairs", "ri"), None),
    )
    return jax.shard_map(
        on_device,
        mesh=mesh,
        in_specs=placed,
        out_specs=P(("pairs", "ri"), None, None),
        check_vma=False,
    )
```

```python
import functools

import jax
import jax.numpy as jnp
from jax import lax
from jax.experimental import pallas as pl
from jax.experimental.pallas import tpu as pltpu
from jax.sharding import PartitionSpec as P

NAUX = 14336
CAP = 3
MAXPNO = 200
MAIN = 16
REM = 4
SPLIT = 128
REST = MAXPNO - SPLIT
LANES = 128
MIB = 1 << 20
RING = 4
CORES = 2
ATOMS = 16
DOM = 12
BAND = MAIN + REM
PICKS = RING * CAP
HALF = PICKS // 2
DEPTH = 256
SPARE = LANES - REST
LEFT = REST - SPARE
FOLD_ROWS = 32
HALF_PACK = 320
PACK = 2 * HALF_PACK
TOP = HALF_PACK - MAXPNO
FOLD_AT = PACK - FOLD_ROWS - 8
DIAG_AT = PACK - 8
COUNTS = PACK - 4
SQUARE_ROWS = 224
SLOTS = 48
SHARE = SLOTS // CORES
HALF_SHARE = SHARE // 2
ROW_LINES = RING * CORES
MAINS = ((0, 1, 2), (3, 4, 5), (6, 7, 8), (10, 11, 12))
RESTS = ((0, 1, 2), (3, 4, 5), (6, 7, 8, 9), (10, 11, 12, 13))
SINGLES = (9, 13)
MESH = pl.DeviceIdType.MESH


def params(mib, **kw):
    return pltpu.CompilerParams(vmem_limit_bytes=mib * MIB, **kw)


class Ports:
    def __init__(self, chunk, gather_to, deliver_to, wire, ring, send, relay, recv, out_sems, in_sems, core):
        self.gather_to, self.deliver_to, self.core = gather_to, deliver_to, core
        self.wire, self.ring, self.send, self.relay, self.recv = wire, ring, send, relay, recv
        self.out_sems, self.in_sems, self.chunk = out_sems, in_sems, chunk

    def copy(self, src, dst, out_at, in_at, to):
        return pltpu.make_async_remote_copy(
            src_ref=src,
            dst_ref=dst,
            send_sem=self.out_sems.at[self.chunk, out_at],
            recv_sem=self.in_sems.at[self.chunk, in_at],
            device_id={"pairs": to},
            device_id_type=MESH,
        )

    def gather_first(self):
        up = self.copy(self.wire, self.ring.at[2], 0, 1, self.gather_to(1, self.core))
        down = self.copy(self.wire, self.ring.at[0], 1, 0, self.gather_to(3, self.core))
        return up, down

    def gather_second(self):
        half = ATOMS // 2
        low, high = pl.ds(0, half), pl.ds(half, half)
        up = self.copy(self.ring.at[2, low], self.ring.at[1, low], 2, 2, self.gather_to(1, self.core))
        down = self.copy(self.ring.at[0, high], self.ring.at[1, high], 3, 3, self.gather_to(3, self.core))
        return up, down

    def place(self, rel, core):
        return (rel * CORES + core) * PICKS

    def far(self):
        up = self.copy(self.send.at[2, :, pl.ds(0, HALF)], self.relay.at[0], 4, 4, self.deliver_to(1, self.core))
        down = self.copy(self.send.at[2, :, pl.ds(HALF, HALF)], self.relay.at[1], 5, 5, self.deliver_to(3, self.core))
        return up, down

    def near(self):
        copies = []
        for n, step in enumerate((1, 3)):
            for core in range(CORES):
                dst = self.recv.at[pl.ds(self.place(RING - step, self.core), PICKS)]
                at = 6 + 2 * n
                copies.append(self.copy(self.send.at[step, core], dst, at + core, at + self.core, self.deliver_to(step, core)))
        other = 1 - self.core
        dst = self.recv.at[pl.ds(self.place(0, self.core), PICKS)]
        copies.append(self.copy(self.send.at[0, other], dst, 10, 10, self.deliver_to(0, other)))
        return copies

    def own(self):
        return pltpu.make_async_copy(
            self.send.at[0, self.core],
            self.recv.at[pl.ds(self.place(0, self.core), PICKS)],
            self.in_sems.at[self.chunk, 11],
        )

    def onward(self):
        copies = []
        for way, step in enumerate((1, 3)):
            for core in range(CORES):
                dst = self.recv.at[pl.ds(self.place(2, self.core) + way * HALF, HALF)]
                at = 12 + 2 * way
                copies.append(self.copy(self.relay.at[way, core], dst, at + core, at + self.core, self.deliver_to(step, core)))
        return copies

    def start_gather(self):
        for copy in self.gather_first():
            copy.start()

    def forward_gather(self):
        up, down = self.gather_second()
        first_up, first_down = self.gather_first()
        first_up.wait_recv()
        up.start()
        first_down.wait_recv()
        down.start()

    def finish_gather(self):
        for copy in self.gather_second():
            copy.wait_recv()

    def start_far(self):
        for copy in self.far():
            copy.start()

    def start_near(self):
        for copy in self.near():
            copy.start()
        self.own().start()

    def forward_delivery(self):
        far, onward = self.far(), self.onward()
        for way in range(2):
            far[way].wait_recv()
            for copy in onward[2 * way : 2 * way + 2]:
                copy.start()

    def finish_delivery(self):
        for n, step in enumerate((1, 3)):
            for core in range(CORES):
                dst = self.recv.at[pl.ds(self.place(step, core), PICKS)]
                at = 6 + 2 * (1 - n)
                self.copy(dst, dst, at + core, at + core, self.deliver_to(1, self.core)).wait_recv()
        other = 1 - self.core
        dst = self.recv.at[pl.ds(self.place(0, other), PICKS)]
        self.copy(dst, dst, 10, 10, self.deliver_to(1, self.core)).wait_recv()
        self.own().wait()
        for way in range(2):
            for core in range(CORES):
                dst = self.recv.at[pl.ds(self.place(2, core) + way * HALF, HALF)]
                at = 12 + 2 * way
                self.copy(dst, dst, at + core, at + core, self.deliver_to(1, self.core)).wait_recv()

    def finish_served(self):
        for copy in self.far() + tuple(self.near()):
            copy.wait_send()

    def finish_sends(self):
        for copy in self.gather_first() + self.gather_second() + tuple(self.onward()):
            copy.wait_send()


class Relay:
    def __init__(self, chunk, first_to, other_to, u, v, core, bufs, out_sems, in_sems):
        self.chunk, self.first_to, self.other_to = chunk, first_to, other_to
        self.u, self.v, self.core = u, v, core
        self.wire, self.table, self.passing, self.send, self.relay, self.recv = bufs
        self.out_sems, self.in_sems = out_sems, in_sems

    def copy(self, src, dst, out_at, in_at, to):
        return pltpu.make_async_remote_copy(
            src_ref=src,
            dst_ref=dst,
            send_sem=self.out_sems.at[self.chunk, out_at],
            recv_sem=self.in_sems.at[self.chunk, in_at],
            device_id={"pairs": to},
            device_id_type=MESH,
        )

    def arrival(self, dst, at):
        return self.copy(dst, dst, at, at, self.first_to(1, self.core))

    def near_u(self, step):
        return lax.rem(self.u + step, RING)

    def near_v(self, step):
        return lax.rem(self.v + step, RING)

    def atoms(self, step, at=0, count=ATOMS):
        base = ((self.v * CORES + self.core) * RING + self.near_u(step)) * ATOMS
        return self.table.at[pl.ds(base + at, count)]

    def block(self, step, core, at=0, count=RING * ATOMS):
        return self.table.at[pl.ds((self.near_v(step) * CORES + core) * RING * ATOMS + at, count)]

    def spread_sends(self):
        half = ATOMS // 2
        far = self.near_u(2)
        up, down = self.first_to(1, self.core), self.first_to(3, self.core)
        return [
            self.copy(self.wire.at[far, pl.ds(0, half)], self.passing.at[0], 2, 2, up),
            self.copy(self.wire.at[far, pl.ds(half, half)], self.passing.at[1], 3, 3, down),
            self.copy(self.wire.at[self.near_u(1)], self.atoms(0), 0, 1, up),
            self.copy(self.wire.at[self.near_u(3)], self.atoms(0), 1, 0, down),
        ]

    def spread_own(self):
        return pltpu.make_async_copy(self.wire.at[self.u], self.atoms(0), self.in_sems.at[self.chunk, 25])

    def spread_onward(self):
        half = ATOMS // 2
        return [
            self.copy(self.passing.at[0], self.atoms(3, 0, half), 4, 4, self.first_to(1, self.core)),
            self.copy(self.passing.at[1], self.atoms(1, half, half), 5, 5, self.first_to(3, self.core)),
        ]

    def start_spread(self):
        for copy in self.spread_sends():
            copy.start()
        self.spread_own().start()

    def forward_spread(self):
        for way, copy in enumerate(self.spread_onward()):
            self.arrival(self.passing.at[way], 2 + way).wait_recv()
            copy.start()

    def finish_spread(self):
        half = ATOMS // 2
        self.spread_own().wait()
        self.arrival(self.atoms(1), 0).wait_recv()
        self.arrival(self.atoms(3), 1).wait_recv()
        self.arrival(self.atoms(2, 0, half), 4).wait_recv()
        self.arrival(self.atoms(2, half, half), 5).wait_recv()

    def gather_first(self):
        own = self.block(0, self.core)
        return [
            self.copy(own, own, 6, 7, self.other_to(1, self.core)),
            self.copy(own, own, 7, 6, self.other_to(3, self.core)),
        ]

    def gather_second(self):
        half = RING * ATOMS // 2
        low, high = self.block(3, self.core, 0, half), self.block(1, self.core, half, half)
        return [
            self.copy(low, low, 8, 8, self.other_to(1, self.core)),
            self.copy(high, high, 9, 9, self.other_to(3, self.core)),
        ]

    def share(self, step):
        mine = self.block(step, self.core)
        return self.copy(mine, mine, 10 + step, 10 + step, self.first_to(0, 1 - self.core))

    def start_gather(self):
        for copy in self.gather_first():
            copy.start()
        self.share(0).start()

    def forward_gather(self):
        low, high = self.gather_second()
        self.arrival(self.block(3, self.core), 7).wait_recv()
        low.start()
        self.share(3).start()
        self.arrival(self.block(1, self.core), 6).wait_recv()
        high.start()
        self.share(1).start()

    def finish_gather(self):
        half = RING * ATOMS // 2
        self.arrival(self.block(2, self.core, 0, half), 8).wait_recv()
        self.arrival(self.block(2, self.core, half, half), 9).wait_recv()
        self.share(2).start()

    def finish_share(self):
        for step in range(RING):
            self.arrival(self.block(step, 1 - self.core), 10 + step).wait_recv()

    def place(self, step, core, at=0, count=SHARE):
        return self.recv.at[self.near_u(step), pl.ds(core * SHARE + at, count)]

    def far(self):
        return [
            self.copy(self.send.at[2, :, pl.ds(0, HALF_SHARE)], self.relay.at[0], 19, 19, self.first_to(1, self.core)),
            self.copy(
                self.send.at[2, :, pl.ds(HALF_SHARE, HALF_SHARE)], self.relay.at[1], 20, 20, self.first_to(3, self.core)
            ),
        ]

    def near(self):
        copies = []
        dst = self.place(0, self.core)
        for n, step in enumerate((1, 3)):
            for core in range(CORES):
                at = 14 + 2 * n
                copies.append(self.copy(self.send.at[step, core], dst, at + core, at + self.core, self.first_to(step, core)))
        other = 1 - self.core
        copies.append(self.copy(self.send.at[0, other], dst, 18, 18, self.first_to(0, other)))
        return copies

    def own(self):
        return pltpu.make_async_copy(
            self.send.at[0, self.core], self.place(0, self.core), self.in_sems.at[self.chunk, 26]
        )

    def onward(self):
        copies = []
        for way, step in enumerate((1, 3)):
            dst = self.place(RING - step, self.core, way * HALF_SHARE, HALF_SHARE)
            for core in range(CORES):
                at = 21 + 2 * way
                copies.append(self.copy(self.relay.at[way, core], dst, at + core, at + self.core, self.first_to(step, core)))
        return copies

    def start_far(self):
        for copy in self.far():
            copy.start()

    def start_near(self):
        for copy in self.near():
            copy.start()
        self.own().start()

    def forward_delivery(self):
        onward = self.onward()
        for way in range(2):
            self.arrival(self.relay.at[way], 19 + way).wait_recv()
            for copy in onward[2 * way : 2 * way + 2]:
                copy.start()

    def finish_delivery(self):
        for core in range(CORES):
            self.arrival(self.place(3, core), 14 + core).wait_recv()
            self.arrival(self.place(1, core), 16 + core).wait_recv()
            for way in range(2):
                at = 21 + 2 * way + core
                self.arrival(self.place(2, core, way * HALF_SHARE, HALF_SHARE), at).wait_recv()
        self.arrival(self.place(0, 1 - self.core), 18).wait_recv()
        self.own().wait()

    def finish_sends(self):
        copies = self.spread_sends() + self.spread_onward() + self.gather_first() + self.gather_second()
        copies += [self.share(step) for step in range(RING)] + self.far() + self.near() + self.onward()
        for copy in copies:
            copy.wait_send()


def main_kernel(
    blocks_hbm, domains, counts, coeff_hbm, out, *scratch
):
    relay_bufs = [scratch[4 * n : 4 * n + 4] for n in range(6)]
    single_bufs = [scratch[24 + 2 * n : 26 + 2 * n] for n in range(5)]
    wires, recvs = relay_bufs[0], relay_bufs[5]
    single_wires, single_recvs = single_bufs[0], single_bufs[4]
    asked, asked_smem, tables, places, request, ids, perm_main, perm_rest = scratch[34:42]
    coeff, coeff_t, perm, blk, total, sums, fresh, same, squares, blocks = scratch[42:52]
    out_sems, in_sems, single_out, single_in, ask_out, ask_in, local_sems, sum_out, sum_in = scratch[52:61]
    me = lax.axis_index("pairs")
    at_z = lax.axis_index("ri")
    planes = 2 * (sums.shape[1] - 1)
    above, below = lax.rem(at_z + 1, planes), lax.rem(at_z + planes - 1, planes)
    core = lax.rem(me, CORES)
    chip = lax.div(me, CORES)
    at_x = lax.rem(chip, RING)
    at_y = lax.div(chip, RING)

    def along_x(step, to_core):
        return (at_y * RING + lax.rem(at_x + step, RING)) * CORES + to_core

    def along_y(step, to_core):
        return (lax.rem(at_y + step, RING) * RING + at_x) * CORES + to_core

    peers = []
    for to_core in range(2):
        for step in range(1, RING):
            peers.append((along_y(step, to_core), step * CORES + to_core, (RING - step) * CORES + core))
            peers.append(
                (along_x(step, to_core), (RING + step) * CORES + to_core, (2 * RING - step) * CORES + core)
            )
    peers.append((along_x(0, 1 - core), 1 - core, core))

    barrier = pltpu.get_barrier_semaphore()
    for peer, _, _ in peers:
        pl.semaphore_signal(barrier, inc=1, device_id={"pairs": peer}, device_id_type=MESH)
    for plane in (above, below):
        pl.semaphore_signal(barrier, inc=1, device_id={"ri": plane}, device_id_type=MESH)

    def ask(n):
        peer, _, there = peers[n]
        return pltpu.make_async_remote_copy(
            src_ref=request,
            dst_ref=asked.at[there],
            send_sem=ask_out.at[n],
            recv_sem=ask_in.at[there],
            device_id={"pairs": peer},
            device_id_type=MESH,
        )

    ports = []
    for chunk in range(4):
        by_x = chunk % 2 == 0
        first_to, other_to = (along_x, along_y) if by_x else (along_y, along_x)
        u, v = (at_x, at_y) if by_x else (at_y, at_x)
        bufs = [group_bufs[chunk] for group_bufs in relay_bufs]
        ports.append(Relay(chunk, first_to, other_to, u, v, core, bufs, out_sems, in_sems))
    singles = []
    for n in range(2):
        gather_to, deliver_to = (along_x, along_y) if n == 0 else (along_y, along_x)
        bufs = [group_bufs[n] for group_bufs in single_bufs]
        singles.append(Ports(n, gather_to, deliver_to, *bufs, single_out, single_in, core))

    fetches = []
    for chunk in range(4):
        tiles = RESTS[chunk]
        cols = pl.ds(tiles[0] * LANES, len(tiles) * LANES)
        fetches.append(
            pltpu.make_async_copy(blocks_hbm.at[:, :, cols], blocks.at[:, :, cols], local_sems.at[4 + chunk])
        )
        fetches[chunk].start()
    fetch = pltpu.make_async_copy(coeff_hbm, coeff, local_sems.at[0])
    fetch.start()

    square = (ATOMS * MAIN, ATOMS * MAIN)
    out_at = lax.broadcasted_iota(jnp.int32, square, 0)
    from_at = lax.broadcasted_iota(jnp.int32, square, 1)
    band_at, atom_at = out_at & (MAIN - 1), lax.shift_right_logical(out_at, 4)
    perm_main[...] = jnp.where(band_at * ATOMS + atom_at == from_at, 1.0, 0.0).astype(jnp.bfloat16)
    rest_at = lax.shift_right_logical(band_at, 2) * (REM * ATOMS) + (band_at & (REM - 1)) * ATOMS + atom_at
    perm_rest[...] = jnp.where(rest_at == from_at, 1.0, 0.0).astype(jnp.bfloat16)

    def main_rows(tiles):
        flat = blocks[:MAIN, :, tiles[0] * LANES : (tiles[-1] + 1) * LANES]
        flat = flat.reshape(MAIN * ATOMS, len(tiles) * LANES)
        return jnp.dot(perm_main[...], flat, preferred_element_type=jnp.float32).astype(jnp.bfloat16)

    def form(chunk):
        fetches[chunk].wait()
        main = main_rows(MAINS[chunk])
        for n in range(len(MAINS[chunk])):
            wires[chunk][n] = main[:, n * LANES : (n + 1) * LANES].reshape(ATOMS, MAIN, LANES)
        parts = [blocks[MAIN:, :, t * LANES : (t + 1) * LANES].reshape(REM * ATOMS, LANES) for t in RESTS[chunk]]
        stacked = jnp.concatenate(parts, axis=0)
        depth = stacked.shape[0]
        late = jnp.dot(perm_rest[:, :depth], stacked, preferred_element_type=jnp.float32).astype(jnp.bfloat16)
        wires[chunk][RING - 1] = late.reshape(ATOMS, MAIN, LANES)

    form(0)
    pl.semaphore_wait(barrier, len(peers) + 2)
    ports[0].start_spread()
    for chunk in range(1, 4):
        form(chunk)
        ports[chunk].start_spread()
    for n in range(2):
        single_wires[n][...] = main_rows(SINGLES[n : n + 1]).reshape(ATOMS, MAIN, LANES)
    for chunk in (0, 1):
        ports[chunk].forward_spread()
    for chunk in (0, 1):
        ports[chunk].finish_spread()
        ports[chunk].start_gather()

    for chunk in (2, 3):
        ports[chunk].forward_spread()

    def parts_of(atom):
        owner = lax.shift_right_logical(atom, 4)
        chip = lax.shift_right_logical(owner, 1)
        return owner, owner & (CORES - 1), chip & (RING - 1), lax.shift_right_logical(chip, 2), atom & (ATOMS - 1)

    map_shape = (8, LANES)
    map_row = lax.broadcasted_iota(jnp.int32, map_shape, 0)
    map_lane = lax.broadcasted_iota(jnp.int32, map_shape, 1)
    atom_map = map_row * LANES + map_lane
    pairs = domains.shape[1]

    def mark(pair, seen):
        for k in range(DOM):
            seen = jnp.where(atom_map == domains[k, pair], 1, seen)
        return seen

    named = lax.fori_loop(0, pairs, mark, jnp.zeros(map_shape, jnp.int32))
    owner, owner_core, owner_x, owner_y, local = parts_of(atom_map)
    rank = named
    for shift in (1, 2, 4, 8):
        rank = rank + jnp.where(local >= shift, pltpu.roll(rank, shift, 1), 0)
    order = named
    for shift in (1, 2, 4, 8, 16, 32, 64):
        order = order + jnp.where(map_lane >= shift, pltpu.roll(order, shift, 1), 0)
    counted = order
    map_rows = ATOMS * RING * RING * CORES // LANES
    for n in range(map_rows - 1):
        order = order + jnp.where(map_row > n, counted[n : n + 1, LANES - 1 :], 0)
    rel_x = (owner_x + RING - at_x) & (RING - 1)
    rel_y = (owner_y + RING - at_y) & (RING - 1)
    tables[0] = order - 1
    tables[1] = ((rel_y * CORES + owner_core) * RING + rel_x) * CAP + rank - 1
    tables[2] = ((rel_x * CORES + owner_core) * RING + rel_y) * CAP + rank - 1
    table_copy = pltpu.make_async_copy(tables, places, local_sems.at[3])
    table_copy.start()

    ids[:map_rows, :] = jnp.where(named > 0, order, 0)[:map_rows]
    ids[map_rows:, :] = jnp.where(named > 0, rank, 0)[:map_rows]
    upright = ids[...].T
    list_shape = (LANES, LANES)
    list_row = lax.broadcasted_iota(jnp.int32, list_shape, 0)
    list_lane = lax.broadcasted_iota(jnp.int32, list_shape, 1)
    rows = [jnp.zeros((1, LANES), jnp.int32) for _ in range(CAP + 2)]
    for n in range(map_rows):
        owner, owner_core, owner_x, owner_y, local = parts_of(list_row + n * LANES)
        own_lane = jnp.where(owner == list_lane, local, 0)
        order_at = jnp.broadcast_to(upright[:, n : n + 1], list_shape)
        rank_at = jnp.broadcast_to(upright[:, map_rows + n : map_rows + n + 1], list_shape)
        for j in range(CAP):
            rows[j] += jnp.sum(jnp.where(rank_at == j + 1, own_lane, 0), axis=0, keepdims=True)
        for j, (u, v) in enumerate(((owner_x, owner_y), (owner_y, owner_x))):
            held_at = ((v * CORES + owner_core) * RING + u) * ATOMS + local
            rows[CAP + j] += jnp.sum(jnp.where(order_at == list_lane + 1, held_at, 0), axis=0, keepdims=True)
    for n in range(CAP + 2):
        request[n : n + 1, :] = rows[n]
    request[CAP + 2 :, :] = jnp.zeros((6 - CAP, LANES), jnp.int32)

    for n in range(len(peers)):
        ask(n).start()
    own_ask = pltpu.make_async_copy(request, asked.at[core], local_sems.at[1])
    own_ask.start()
    for chunk in (2, 3):
        ports[chunk].finish_spread()

    shape = (DEPTH, DOM * BAND)
    row = lax.broadcasted_iota(jnp.int32, shape, 0)
    col = lax.broadcasted_iota(jnp.int32, shape, 1)
    split = DOM * MAIN
    late = row - split
    source = jnp.where(
        row < split,
        lax.shift_right_logical(row, 4) * BAND + (row & (MAIN - 1)),
        lax.shift_right_arithmetic(late, 2) * BAND + MAIN + (late & (REM - 1)),
    )
    perm[...] = jnp.where((source == col) & (row < DOM * BAND), 1.0, 0.0).astype(jnp.bfloat16)
    same[...] = jnp.where(
        lax.broadcasted_iota(jnp.int32, same.shape, 0) == lax.broadcasted_iota(jnp.int32, same.shape, 1), 1.0, 0.0
    ).astype(jnp.bfloat16)
    for n in range(2):
        blk[n, DOM * BAND :, :] = jnp.zeros((DEPTH - DOM * BAND, blk.shape[2]), jnp.bfloat16)
    fetch.wait()

    def prepare(begin, end):
        def turn(pair, _):
            ordered = [
                jnp.dot(perm[...], coeff[4 * pair + n], preferred_element_type=jnp.float32).astype(jnp.bfloat16)
                for n in range(4)
            ]
            for n in range(4):
                turned = lax.dot_general(
                    same[...], ordered[n], (((1,), (1,)), ((), ())), preferred_element_type=jnp.float32
                )
                coeff_t[4 * pair + n] = turned.astype(jnp.bfloat16)
            return 0

        lax.fori_loop(begin // 4, end // 4, turn, 0)

    prepare(0, 4)
    for chunk in (0, 1):
        ports[chunk].forward_gather()
    for chunk in (2, 3):
        ports[chunk].start_gather()

    for single in singles:
        single.start_gather()
    prepare(4, 12)

    own_ask.wait()
    for n in range(len(peers)):
        _, here, _ = peers[n]
        pltpu.make_async_remote_copy(
            src_ref=request,
            dst_ref=asked.at[here],
            send_sem=ask_out.at[n],
            recv_sem=ask_in.at[here],
            device_id={"pairs": peers[n][0]},
            device_id_type=MESH,
        ).wait_recv()
    to_smem = pltpu.make_async_copy(asked, asked_smem, local_sems.at[2])
    to_smem.start()
    to_smem.wait()

    def line_of(dest, on_row):
        return jnp.where(dest < CORES, dest, dest + ROW_LINES) if on_row else dest

    def pick_single(n):
        port = singles[n]
        owner_of = along_x if n == 0 else along_y

        def serve(dest, _):
            line = line_of(dest, n == 1)
            step, to_core = dest // CORES, dest % CORES
            for r in range(RING):
                for j in range(CAP):
                    atom = asked_smem[line, j, owner_of(r, core)]
                    found = port.wire[atom] if r == 0 else port.ring[r - 1, atom]
                    port.send[step, to_core, r * CAP + j] = found
            return 0

        lax.fori_loop(2 * CORES, 3 * CORES, serve, 0)
        port.start_far()

        def serve_near(dest, _):
            return serve(jnp.where(dest < 2 * CORES, dest, dest + CORES), 0)

        lax.fori_loop(0, 3 * CORES, serve_near, 0)
        port.start_near()

    def pick(chunk):
        port = ports[chunk]

        def serve(dest, _):
            line = line_of(dest, chunk % 2 == 0)
            step, to_core = dest // CORES, dest % CORES
            for n in range(SHARE):
                port.send[step, to_core, n] = port.table[asked_smem[line, CAP + chunk % 2, core * SHARE + n]]
            return 0

        lax.fori_loop(2 * CORES, 3 * CORES, serve, 0)
        port.start_far()

        def serve_near(dest, _):
            return serve(jnp.where(dest < 2 * CORES, dest, dest + CORES), 0)

        lax.fori_loop(0, 3 * CORES, serve_near, 0)
        port.start_near()

    for chunk in (0, 1):
        ports[chunk].finish_gather()
    for chunk in (0, 1):
        ports[chunk].finish_share()
        pick(chunk)
    for chunk in (2, 3):
        ports[chunk].forward_gather()
    for single in singles:
        single.forward_gather()
    prepare(12, 20)
    for chunk in (0, 1):
        ports[chunk].forward_delivery()
    prepare(20, 24)
    for chunk in (2, 3):
        ports[chunk].finish_gather()
    for n in range(2):
        singles[n].finish_gather()
        pick_single(n)
    for chunk in (2, 3):
        ports[chunk].finish_share()
        pick(chunk)
    prepare(24, 32)
    for single in singles:
        single.forward_delivery()
    for chunk in (2, 3):
        ports[chunk].forward_delivery()

    pack_row = lax.broadcasted_iota(jnp.int32, (MAXPNO, MAXPNO), 0)
    pack_col = lax.broadcasted_iota(jnp.int32, (MAXPNO, MAXPNO), 1)
    pack_lane = lax.broadcasted_iota(jnp.int32, (MAXPNO, LANES), 1)
    fold_lane = lax.broadcasted_iota(jnp.int32, (FOLD_ROWS, LANES), 1)

    def assemble(pair, slot, chunks):
        base = MAIN * DOM
        begin = 0
        upper = lax.broadcasted_iota(jnp.int32, (8, LANES), 0) < REM

        names = [domains[k, pair] for k in range(DOM)]

        def named_at(table):
            return [places[table, lax.shift_right_logical(a, 7), a & (LANES - 1)] for a in names]

        at = named_at(0)
        for chunk in chunks:
            tiles = len(RESTS[chunk])
            for n in range(RING - 1):
                span = slice(begin + n * LANES, begin + (n + 1) * LANES)
                for k in range(DOM):
                    blk[slot, MAIN * k : MAIN * (k + 1), span] = recvs[chunk][n, at[k]]
            if tiles == RING:
                span = slice(begin + (RING - 1) * LANES, begin + RING * LANES)
                single_at = named_at(1 + chunk % 2)
                for k in range(DOM):
                    blk[slot, MAIN * k : MAIN * (k + 1), span] = single_recvs[chunk % 2][single_at[k]]
            for k in range(0, DOM, 4):
                rest = [recvs[chunk][RING - 1, at[k + n]].astype(jnp.float32) for n in range(4)]
                for half in range((tiles + 1) // 2):
                    parts = [r[8 * half : 8 * half + 8] for r in rest]
                    shifted = [pltpu.roll(part, REM, 0) for part in parts]
                    for q in range(2 * half, min(2 * half + 2, tiles)):
                        first, second = (parts, shifted) if q % 2 == 0 else (shifted, parts)
                        low = jnp.where(upper, first[0], second[1])
                        high = jnp.where(upper, first[2], second[3])
                        both = jnp.concatenate([low, high], axis=0).astype(jnp.bfloat16)
                        tile = slice(begin + q * LANES, begin + (q + 1) * LANES)
                        blk[slot, base + REM * k : base + REM * (k + 4), tile] = both
            begin += tiles * LANES
        return begin

    def multiply(pair, slot, cols):
        weights = coeff_t[pair]
        vecs = []
        for at in range(0, cols, 256):
            vec = jnp.dot(weights, blk[slot, :, at : at + 256], preferred_element_type=jnp.float32)
            vecs.append(vec.astype(jnp.bfloat16))
        vecs = jnp.concatenate(vecs, axis=1)
        return lax.dot_general(vecs, vecs, (((1,), (1,)), ((), ())), preferred_element_type=jnp.float32)

    early_cols = LANES * (len(RESTS[0]) + len(RESTS[1]))
    late_cols = LANES * (len(RESTS[2]) + len(RESTS[3]))
    group = coeff.shape[0] // planes
    half_ring = planes // 2
    part = HALF_PACK // 2

    def rows_of(half, piece):
        return pl.ds(pl.multiple_of(half * HALF_PACK + piece * part, 8), part)

    def chain(way, step, half, piece):
        rows = rows_of(half, piece)
        return pltpu.make_async_remote_copy(
            src_ref=sums.at[way, step, rows],
            dst_ref=sums.at[way, step + 1, rows],
            send_sem=sum_out.at[(way * half_ring + step) * 2 + half, piece],
            recv_sem=sum_in.at[(way * half_ring + step) * 2 + half, piece],
            device_id={"ri": jnp.where(way == 0, above, below)},
            device_id_type=MESH,
        )

    def locate(item):
        step = (item + 1) // 2
        way = jnp.where(item == 0, 0, (item + 1) % 2)
        away = jnp.where(way == 0, half_ring - step, half_ring + step)
        return way, step, lax.rem(at_z + away, planes) * group

    def first_half(step, _):
        pair = locate(step // 2)[2] + 2 * (step % 2)
        following = locate((step + 1) // 2)[2] + 2 * ((step + 1) % 2)
        assemble(pair + 1, 1, (0, 1))
        total[pair] = multiply(pair, 0, early_cols)
        assemble(following, 0, (0, 1))
        total[pair + 1] = multiply(pair + 1, 1, early_cols)
        return 0

    def block_products(slot, first, following, whole):
        chunks = (0, 1, 2, 3) if whole else (2, 3)
        cols = early_cols + late_cols if whole else late_cols

        def one(duo, _):
            pair = first + 2 * duo
            assemble(pair + 1, 1, chunks)
            here = multiply(pair, 0, cols)
            assemble(jnp.where(duo == 0, pair + 2, following), 0, chunks)
            there = multiply(pair + 1, 1, cols)
            if not whole:
                here += total[pair]
                there += total[pair + 1]
            squares[duo, :MAXPNO, :MAXPNO] = jnp.where(pack_row >= pack_col, here, there)
            diagonal = jnp.sum(jnp.where(pack_row == pack_col, there, 0.0), axis=0, keepdims=True)
            at = DIAG_AT + 2 * duo
            fresh[slot, pl.ds(at, 1), :] = diagonal[:, :LANES]
            fresh[slot, pl.ds(at + 1, 1), :REST] = diagonal[:, LANES:]
            return 0

        lax.fori_loop(0, 2, one, 0)
        fresh[slot, :MAXPNO, :] = squares[0, :MAXPNO, :LANES]
        fresh[slot, HALF_PACK : HALF_PACK + MAXPNO, :] = squares[1, :MAXPNO, :LANES]
        shared = jnp.where(
            pack_lane < REST, squares[0, :MAXPNO, LANES:], pltpu.roll(squares[1, :MAXPNO, LANES:], REST, 1)
        )
        fresh[slot, MAXPNO:HALF_PACK, :] = shared[:TOP]
        fresh[slot, HALF_PACK + MAXPNO : FOLD_AT, :] = shared[TOP:]
        folded = jnp.zeros((FOLD_ROWS, LANES), jnp.float32)
        for n in range(SQUARE_ROWS // FOLD_ROWS):
            rows = squares[1, n * FOLD_ROWS : (n + 1) * FOLD_ROWS, LANES:]
            moved = pltpu.roll(rows, (n * LEFT - SPARE) % LANES, 1)
            folded = jnp.where((fold_lane >= n * LEFT) & (fold_lane < (n + 1) * LEFT), moved, folded)
        fresh[slot, FOLD_AT:DIAG_AT, :] = folded

    def begin_half(slot, way, step, half):
        for piece in range(2):
            rows = rows_of(half, piece)
            sums[way, step, rows, :] = fresh[slot, rows, :]
            chain(way, step, half, piece).start()

    def add_half(way, step, half):
        for piece in range(2):
            rows = rows_of(half, piece)
            chain(way, step - 1, half, piece).wait_recv()
            sums[way, step, rows, :] = sums[way, step, rows, :] + fresh[way, rows, :]
            chain(way, step, half, piece).start()

    def ring_item(whole, item, _):
        way, step, first = locate(item)
        block_products(way, first, locate(item + 1)[2], whole)

        @pl.when(item == 0)
        def _():
            begin_half(0, 0, 0, 0)
            begin_half(0, 1, 0, 1)

        @pl.when(step == 1)
        def _():
            begin_half(way, way, step, 1 - way)

        @pl.when((step > 1) & (step < half_ring))
        def _():
            add_half(way, step, 1 - way)

        @pl.when((way == 1) & (step < half_ring))
        def _():
            add_half(0, step, 0)
            add_half(1, step, 1)

        @pl.when(item == 2)
        def _():
            for n in range(len(peers)):
                ask(n).wait_send()
            for port in ports:
                port.finish_sends()
            for single in singles:
                single.finish_served()
                single.finish_sends()

        return 0

    fresh[...] = jnp.zeros_like(fresh)
    squares[...] = jnp.zeros_like(squares)
    ahead = 4
    table_copy.wait()
    ports[0].finish_delivery()
    ports[1].finish_delivery()
    assemble(locate(0)[2], 0, (0, 1))
    lax.fori_loop(0, 2 * ahead, first_half, 0)
    for single in singles:
        single.finish_delivery()
    ports[2].finish_delivery()
    ports[3].finish_delivery()
    assemble(locate(0)[2], 0, (2, 3))
    lax.fori_loop(0, ahead, functools.partial(ring_item, False), 0)
    assemble(locate(ahead)[2], 0, (0, 1, 2, 3))
    lax.fori_loop(ahead, planes, functools.partial(ring_item, True), 0)
    for half in (1, 0):
        for piece in range(2):
            rows = rows_of(half, piece)
            for way in range(2):
                chain(way, half_ring - 1, half, piece).wait_recv()
            arrived = sums[0, half_ring, rows, :] + sums[1, half_ring, rows, :]
            out[rows, :] = arrived + fresh[0, rows, :]
    for n in range(group):
        count = counts[at_z * group + n].astype(jnp.float32)
        out[COUNTS + n : COUNTS + n + 1, :] = jnp.full((1, LANES), count)
    for step in range(half_ring):
        for way in range(2):
            for half in range(2):
                if step or half == way:
                    for piece in range(2):
                        chain(way, step, half, piece).wait_send()


def pair_products(blocks, domains, counts, coeff, planes):
    pair_dev, depth, slots = coeff.shape
    lines = 2 * RING * CORES
    bf16 = jnp.bfloat16
    tile = (MAIN, LANES)
    scratch = []
    for shape in (
        (RING, ATOMS),
        (RING * RING * CORES * ATOMS,),
        (2, ATOMS // 2),
        (RING, CORES, SHARE),
        (2, CORES, HALF_SHARE),
        (RING, SLOTS),
    ):
        scratch += [pltpu.VMEM(shape + tile, bf16)] * 4
    for shape in (
        (ATOMS,),
        (RING - 1, ATOMS),
        (RING, CORES, PICKS),
        (2, CORES, HALF),
        (RING * CORES * PICKS,),
    ):
        scratch += [pltpu.VMEM(shape + tile, bf16)] * 2
    scratch += [
        pltpu.VMEM((lines, 8, LANES), jnp.int32),
        pltpu.SMEM((lines, 8, LANES), jnp.int32),
        pltpu.VMEM((3, 8, LANES), jnp.int32),
        pltpu.SMEM((3, 8, LANES), jnp.int32),
        pltpu.VMEM((8, LANES), jnp.int32),
        pltpu.VMEM((8, LANES), jnp.int32),
        pltpu.VMEM((ATOMS * MAIN, ATOMS * MAIN), bf16),
        pltpu.VMEM((ATOMS * MAIN, ATOMS * MAIN), bf16),
        pltpu.VMEM((pair_dev, depth, slots), bf16),
        pltpu.VMEM((pair_dev, MAXPNO, DEPTH), bf16),
        pltpu.VMEM((DEPTH, depth), bf16),
        pltpu.VMEM((2, DEPTH, blocks.shape[2]), bf16),
        pltpu.VMEM((pair_dev, MAXPNO, MAXPNO), jnp.float32),
        pltpu.VMEM((2, planes // 2 + 1, PACK, LANES), jnp.float32),
        pltpu.VMEM((2, PACK, LANES), jnp.float32),
        pltpu.VMEM((MAXPNO, slots), bf16),
        pltpu.VMEM((2, SQUARE_ROWS, 2 * LANES), jnp.float32),
        pltpu.VMEM(blocks.shape, bf16),
        pltpu.SemaphoreType.DMA((4, 27)),
        pltpu.SemaphoreType.DMA((4, 27)),
        pltpu.SemaphoreType.DMA((2, 16)),
        pltpu.SemaphoreType.DMA((2, 16)),
        pltpu.SemaphoreType.DMA((lines,)),
        pltpu.SemaphoreType.DMA((lines,)),
        pltpu.SemaphoreType.DMA((8,)),
        pltpu.SemaphoreType.DMA((2 * planes, 2)),
        pltpu.SemaphoreType.DMA((2 * planes, 2)),
    ]
    return pl.pallas_call(
        main_kernel,
        out_shape=pltpu.VMEM((PACK, LANES), jnp.float32),
        in_specs=[
            pl.BlockSpec(memory_space=pl.ANY),
            pl.BlockSpec(memory_space=pltpu.SMEM),
            pl.BlockSpec(memory_space=pltpu.SMEM),
            pl.BlockSpec(memory_space=pl.ANY),
        ],
        out_specs=pl.BlockSpec(memory_space=pltpu.VMEM),
        scratch_shapes=scratch,
        compiler_params=params(60, collective_id=0, has_side_effects=True),
    )(blocks, domains, counts, coeff)


def tail_kernel(packed, amp, energy_row, energy_col, out, wide):
    slots = amp.shape[1]
    step = pl.program_id(0)
    full_row = lax.broadcasted_iota(jnp.int32, (slots, slots), 0)
    full_col = lax.broadcasted_iota(jnp.int32, (slots, slots), 1)
    lane = lax.broadcasted_iota(jnp.int32, (MAXPNO, LANES), 1)
    fold_lane = lax.broadcasted_iota(jnp.int32, (FOLD_ROWS, LANES), 1)
    wide[MAXPNO:, :] = jnp.zeros((slots - MAXPNO, slots), jnp.float32)

    def shared_at(begin, end):
        if end <= TOP:
            return packed[MAXPNO + begin : MAXPNO + end, :]
        return packed[HALF_PACK + MAXPNO + begin - TOP : HALF_PACK + MAXPNO + end - TOP, :]

    @pl.when(step == 0)
    def _():
        wide[:MAXPNO, :LANES] = packed[:MAXPNO, :]
        for begin, end in ((0, TOP), (TOP, MAXPNO)):
            wide[begin:end, LANES:] = jnp.where(lane[begin:end] < REST, shared_at(begin, end), 0.0)

    @pl.when(step == 1)
    def _():
        wide[:MAXPNO, :LANES] = packed[HALF_PACK : HALF_PACK + MAXPNO, :]
        for begin, end in ((0, TOP), (TOP, MAXPNO)):
            turned = pltpu.roll(shared_at(begin, end), SPARE, 1)
            wide[begin:end, LANES:] = jnp.where(lane[begin:end] < SPARE, turned, 0.0)
        folded = packed[FOLD_AT:DIAG_AT, :]
        for n in range(SQUARE_ROWS // FOLD_ROWS):
            begin, end = n * FOLD_ROWS, min((n + 1) * FOLD_ROWS, MAXPNO)
            moved = pltpu.roll(folded, (SPARE - n * LEFT) % LANES, 1)
            left = (fold_lane >= SPARE) & (fold_lane < REST)
            held = wide[begin:end, LANES:]
            wide[begin:end, LANES:] = jnp.where(left[: end - begin], moved[: end - begin], held)

    square = wide[...]
    at = DIAG_AT + 2 * step
    diagonal = jnp.concatenate([packed[pl.ds(at, 1), :], packed[pl.ds(at + 1, 1), :]], axis=1)
    on_diagonal = full_row == full_col
    for n in range(2):
        count = packed[pl.ds(COUNTS + 2 * step + n, 1), :][:, :1].astype(jnp.int32)
        if n == 0:
            held = jnp.where(full_row >= full_col, square, 0.0)
        else:
            held = jnp.where(full_row < full_col, square, jnp.where(on_diagonal, diagonal, 0.0))
        products = held + jnp.where(on_diagonal, 0.0, held.T)
        valid = (full_row < count) & (full_col < count)
        products = jnp.where(valid, products / NAUX, 0.0)
        amps = amp[n]
        contract = (((1,), (1,)), ((), ()))
        high = products.astype(jnp.bfloat16)
        left = products - high.astype(jnp.float32)
        mid = left.astype(jnp.bfloat16)
        low = (left - mid.astype(jnp.float32)).astype(jnp.bfloat16)
        coupled = lax.dot_general(low, amps, contract, preferred_element_type=jnp.float32)
        coupled += lax.dot_general(mid, amps, contract, preferred_element_type=jnp.float32)
        coupled += lax.dot_general(high, amps, contract, preferred_element_type=jnp.float32)
        energies = energy_col[n] + energy_row[pl.ds(2 * step + n, 1), :]
        result = products + coupled + energies * amps.astype(jnp.float32)
        out[n] = jnp.where(valid, result, 0.0)


def tail(packed, amp, energy):
    subs, slots, _ = amp.shape
    return pl.pallas_call(
        tail_kernel,
        out_shape=jax.ShapeDtypeStruct((subs, slots, slots), jnp.float32),
        grid=(subs // 2,),
        in_specs=[
            pl.BlockSpec((PACK, LANES), lambda i: (0, 0)),
            pl.BlockSpec((2, slots, slots), lambda i: (i, 0, 0)),
            pl.BlockSpec((subs, slots), lambda i: (0, 0)),
            pl.BlockSpec((2, slots, 1), lambda i: (i, 0, 0)),
        ],
        out_specs=pl.BlockSpec((2, slots, slots), lambda i: (i, 0, 0)),
        scratch_shapes=[pltpu.VMEM((slots, slots), jnp.float32)],
        compiler_params=params(32),
    )(packed, amp, energy, energy[:, :, None])


def on_device(atom_blocks, domains, pno_counts, pno_coeffs, amplitudes, pno_energies):
    planes = lax.axis_size("ri")
    mine = pair_products(atom_blocks.transpose(1, 0, 2), domains.T, pno_counts, pno_coeffs, planes)
    return tail(mine, amplitudes, pno_energies)


def solution(mesh):
    placed = (
        P("pairs", None, "ri"),
        P("pairs", None),
        P("pairs"),
        P("pairs", None, None),
        P(("pairs", "ri"), None, None),
        P(("pairs", "ri"), None),
    )
    return jax.shard_map(
        on_device,
        mesh=mesh,
        in_specs=placed,
        out_specs=P(("pairs", "ri"), None, None),
        check_vma=False,
    )
```

```python
import functools

import jax
import jax.numpy as jnp
from jax import lax
from jax.experimental import pallas as pl
from jax.experimental.pallas import tpu as pltpu
from jax.sharding import PartitionSpec as P

NAUX = 14336
CAP = 3
MAXPNO = 200
MAIN = 16
REM = 4
SPLIT = 128
REST = MAXPNO - SPLIT
LANES = 128
MIB = 1 << 20
RING = 4
CORES = 2
ATOMS = 16
DOM = 12
BAND = MAIN + REM
PICKS = RING * CAP
HALF = PICKS // 2
DEPTH = 256
SPARE = LANES - REST
LEFT = REST - SPARE
FOLD_ROWS = 32
HALF_PACK = 320
PACK = 2 * HALF_PACK
TOP = HALF_PACK - MAXPNO
FOLD_AT = PACK - FOLD_ROWS - 8
DIAG_AT = PACK - 8
COUNTS = PACK - 4
SQUARE_ROWS = 224
SLOTS = 48
SHARE = SLOTS // CORES
HALF_SHARE = SHARE // 2
ROW_LINES = RING * CORES
MAINS = ((0, 1, 2), (3, 4, 5), (6, 7, 8), (10, 11, 12))
RESTS = ((0, 1, 2), (3, 4, 5), (6, 7, 8, 9), (10, 11, 12, 13))
SINGLES = (9, 13)
MESH = pl.DeviceIdType.MESH


def params(mib, **kw):
    return pltpu.CompilerParams(vmem_limit_bytes=mib * MIB, **kw)


class Ports:
    def __init__(self, chunk, gather_to, deliver_to, wire, ring, send, relay, recv, out_sems, in_sems, core):
        self.gather_to, self.deliver_to, self.core = gather_to, deliver_to, core
        self.wire, self.ring, self.send, self.relay, self.recv = wire, ring, send, relay, recv
        self.out_sems, self.in_sems, self.chunk = out_sems, in_sems, chunk

    def copy(self, src, dst, out_at, in_at, to):
        return pltpu.make_async_remote_copy(
            src_ref=src,
            dst_ref=dst,
            send_sem=self.out_sems.at[self.chunk, out_at],
            recv_sem=self.in_sems.at[self.chunk, in_at],
            device_id={"pairs": to},
            device_id_type=MESH,
        )

    def gather_first(self):
        up = self.copy(self.wire, self.ring.at[2], 0, 1, self.gather_to(1, self.core))
        down = self.copy(self.wire, self.ring.at[0], 1, 0, self.gather_to(3, self.core))
        return up, down

    def gather_second(self):
        half = ATOMS // 2
        low, high = pl.ds(0, half), pl.ds(half, half)
        up = self.copy(self.ring.at[2, low], self.ring.at[1, low], 2, 2, self.gather_to(1, self.core))
        down = self.copy(self.ring.at[0, high], self.ring.at[1, high], 3, 3, self.gather_to(3, self.core))
        return up, down

    def place(self, rel, core):
        return (rel * CORES + core) * PICKS

    def far(self):
        up = self.copy(self.send.at[2, :, pl.ds(0, HALF)], self.relay.at[0], 4, 4, self.deliver_to(1, self.core))
        down = self.copy(self.send.at[2, :, pl.ds(HALF, HALF)], self.relay.at[1], 5, 5, self.deliver_to(3, self.core))
        return up, down

    def near(self):
        copies = []
        for n, step in enumerate((1, 3)):
            for core in range(CORES):
                dst = self.recv.at[pl.ds(self.place(RING - step, self.core), PICKS)]
                at = 6 + 2 * n
                copies.append(self.copy(self.send.at[step, core], dst, at + core, at + self.core, self.deliver_to(step, core)))
        other = 1 - self.core
        dst = self.recv.at[pl.ds(self.place(0, self.core), PICKS)]
        copies.append(self.copy(self.send.at[0, other], dst, 10, 10, self.deliver_to(0, other)))
        return copies

    def own(self):
        return pltpu.make_async_copy(
            self.send.at[0, self.core],
            self.recv.at[pl.ds(self.place(0, self.core), PICKS)],
            self.in_sems.at[self.chunk, 11],
        )

    def onward(self):
        copies = []
        for way, step in enumerate((1, 3)):
            for core in range(CORES):
                dst = self.recv.at[pl.ds(self.place(2, self.core) + way * HALF, HALF)]
                at = 12 + 2 * way
                copies.append(self.copy(self.relay.at[way, core], dst, at + core, at + self.core, self.deliver_to(step, core)))
        return copies

    def start_gather(self):
        for copy in self.gather_first():
            copy.start()

    def forward_gather(self):
        up, down = self.gather_second()
        first_up, first_down = self.gather_first()
        first_up.wait_recv()
        up.start()
        first_down.wait_recv()
        down.start()

    def finish_gather(self):
        for copy in self.gather_second():
            copy.wait_recv()

    def start_far(self):
        for copy in self.far():
            copy.start()

    def start_near(self):
        for copy in self.near():
            copy.start()
        self.own().start()

    def forward_delivery(self):
        far, onward = self.far(), self.onward()
        for way in range(2):
            far[way].wait_recv()
            for copy in onward[2 * way : 2 * way + 2]:
                copy.start()

    def finish_delivery(self):
        for n, step in enumerate((1, 3)):
            for core in range(CORES):
                dst = self.recv.at[pl.ds(self.place(step, core), PICKS)]
                at = 6 + 2 * (1 - n)
                self.copy(dst, dst, at + core, at + core, self.deliver_to(1, self.core)).wait_recv()
        other = 1 - self.core
        dst = self.recv.at[pl.ds(self.place(0, other), PICKS)]
        self.copy(dst, dst, 10, 10, self.deliver_to(1, self.core)).wait_recv()
        self.own().wait()
        for way in range(2):
            for core in range(CORES):
                dst = self.recv.at[pl.ds(self.place(2, core) + way * HALF, HALF)]
                at = 12 + 2 * way
                self.copy(dst, dst, at + core, at + core, self.deliver_to(1, self.core)).wait_recv()

    def finish_served(self):
        for copy in self.far() + tuple(self.near()):
            copy.wait_send()

    def finish_sends(self):
        for copy in self.gather_first() + self.gather_second() + tuple(self.onward()):
            copy.wait_send()


class Relay:
    def __init__(self, chunk, first_to, other_to, u, v, core, bufs, out_sems, in_sems):
        self.chunk, self.first_to, self.other_to = chunk, first_to, other_to
        self.u, self.v, self.core = u, v, core
        self.wire, self.table, self.passing, self.send, self.relay, self.recv = bufs
        self.out_sems, self.in_sems = out_sems, in_sems

    def copy(self, src, dst, out_at, in_at, to):
        return pltpu.make_async_remote_copy(
            src_ref=src,
            dst_ref=dst,
            send_sem=self.out_sems.at[self.chunk, out_at],
            recv_sem=self.in_sems.at[self.chunk, in_at],
            device_id={"pairs": to},
            device_id_type=MESH,
        )

    def arrival(self, dst, at):
        return self.copy(dst, dst, at, at, self.first_to(1, self.core))

    def near_u(self, step):
        return lax.rem(self.u + step, RING)

    def near_v(self, step):
        return lax.rem(self.v + step, RING)

    def atoms(self, step, at=0, count=ATOMS):
        base = ((self.v * CORES + self.core) * RING + self.near_u(step)) * ATOMS
        return self.table.at[pl.ds(base + at, count)]

    def block(self, step, core, at=0, count=RING * ATOMS):
        return self.table.at[pl.ds((self.near_v(step) * CORES + core) * RING * ATOMS + at, count)]

    def spread_sends(self):
        half = ATOMS // 2
        far = self.near_u(2)
        up, down = self.first_to(1, self.core), self.first_to(3, self.core)
        return [
            self.copy(self.wire.at[far, pl.ds(0, half)], self.passing.at[0], 2, 2, up),
            self.copy(self.wire.at[far, pl.ds(half, half)], self.passing.at[1], 3, 3, down),
            self.copy(self.wire.at[self.near_u(1)], self.atoms(0), 0, 1, up),
            self.copy(self.wire.at[self.near_u(3)], self.atoms(0), 1, 0, down),
        ]

    def spread_own(self):
        return pltpu.make_async_copy(self.wire.at[self.u], self.atoms(0), self.in_sems.at[self.chunk, 25])

    def spread_onward(self):
        half = ATOMS // 2
        return [
            self.copy(self.passing.at[0], self.atoms(3, 0, half), 4, 4, self.first_to(1, self.core)),
            self.copy(self.passing.at[1], self.atoms(1, half, half), 5, 5, self.first_to(3, self.core)),
        ]

    def start_spread(self):
        for copy in self.spread_sends():
            copy.start()
        self.spread_own().start()

    def forward_spread(self):
        for way, copy in enumerate(self.spread_onward()):
            self.arrival(self.passing.at[way], 2 + way).wait_recv()
            copy.start()

    def finish_spread(self):
        half = ATOMS // 2
        self.spread_own().wait()
        self.arrival(self.atoms(1), 0).wait_recv()
        self.arrival(self.atoms(3), 1).wait_recv()
        self.arrival(self.atoms(2, 0, half), 4).wait_recv()
        self.arrival(self.atoms(2, half, half), 5).wait_recv()

    def gather_first(self):
        own = self.block(0, self.core)
        return [
            self.copy(own, own, 6, 7, self.other_to(1, self.core)),
            self.copy(own, own, 7, 6, self.other_to(3, self.core)),
        ]

    def gather_second(self):
        half = RING * ATOMS // 2
        low, high = self.block(3, self.core, 0, half), self.block(1, self.core, half, half)
        return [
            self.copy(low, low, 8, 8, self.other_to(1, self.core)),
            self.copy(high, high, 9, 9, self.other_to(3, self.core)),
        ]

    def share(self, step):
        mine = self.block(step, self.core)
        return self.copy(mine, mine, 10 + step, 10 + step, self.first_to(0, 1 - self.core))

    def start_gather(self):
        for copy in self.gather_first():
            copy.start()
        self.share(0).start()

    def forward_gather(self):
        low, high = self.gather_second()
        self.arrival(self.block(3, self.core), 7).wait_recv()
        low.start()
        self.share(3).start()
        self.arrival(self.block(1, self.core), 6).wait_recv()
        high.start()
        self.share(1).start()

    def finish_gather(self):
        half = RING * ATOMS // 2
        self.arrival(self.block(2, self.core, 0, half), 8).wait_recv()
        self.arrival(self.block(2, self.core, half, half), 9).wait_recv()
        self.share(2).start()

    def finish_share(self):
        for step in range(RING):
            self.arrival(self.block(step, 1 - self.core), 10 + step).wait_recv()

    def place(self, step, core, at=0, count=SHARE):
        return self.recv.at[self.near_u(step), pl.ds(core * SHARE + at, count)]

    def far(self):
        return [
            self.copy(self.send.at[2, :, pl.ds(0, HALF_SHARE)], self.relay.at[0], 19, 19, self.first_to(1, self.core)),
            self.copy(
                self.send.at[2, :, pl.ds(HALF_SHARE, HALF_SHARE)], self.relay.at[1], 20, 20, self.first_to(3, self.core)
            ),
        ]

    def near(self):
        copies = []
        dst = self.place(0, self.core)
        for n, step in enumerate((1, 3)):
            for core in range(CORES):
                at = 14 + 2 * n
                copies.append(self.copy(self.send.at[step, core], dst, at + core, at + self.core, self.first_to(step, core)))
        other = 1 - self.core
        copies.append(self.copy(self.send.at[0, other], dst, 18, 18, self.first_to(0, other)))
        return copies

    def own(self):
        return pltpu.make_async_copy(
            self.send.at[0, self.core], self.place(0, self.core), self.in_sems.at[self.chunk, 26]
        )

    def onward(self):
        copies = []
        for way, step in enumerate((1, 3)):
            dst = self.place(RING - step, self.core, way * HALF_SHARE, HALF_SHARE)
            for core in range(CORES):
                at = 21 + 2 * way
                copies.append(self.copy(self.relay.at[way, core], dst, at + core, at + self.core, self.first_to(step, core)))
        return copies

    def start_far(self):
        for copy in self.far():
            copy.start()

    def start_near(self):
        for copy in self.near():
            copy.start()
        self.own().start()

    def forward_delivery(self):
        onward = self.onward()
        for way in range(2):
            self.arrival(self.relay.at[way], 19 + way).wait_recv()
            for copy in onward[2 * way : 2 * way + 2]:
                copy.start()

    def finish_delivery(self):
        for core in range(CORES):
            self.arrival(self.place(3, core), 14 + core).wait_recv()
            self.arrival(self.place(1, core), 16 + core).wait_recv()
            for way in range(2):
                at = 21 + 2 * way + core
                self.arrival(self.place(2, core, way * HALF_SHARE, HALF_SHARE), at).wait_recv()
        self.arrival(self.place(0, 1 - self.core), 18).wait_recv()
        self.own().wait()

    def finish_sends(self):
        copies = self.spread_sends() + self.spread_onward() + self.gather_first() + self.gather_second()
        copies += [self.share(step) for step in range(RING)] + self.far() + self.near() + self.onward()
        for copy in copies:
            copy.wait_send()


def main_kernel(
    blocks_hbm, domains, counts, coeff_hbm, out, *scratch
):
    relay_bufs = [scratch[4 * n : 4 * n + 4] for n in range(6)]
    single_bufs = [scratch[24 + 2 * n : 26 + 2 * n] for n in range(5)]
    wires, recvs = relay_bufs[0], relay_bufs[5]
    single_wires, single_recvs = single_bufs[0], single_bufs[4]
    asked, asked_smem, tables, places, request, ids, perm_main, perm_rest = scratch[34:42]
    coeff, coeff_t, perm, blk, total, sums, fresh, same, squares, blocks = scratch[42:52]
    out_sems, in_sems, single_out, single_in, ask_out, ask_in, local_sems, sum_out, sum_in = scratch[52:61]
    me = lax.axis_index("pairs")
    at_z = lax.axis_index("ri")
    planes = 2 * (sums.shape[1] - 1)
    above, below = lax.rem(at_z + 1, planes), lax.rem(at_z + planes - 1, planes)
    core = lax.rem(me, CORES)
    chip = lax.div(me, CORES)
    at_x = lax.rem(chip, RING)
    at_y = lax.div(chip, RING)

    def along_x(step, to_core):
        return (at_y * RING + lax.rem(at_x + step, RING)) * CORES + to_core

    def along_y(step, to_core):
        return (lax.rem(at_y + step, RING) * RING + at_x) * CORES + to_core

    peers = []
    for to_core in range(2):
        for step in range(1, RING):
            peers.append((along_y(step, to_core), step * CORES + to_core, (RING - step) * CORES + core))
            peers.append(
                (along_x(step, to_core), (RING + step) * CORES + to_core, (2 * RING - step) * CORES + core)
            )
    peers.append((along_x(0, 1 - core), 1 - core, core))

    barrier = pltpu.get_barrier_semaphore()
    for peer, _, _ in peers:
        pl.semaphore_signal(barrier, inc=1, device_id={"pairs": peer}, device_id_type=MESH)
    for plane in (above, below):
        pl.semaphore_signal(barrier, inc=1, device_id={"ri": plane}, device_id_type=MESH)

    def ask(n):
        peer, _, there = peers[n]
        return pltpu.make_async_remote_copy(
            src_ref=request,
            dst_ref=asked.at[there],
            send_sem=ask_out.at[n],
            recv_sem=ask_in.at[there],
            device_id={"pairs": peer},
            device_id_type=MESH,
        )

    ports = []
    for chunk in range(4):
        by_x = chunk % 2 == 0
        first_to, other_to = (along_x, along_y) if by_x else (along_y, along_x)
        u, v = (at_x, at_y) if by_x else (at_y, at_x)
        bufs = [group_bufs[chunk] for group_bufs in relay_bufs]
        ports.append(Relay(chunk, first_to, other_to, u, v, core, bufs, out_sems, in_sems))
    singles = []
    for n in range(2):
        gather_to, deliver_to = (along_x, along_y) if n == 0 else (along_y, along_x)
        bufs = [group_bufs[n] for group_bufs in single_bufs]
        singles.append(Ports(n, gather_to, deliver_to, *bufs, single_out, single_in, core))

    fetches = []
    for chunk in range(4):
        tiles = RESTS[chunk]
        cols = pl.ds(tiles[0] * LANES, len(tiles) * LANES)
        fetches.append(
            pltpu.make_async_copy(blocks_hbm.at[:, :, cols], blocks.at[:, :, cols], local_sems.at[4 + chunk])
        )
        fetches[chunk].start()
    fetch = pltpu.make_async_copy(coeff_hbm, coeff, local_sems.at[0])
    fetch.start()

    square = (ATOMS * MAIN, ATOMS * MAIN)
    out_at = lax.broadcasted_iota(jnp.int32, square, 0)
    from_at = lax.broadcasted_iota(jnp.int32, square, 1)
    band_at, atom_at = out_at & (MAIN - 1), lax.shift_right_logical(out_at, 4)
    perm_main[...] = jnp.where(band_at * ATOMS + atom_at == from_at, 1.0, 0.0).astype(jnp.bfloat16)
    rest_at = lax.shift_right_logical(band_at, 2) * (REM * ATOMS) + (band_at & (REM - 1)) * ATOMS + atom_at
    perm_rest[...] = jnp.where(rest_at == from_at, 1.0, 0.0).astype(jnp.bfloat16)

    def main_rows(tiles):
        flat = blocks[:MAIN, :, tiles[0] * LANES : (tiles[-1] + 1) * LANES]
        flat = flat.reshape(MAIN * ATOMS, len(tiles) * LANES)
        return jnp.dot(perm_main[...], flat, preferred_element_type=jnp.float32).astype(jnp.bfloat16)

    def form(chunk):
        fetches[chunk].wait()
        main = main_rows(MAINS[chunk])
        for n in range(len(MAINS[chunk])):
            wires[chunk][n] = main[:, n * LANES : (n + 1) * LANES].reshape(ATOMS, MAIN, LANES)
        parts = [blocks[MAIN:, :, t * LANES : (t + 1) * LANES].reshape(REM * ATOMS, LANES) for t in RESTS[chunk]]
        stacked = jnp.concatenate(parts, axis=0)
        depth = stacked.shape[0]
        late = jnp.dot(perm_rest[:, :depth], stacked, preferred_element_type=jnp.float32).astype(jnp.bfloat16)
        wires[chunk][RING - 1] = late.reshape(ATOMS, MAIN, LANES)

    form(0)
    pl.semaphore_wait(barrier, len(peers) + 2)
    ports[0].start_spread()
    for chunk in range(1, 4):
        form(chunk)
        ports[chunk].start_spread()
    for n in range(2):
        single_wires[n][...] = main_rows(SINGLES[n : n + 1]).reshape(ATOMS, MAIN, LANES)
    for chunk in (0, 1):
        ports[chunk].forward_spread()
    for chunk in (0, 1):
        ports[chunk].finish_spread()
        ports[chunk].start_gather()

    for chunk in (2, 3):
        ports[chunk].forward_spread()

    def parts_of(atom):
        owner = lax.shift_right_logical(atom, 4)
        chip = lax.shift_right_logical(owner, 1)
        return owner, owner & (CORES - 1), chip & (RING - 1), lax.shift_right_logical(chip, 2), atom & (ATOMS - 1)

    map_shape = (8, LANES)
    map_row = lax.broadcasted_iota(jnp.int32, map_shape, 0)
    map_lane = lax.broadcasted_iota(jnp.int32, map_shape, 1)
    atom_map = map_row * LANES + map_lane
    pairs = domains.shape[1]

    def mark(pair, seen):
        for k in range(DOM):
            seen = jnp.where(atom_map == domains[k, pair], 1, seen)
        return seen

    named = lax.fori_loop(0, pairs, mark, jnp.zeros(map_shape, jnp.int32))
    owner, owner_core, owner_x, owner_y, local = parts_of(atom_map)
    rank = named
    for shift in (1, 2, 4, 8):
        rank = rank + jnp.where(local >= shift, pltpu.roll(rank, shift, 1), 0)
    order = named
    for shift in (1, 2, 4, 8, 16, 32, 64):
        order = order + jnp.where(map_lane >= shift, pltpu.roll(order, shift, 1), 0)
    counted = order
    map_rows = ATOMS * RING * RING * CORES // LANES
    for n in range(map_rows - 1):
        order = order + jnp.where(map_row > n, counted[n : n + 1, LANES - 1 :], 0)
    rel_x = (owner_x + RING - at_x) & (RING - 1)
    rel_y = (owner_y + RING - at_y) & (RING - 1)
    tables[0] = order - 1
    tables[1] = ((rel_y * CORES + owner_core) * RING + rel_x) * CAP + rank - 1
    tables[2] = ((rel_x * CORES + owner_core) * RING + rel_y) * CAP + rank - 1
    table_copy = pltpu.make_async_copy(tables, places, local_sems.at[3])
    table_copy.start()

    ids[:map_rows, :] = jnp.where(named > 0, order, 0)[:map_rows]
    ids[map_rows:, :] = jnp.where(named > 0, rank, 0)[:map_rows]
    upright = ids[...].T
    list_shape = (LANES, LANES)
    list_row = lax.broadcasted_iota(jnp.int32, list_shape, 0)
    list_lane = lax.broadcasted_iota(jnp.int32, list_shape, 1)
    rows = [jnp.zeros((1, LANES), jnp.int32) for _ in range(CAP + 2)]
    for n in range(map_rows):
        owner, owner_core, owner_x, owner_y, local = parts_of(list_row + n * LANES)
        own_lane = jnp.where(owner == list_lane, local, 0)
        order_at = jnp.broadcast_to(upright[:, n : n + 1], list_shape)
        rank_at = jnp.broadcast_to(upright[:, map_rows + n : map_rows + n + 1], list_shape)
        for j in range(CAP):
            rows[j] += jnp.sum(jnp.where(rank_at == j + 1, own_lane, 0), axis=0, keepdims=True)
        for j, (u, v) in enumerate(((owner_x, owner_y), (owner_y, owner_x))):
            held_at = ((v * CORES + owner_core) * RING + u) * ATOMS + local
            rows[CAP + j] += jnp.sum(jnp.where(order_at == list_lane + 1, held_at, 0), axis=0, keepdims=True)
    for n in range(CAP + 2):
        request[n : n + 1, :] = rows[n]
    request[CAP + 2 :, :] = jnp.zeros((6 - CAP, LANES), jnp.int32)

    for n in range(len(peers)):
        ask(n).start()
    own_ask = pltpu.make_async_copy(request, asked.at[core], local_sems.at[1])
    own_ask.start()
    for chunk in (2, 3):
        ports[chunk].finish_spread()

    shape = (DEPTH, DOM * BAND)
    row = lax.broadcasted_iota(jnp.int32, shape, 0)
    col = lax.broadcasted_iota(jnp.int32, shape, 1)
    split = DOM * MAIN
    late = row - split
    source = jnp.where(
        row < split,
        lax.shift_right_logical(row, 4) * BAND + (row & (MAIN - 1)),
        lax.shift_right_arithmetic(late, 2) * BAND + MAIN + (late & (REM - 1)),
    )
    perm[...] = jnp.where((source == col) & (row < DOM * BAND), 1.0, 0.0).astype(jnp.bfloat16)
    same[...] = jnp.where(
        lax.broadcasted_iota(jnp.int32, same.shape, 0) == lax.broadcasted_iota(jnp.int32, same.shape, 1), 1.0, 0.0
    ).astype(jnp.bfloat16)
    for n in range(2):
        blk[n, DOM * BAND :, :] = jnp.zeros((DEPTH - DOM * BAND, blk.shape[2]), jnp.bfloat16)
    fetch.wait()

    group = coeff.shape[0] // planes
    half_ring = planes // 2

    def locate(item):
        step = (item + 1) // 2
        way = jnp.where(item == 0, 0, (item + 1) % 2)
        away = jnp.where(way == 0, half_ring - step, half_ring + step)
        return way, step, lax.rem(at_z + away, planes) * group

    def prepare(begin, end):
        def turn(item, _):
            first = locate(item)[2]
            ordered = [
                jnp.dot(perm[...], coeff[first + n], preferred_element_type=jnp.float32).astype(jnp.bfloat16)
                for n in range(group)
            ]
            for n in range(group):
                turned = lax.dot_general(
                    same[...], ordered[n], (((1,), (1,)), ((), ())), preferred_element_type=jnp.float32
                )
                coeff_t[first + n] = turned.astype(jnp.bfloat16)
            return 0

        lax.fori_loop(begin, end, turn, 0)

    prepare(0, 1)
    for chunk in (2, 3):
        ports[chunk].start_gather()
    for chunk in (0, 1):
        ports[chunk].forward_gather()

    for single in singles:
        single.start_gather()
    prepare(1, 3)

    own_ask.wait()
    for n in range(len(peers)):
        _, here, _ = peers[n]
        pltpu.make_async_remote_copy(
            src_ref=request,
            dst_ref=asked.at[here],
            send_sem=ask_out.at[n],
            recv_sem=ask_in.at[here],
            device_id={"pairs": peers[n][0]},
            device_id_type=MESH,
        ).wait_recv()
    to_smem = pltpu.make_async_copy(asked, asked_smem, local_sems.at[2])
    to_smem.start()
    to_smem.wait()

    def line_of(dest, on_row):
        return jnp.where(dest < CORES, dest, dest + ROW_LINES) if on_row else dest

    def pick_single(n):
        port = singles[n]
        owner_of = along_x if n == 0 else along_y

        def serve(dest, _):
            line = line_of(dest, n == 1)
            step, to_core = dest // CORES, dest % CORES
            for r in range(RING):
                for j in range(CAP):
                    atom = asked_smem[line, j, owner_of(r, core)]
                    found = port.wire[atom] if r == 0 else port.ring[r - 1, atom]
                    port.send[step, to_core, r * CAP + j] = found
            return 0

        lax.fori_loop(2 * CORES, 3 * CORES, serve, 0)
        port.start_far()

        def serve_near(dest, _):
            return serve(jnp.where(dest < 2 * CORES, dest, dest + CORES), 0)

        lax.fori_loop(0, 3 * CORES, serve_near, 0)
        port.start_near()

    def pick(chunk):
        port = ports[chunk]

        def serve(dest, _):
            line = line_of(dest, chunk % 2 == 0)
            step, to_core = dest // CORES, dest % CORES
            for n in range(SHARE):
                port.send[step, to_core, n] = port.table[asked_smem[line, CAP + chunk % 2, core * SHARE + n]]
            return 0

        lax.fori_loop(2 * CORES, 3 * CORES, serve, 0)
        port.start_far()

        def serve_near(dest, _):
            return serve(jnp.where(dest < 2 * CORES, dest, dest + CORES), 0)

        lax.fori_loop(0, 3 * CORES, serve_near, 0)
        port.start_near()

    for chunk in (0, 1):
        ports[chunk].finish_gather()
    for chunk in (0, 1):
        ports[chunk].finish_share()
        pick(chunk)
    for chunk in (2, 3):
        ports[chunk].forward_gather()
    for single in singles:
        single.forward_gather()
    prepare(3, 5)
    for chunk in (0, 1):
        ports[chunk].forward_delivery()
    prepare(5, 6)
    for chunk in (2, 3):
        ports[chunk].finish_gather()
    for n in range(2):
        singles[n].finish_gather()
        pick_single(n)
    for chunk in (2, 3):
        ports[chunk].finish_share()
        pick(chunk)
    prepare(6, planes - 1)
    for single in singles:
        single.forward_delivery()
    for chunk in (2, 3):
        ports[chunk].forward_delivery()

    pack_row = lax.broadcasted_iota(jnp.int32, (MAXPNO, MAXPNO), 0)
    pack_col = lax.broadcasted_iota(jnp.int32, (MAXPNO, MAXPNO), 1)
    pack_lane = lax.broadcasted_iota(jnp.int32, (MAXPNO, LANES), 1)
    fold_lane = lax.broadcasted_iota(jnp.int32, (FOLD_ROWS, LANES), 1)

    def assemble(pair, slot, chunks):
        base = MAIN * DOM
        begin = 0
        upper = lax.broadcasted_iota(jnp.int32, (8, LANES), 0) < REM

        names = [domains[k, pair] for k in range(DOM)]

        def named_at(table):
            return [places[table, lax.shift_right_logical(a, 7), a & (LANES - 1)] for a in names]

        at = named_at(0)
        for chunk in chunks:
            tiles = len(RESTS[chunk])
            for n in range(RING - 1):
                span = slice(begin + n * LANES, begin + (n + 1) * LANES)
                for k in range(DOM):
                    blk[slot, MAIN * k : MAIN * (k + 1), span] = recvs[chunk][n, at[k]]
            if tiles == RING:
                span = slice(begin + (RING - 1) * LANES, begin + RING * LANES)
                single_at = named_at(1 + chunk % 2)
                for k in range(DOM):
                    blk[slot, MAIN * k : MAIN * (k + 1), span] = single_recvs[chunk % 2][single_at[k]]
            for k in range(0, DOM, 4):
                rest = [recvs[chunk][RING - 1, at[k + n]].astype(jnp.float32) for n in range(4)]
                for half in range((tiles + 1) // 2):
                    parts = [r[8 * half : 8 * half + 8] for r in rest]
                    shifted = [pltpu.roll(part, REM, 0) for part in parts]
                    for q in range(2 * half, min(2 * half + 2, tiles)):
                        first, second = (parts, shifted) if q % 2 == 0 else (shifted, parts)
                        low = jnp.where(upper, first[0], second[1])
                        high = jnp.where(upper, first[2], second[3])
                        both = jnp.concatenate([low, high], axis=0).astype(jnp.bfloat16)
                        tile = slice(begin + q * LANES, begin + (q + 1) * LANES)
                        blk[slot, base + REM * k : base + REM * (k + 4), tile] = both
            begin += tiles * LANES
        return begin

    def multiply(pair, slot, cols):
        weights = coeff_t[pair]
        vecs = []
        for at in range(0, cols, 256):
            vec = jnp.dot(weights, blk[slot, :, at : at + 256], preferred_element_type=jnp.float32)
            vecs.append(vec.astype(jnp.bfloat16))
        vecs = jnp.concatenate(vecs, axis=1)
        return lax.dot_general(vecs, vecs, (((1,), (1,)), ((), ())), preferred_element_type=jnp.float32)

    early_cols = LANES * (len(RESTS[0]) + len(RESTS[1]))
    late_cols = LANES * (len(RESTS[2]) + len(RESTS[3]))
    part = HALF_PACK // 2

    def rows_of(half, piece):
        return pl.ds(pl.multiple_of(half * HALF_PACK + piece * part, 8), part)

    def chain(way, step, half, piece):
        rows = rows_of(half, piece)
        return pltpu.make_async_remote_copy(
            src_ref=sums.at[way, step, rows],
            dst_ref=sums.at[way, step + 1, rows],
            send_sem=sum_out.at[(way * half_ring + step) * 2 + half, piece],
            recv_sem=sum_in.at[(way * half_ring + step) * 2 + half, piece],
            device_id={"ri": jnp.where(way == 0, above, below)},
            device_id_type=MESH,
        )

    def first_half(step, _):
        pair = locate(step // 2)[2] + 2 * (step % 2)
        following = locate((step + 1) // 2)[2] + 2 * ((step + 1) % 2)
        assemble(pair + 1, 1, (0, 1))
        total[pair] = multiply(pair, 0, early_cols)
        assemble(following, 0, (0, 1))
        total[pair + 1] = multiply(pair + 1, 1, early_cols)
        return 0

    def block_products(slot, first, following, whole):
        chunks = (0, 1, 2, 3) if whole else (2, 3)
        cols = early_cols + late_cols if whole else late_cols

        def one(duo, _):
            pair = first + 2 * duo
            assemble(pair + 1, 1, chunks)
            here = multiply(pair, 0, cols)
            assemble(jnp.where(duo == 0, pair + 2, following), 0, chunks)
            there = multiply(pair + 1, 1, cols)
            if not whole:
                here += total[pair]
                there += total[pair + 1]
            squares[duo, :MAXPNO, :MAXPNO] = jnp.where(pack_row >= pack_col, here, there)
            diagonal = jnp.sum(jnp.where(pack_row == pack_col, there, 0.0), axis=0, keepdims=True)
            at = DIAG_AT + 2 * duo
            fresh[slot, pl.ds(at, 1), :] = diagonal[:, :LANES]
            fresh[slot, pl.ds(at + 1, 1), :REST] = diagonal[:, LANES:]
            return 0

        lax.fori_loop(0, 2, one, 0)
        fresh[slot, :MAXPNO, :] = squares[0, :MAXPNO, :LANES]
        fresh[slot, HALF_PACK : HALF_PACK + MAXPNO, :] = squares[1, :MAXPNO, :LANES]
        shared = jnp.where(
            pack_lane < REST, squares[0, :MAXPNO, LANES:], pltpu.roll(squares[1, :MAXPNO, LANES:], REST, 1)
        )
        fresh[slot, MAXPNO:HALF_PACK, :] = shared[:TOP]
        fresh[slot, HALF_PACK + MAXPNO : FOLD_AT, :] = shared[TOP:]
        folded = jnp.zeros((FOLD_ROWS, LANES), jnp.float32)
        for n in range(SQUARE_ROWS // FOLD_ROWS):
            rows = squares[1, n * FOLD_ROWS : (n + 1) * FOLD_ROWS, LANES:]
            moved = pltpu.roll(rows, (n * LEFT - SPARE) % LANES, 1)
            folded = jnp.where((fold_lane >= n * LEFT) & (fold_lane < (n + 1) * LEFT), moved, folded)
        fresh[slot, FOLD_AT:DIAG_AT, :] = folded

    def begin_half(slot, way, step, half):
        for piece in range(2):
            rows = rows_of(half, piece)
            sums[way, step, rows, :] = fresh[slot, rows, :]
            chain(way, step, half, piece).start()

    def add_half(way, step, half):
        for piece in range(2):
            rows = rows_of(half, piece)
            chain(way, step - 1, half, piece).wait_recv()
            sums[way, step, rows, :] = sums[way, step, rows, :] + fresh[way, rows, :]
            chain(way, step, half, piece).start()

    def ring_item(whole, item, _):
        way, step, first = locate(item)

        @pl.when(item == planes - 1)
        def _():
            prepare(planes - 1, planes)

        block_products(way, first, locate(item + 1)[2], whole)

        @pl.when(item == 0)
        def _():
            begin_half(0, 0, 0, 0)
            begin_half(0, 1, 0, 1)

        @pl.when(step == 1)
        def _():
            begin_half(way, way, step, 1 - way)

        @pl.when((step > 1) & (step < half_ring))
        def _():
            add_half(way, step, 1 - way)

        @pl.when((way == 1) & (step < half_ring))
        def _():
            add_half(0, step, 0)
            add_half(1, step, 1)

        @pl.when(item == 2)
        def _():
            for n in range(len(peers)):
                ask(n).wait_send()
            for port in ports:
                port.finish_sends()
            for single in singles:
                single.finish_served()
                single.finish_sends()

        return 0

    fresh[...] = jnp.zeros_like(fresh)
    squares[...] = jnp.zeros_like(squares)
    ahead = 3
    table_copy.wait()
    ports[0].finish_delivery()
    ports[1].finish_delivery()
    assemble(locate(0)[2], 0, (0, 1))
    lax.fori_loop(0, 2 * ahead, first_half, 0)
    for single in singles:
        single.finish_delivery()
    ports[2].finish_delivery()
    ports[3].finish_delivery()
    assemble(locate(0)[2], 0, (2, 3))
    lax.fori_loop(0, ahead, functools.partial(ring_item, False), 0)
    assemble(locate(ahead)[2], 0, (0, 1, 2, 3))
    lax.fori_loop(ahead, planes, functools.partial(ring_item, True), 0)
    for half in (1, 0):
        for piece in range(2):
            rows = rows_of(half, piece)
            for way in range(2):
                chain(way, half_ring - 1, half, piece).wait_recv()
            arrived = sums[0, half_ring, rows, :] + sums[1, half_ring, rows, :]
            out[rows, :] = arrived + fresh[0, rows, :]
    for n in range(group):
        count = counts[at_z * group + n].astype(jnp.float32)
        out[COUNTS + n : COUNTS + n + 1, :] = jnp.full((1, LANES), count)
    for step in range(half_ring):
        for way in range(2):
            for half in range(2):
                if step or half == way:
                    for piece in range(2):
                        chain(way, step, half, piece).wait_send()


def pair_products(blocks, domains, counts, coeff, planes):
    pair_dev, depth, slots = coeff.shape
    lines = 2 * RING * CORES
    bf16 = jnp.bfloat16
    tile = (MAIN, LANES)
    scratch = []
    for shape in (
        (RING, ATOMS),
        (RING * RING * CORES * ATOMS,),
        (2, ATOMS // 2),
        (RING, CORES, SHARE),
        (2, CORES, HALF_SHARE),
        (RING, SLOTS),
    ):
        scratch += [pltpu.VMEM(shape + tile, bf16)] * 4
    for shape in (
        (ATOMS,),
        (RING - 1, ATOMS),
        (RING, CORES, PICKS),
        (2, CORES, HALF),
        (RING * CORES * PICKS,),
    ):
        scratch += [pltpu.VMEM(shape + tile, bf16)] * 2
    scratch += [
        pltpu.VMEM((lines, 8, LANES), jnp.int32),
        pltpu.SMEM((lines, 8, LANES), jnp.int32),
        pltpu.VMEM((3, 8, LANES), jnp.int32),
        pltpu.SMEM((3, 8, LANES), jnp.int32),
        pltpu.VMEM((8, LANES), jnp.int32),
        pltpu.VMEM((8, LANES), jnp.int32),
        pltpu.VMEM((ATOMS * MAIN, ATOMS * MAIN), bf16),
        pltpu.VMEM((ATOMS * MAIN, ATOMS * MAIN), bf16),
        pltpu.VMEM((pair_dev, depth, slots), bf16),
        pltpu.VMEM((pair_dev, MAXPNO, DEPTH), bf16),
        pltpu.VMEM((DEPTH, depth), bf16),
        pltpu.VMEM((2, DEPTH, blocks.shape[2]), bf16),
        pltpu.VMEM((pair_dev, MAXPNO, MAXPNO), jnp.float32),
        pltpu.VMEM((2, planes // 2 + 1, PACK, LANES), jnp.float32),
        pltpu.VMEM((2, PACK, LANES), jnp.float32),
        pltpu.VMEM((MAXPNO, slots), bf16),
        pltpu.VMEM((2, SQUARE_ROWS, 2 * LANES), jnp.float32),
        pltpu.VMEM(blocks.shape, bf16),
        pltpu.SemaphoreType.DMA((4, 27)),
        pltpu.SemaphoreType.DMA((4, 27)),
        pltpu.SemaphoreType.DMA((2, 16)),
        pltpu.SemaphoreType.DMA((2, 16)),
        pltpu.SemaphoreType.DMA((lines,)),
        pltpu.SemaphoreType.DMA((lines,)),
        pltpu.SemaphoreType.DMA((8,)),
        pltpu.SemaphoreType.DMA((2 * planes, 2)),
        pltpu.SemaphoreType.DMA((2 * planes, 2)),
    ]
    return pl.pallas_call(
        main_kernel,
        out_shape=pltpu.VMEM((PACK, LANES), jnp.float32),
        in_specs=[
            pl.BlockSpec(memory_space=pl.ANY),
            pl.BlockSpec(memory_space=pltpu.SMEM),
            pl.BlockSpec(memory_space=pltpu.SMEM),
            pl.BlockSpec(memory_space=pl.ANY),
        ],
        out_specs=pl.BlockSpec(memory_space=pltpu.VMEM),
        scratch_shapes=scratch,
        compiler_params=params(60, collective_id=0, has_side_effects=True),
    )(blocks, domains, counts, coeff)


def tail_kernel(packed, amp, energy_row, energy_col, out, wide):
    slots = amp.shape[1]
    step = pl.program_id(0)
    full_row = lax.broadcasted_iota(jnp.int32, (slots, slots), 0)
    full_col = lax.broadcasted_iota(jnp.int32, (slots, slots), 1)
    lane = lax.broadcasted_iota(jnp.int32, (MAXPNO, LANES), 1)
    fold_lane = lax.broadcasted_iota(jnp.int32, (FOLD_ROWS, LANES), 1)
    wide[MAXPNO:, :] = jnp.zeros((slots - MAXPNO, slots), jnp.float32)

    def shared_at(begin, end):
        if end <= TOP:
            return packed[MAXPNO + begin : MAXPNO + end, :]
        return packed[HALF_PACK + MAXPNO + begin - TOP : HALF_PACK + MAXPNO + end - TOP, :]

    @pl.when(step == 0)
    def _():
        wide[:MAXPNO, :LANES] = packed[:MAXPNO, :]
        for begin, end in ((0, TOP), (TOP, MAXPNO)):
            wide[begin:end, LANES:] = jnp.where(lane[begin:end] < REST, shared_at(begin, end), 0.0)

    @pl.when(step == 1)
    def _():
        wide[:MAXPNO, :LANES] = packed[HALF_PACK : HALF_PACK + MAXPNO, :]
        for begin, end in ((0, TOP), (TOP, MAXPNO)):
            turned = pltpu.roll(shared_at(begin, end), SPARE, 1)
            wide[begin:end, LANES:] = jnp.where(lane[begin:end] < SPARE, turned, 0.0)
        folded = packed[FOLD_AT:DIAG_AT, :]
        for n in range(SQUARE_ROWS // FOLD_ROWS):
            begin, end = n * FOLD_ROWS, min((n + 1) * FOLD_ROWS, MAXPNO)
            moved = pltpu.roll(folded, (SPARE - n * LEFT) % LANES, 1)
            left = (fold_lane >= SPARE) & (fold_lane < REST)
            held = wide[begin:end, LANES:]
            wide[begin:end, LANES:] = jnp.where(left[: end - begin], moved[: end - begin], held)

    square = wide[...]
    at = DIAG_AT + 2 * step
    diagonal = jnp.concatenate([packed[pl.ds(at, 1), :], packed[pl.ds(at + 1, 1), :]], axis=1)
    on_diagonal = full_row == full_col
    for n in range(2):
        count = packed[pl.ds(COUNTS + 2 * step + n, 1), :][:, :1].astype(jnp.int32)
        row, col = full_row[:MAXPNO], full_col[:MAXPNO]
        if n == 0:
            held = jnp.where(full_row >= full_col, square, 0.0)
        else:
            held = jnp.where(full_row < full_col, square, jnp.where(on_diagonal, diagonal, 0.0))
        products = held[:MAXPNO] + jnp.where(row == col, 0.0, held.T[:MAXPNO])
        valid = (row < count) & (col < count)
        products = jnp.where(valid, products / NAUX, 0.0)
        amps = amp[n]
        contract = (((1,), (1,)), ((), ()))
        high = products.astype(jnp.bfloat16)
        left = products - high.astype(jnp.float32)
        mid = left.astype(jnp.bfloat16)
        low = (left - mid.astype(jnp.float32)).astype(jnp.bfloat16)
        coupled = lax.dot_general(low, amps, contract, preferred_element_type=jnp.float32)
        coupled += lax.dot_general(mid, amps, contract, preferred_element_type=jnp.float32)
        coupled += lax.dot_general(high, amps, contract, preferred_element_type=jnp.float32)
        energies = energy_col[n, :MAXPNO] + energy_row[pl.ds(2 * step + n, 1), :]
        result = products + coupled + energies * amps[:MAXPNO].astype(jnp.float32)
        out[n, :MAXPNO] = jnp.where(valid, result, 0.0)
        out[n, MAXPNO:] = jnp.zeros((slots - MAXPNO, slots), jnp.float32)


def tail(packed, amp, energy):
    subs, slots, _ = amp.shape
    return pl.pallas_call(
        tail_kernel,
        out_shape=jax.ShapeDtypeStruct((subs, slots, slots), jnp.float32),
        grid=(subs // 2,),
        in_specs=[
            pl.BlockSpec((PACK, LANES), lambda i: (0, 0)),
            pl.BlockSpec((2, slots, slots), lambda i: (i, 0, 0)),
            pl.BlockSpec((subs, slots), lambda i: (0, 0)),
            pl.BlockSpec((2, slots, 1), lambda i: (i, 0, 0)),
        ],
        out_specs=pl.BlockSpec((2, slots, slots), lambda i: (i, 0, 0)),
        scratch_shapes=[pltpu.VMEM((slots, slots), jnp.float32)],
        compiler_params=params(32),
    )(packed, amp, energy, energy[:, :, None])


def on_device(atom_blocks, domains, pno_counts, pno_coeffs, amplitudes, pno_energies):
    planes = lax.axis_size("ri")
    mine = pair_products(atom_blocks.transpose(1, 0, 2), domains.T, pno_counts, pno_coeffs, planes)
    return tail(mine, amplitudes, pno_energies)


def solution(mesh):
    placed = (
        P("pairs", None, "ri"),
        P("pairs", None),
        P("pairs"),
        P("pairs", None, None),
        P(("pairs", "ri"), None, None),
        P(("pairs", "ri"), None),
    )
    return jax.shard_map(
        on_device,
        mesh=mesh,
        in_specs=placed,
        out_specs=P(("pairs", "ri"), None, None),
        check_vma=False,
    )
```

```python
import functools

import jax
import jax.numpy as jnp
from jax import lax
from jax.experimental import pallas as pl
from jax.experimental.pallas import tpu as pltpu
from jax.sharding import PartitionSpec as P

NAUX = 14336
CAP = 3
MAXPNO = 200
MAIN = 16
REM = 4
SPLIT = 128
REST = MAXPNO - SPLIT
LANES = 128
MIB = 1 << 20
RING = 4
CORES = 2
ATOMS = 16
DOM = 12
BAND = MAIN + REM
PICKS = RING * CAP
HALF = PICKS // 2
DEPTH = 256
SPARE = LANES - REST
LEFT = REST - SPARE
FOLD_ROWS = 32
HALF_PACK = 320
PACK = 2 * HALF_PACK
TOP = HALF_PACK - MAXPNO
FOLD_AT = PACK - FOLD_ROWS - 8
DIAG_AT = PACK - 8
COUNTS = PACK - 4
SQUARE_ROWS = 224
SLOTS = 48
SHARE = SLOTS // CORES
HALF_SHARE = SHARE // 2
ROW_LINES = RING * CORES
MAINS = ((0, 1, 2), (3, 4, 5), (6, 7, 8), (10, 11, 12))
RESTS = ((0, 1, 2), (3, 4, 5), (6, 7, 8, 9), (10, 11, 12, 13))
SINGLES = (9, 13)
MESH = pl.DeviceIdType.MESH


def params(mib, **kw):
    return pltpu.CompilerParams(vmem_limit_bytes=mib * MIB, **kw)


class Ports:
    def __init__(self, chunk, gather_to, deliver_to, wire, ring, send, relay, recv, out_sems, in_sems, core):
        self.gather_to, self.deliver_to, self.core = gather_to, deliver_to, core
        self.wire, self.ring, self.send, self.relay, self.recv = wire, ring, send, relay, recv
        self.out_sems, self.in_sems, self.chunk = out_sems, in_sems, chunk

    def copy(self, src, dst, out_at, in_at, to):
        return pltpu.make_async_remote_copy(
            src_ref=src,
            dst_ref=dst,
            send_sem=self.out_sems.at[self.chunk, out_at],
            recv_sem=self.in_sems.at[self.chunk, in_at],
            device_id={"pairs": to},
            device_id_type=MESH,
        )

    def gather_first(self):
        up = self.copy(self.wire, self.ring.at[2], 0, 1, self.gather_to(1, self.core))
        down = self.copy(self.wire, self.ring.at[0], 1, 0, self.gather_to(3, self.core))
        return up, down

    def gather_second(self):
        half = ATOMS // 2
        low, high = pl.ds(0, half), pl.ds(half, half)
        up = self.copy(self.ring.at[2, low], self.ring.at[1, low], 2, 2, self.gather_to(1, self.core))
        down = self.copy(self.ring.at[0, high], self.ring.at[1, high], 3, 3, self.gather_to(3, self.core))
        return up, down

    def place(self, rel, core):
        return (rel * CORES + core) * PICKS

    def far(self):
        up = self.copy(self.send.at[2, :, pl.ds(0, HALF)], self.relay.at[0], 4, 4, self.deliver_to(1, self.core))
        down = self.copy(self.send.at[2, :, pl.ds(HALF, HALF)], self.relay.at[1], 5, 5, self.deliver_to(3, self.core))
        return up, down

    def near(self):
        copies = []
        for n, step in enumerate((1, 3)):
            for core in range(CORES):
                dst = self.recv.at[pl.ds(self.place(RING - step, self.core), PICKS)]
                at = 6 + 2 * n
                copies.append(self.copy(self.send.at[step, core], dst, at + core, at + self.core, self.deliver_to(step, core)))
        other = 1 - self.core
        dst = self.recv.at[pl.ds(self.place(0, self.core), PICKS)]
        copies.append(self.copy(self.send.at[0, other], dst, 10, 10, self.deliver_to(0, other)))
        return copies

    def own(self):
        return pltpu.make_async_copy(
            self.send.at[0, self.core],
            self.recv.at[pl.ds(self.place(0, self.core), PICKS)],
            self.in_sems.at[self.chunk, 11],
        )

    def onward(self):
        copies = []
        for way, step in enumerate((1, 3)):
            for core in range(CORES):
                dst = self.recv.at[pl.ds(self.place(2, self.core) + way * HALF, HALF)]
                at = 12 + 2 * way
                copies.append(self.copy(self.relay.at[way, core], dst, at + core, at + self.core, self.deliver_to(step, core)))
        return copies

    def start_gather(self):
        for copy in self.gather_first():
            copy.start()

    def forward_gather(self):
        up, down = self.gather_second()
        first_up, first_down = self.gather_first()
        first_up.wait_recv()
        up.start()
        first_down.wait_recv()
        down.start()

    def finish_gather(self):
        for copy in self.gather_second():
            copy.wait_recv()

    def start_far(self):
        for copy in self.far():
            copy.start()

    def start_near(self):
        for copy in self.near():
            copy.start()
        self.own().start()

    def forward_delivery(self):
        far, onward = self.far(), self.onward()
        for way in range(2):
            far[way].wait_recv()
            for copy in onward[2 * way : 2 * way + 2]:
                copy.start()

    def finish_delivery(self):
        for n, step in enumerate((1, 3)):
            for core in range(CORES):
                dst = self.recv.at[pl.ds(self.place(step, core), PICKS)]
                at = 6 + 2 * (1 - n)
                self.copy(dst, dst, at + core, at + core, self.deliver_to(1, self.core)).wait_recv()
        other = 1 - self.core
        dst = self.recv.at[pl.ds(self.place(0, other), PICKS)]
        self.copy(dst, dst, 10, 10, self.deliver_to(1, self.core)).wait_recv()
        self.own().wait()
        for way in range(2):
            for core in range(CORES):
                dst = self.recv.at[pl.ds(self.place(2, core) + way * HALF, HALF)]
                at = 12 + 2 * way
                self.copy(dst, dst, at + core, at + core, self.deliver_to(1, self.core)).wait_recv()

    def finish_served(self):
        for copy in self.far() + tuple(self.near()):
            copy.wait_send()

    def finish_sends(self):
        for copy in self.gather_first() + self.gather_second() + tuple(self.onward()):
            copy.wait_send()


class Relay:
    def __init__(self, chunk, first_to, other_to, u, v, core, bufs, out_sems, in_sems):
        self.chunk, self.first_to, self.other_to = chunk, first_to, other_to
        self.u, self.v, self.core = u, v, core
        self.wire, self.table, self.passing, self.send, self.relay, self.recv = bufs
        self.out_sems, self.in_sems = out_sems, in_sems

    def copy(self, src, dst, out_at, in_at, to):
        return pltpu.make_async_remote_copy(
            src_ref=src,
            dst_ref=dst,
            send_sem=self.out_sems.at[self.chunk, out_at],
            recv_sem=self.in_sems.at[self.chunk, in_at],
            device_id={"pairs": to},
            device_id_type=MESH,
        )

    def arrival(self, dst, at):
        return self.copy(dst, dst, at, at, self.first_to(1, self.core))

    def near_u(self, step):
        return lax.rem(self.u + step, RING)

    def near_v(self, step):
        return lax.rem(self.v + step, RING)

    def atoms(self, step, at=0, count=ATOMS):
        base = ((self.v * CORES + self.core) * RING + self.near_u(step)) * ATOMS
        return self.table.at[pl.ds(base + at, count)]

    def block(self, step, core, at=0, count=RING * ATOMS):
        return self.table.at[pl.ds((self.near_v(step) * CORES + core) * RING * ATOMS + at, count)]

    def spread_sends(self):
        half = ATOMS // 2
        far = self.near_u(2)
        up, down = self.first_to(1, self.core), self.first_to(3, self.core)
        return [
            self.copy(self.wire.at[far, pl.ds(0, half)], self.passing.at[0], 2, 2, up),
            self.copy(self.wire.at[far, pl.ds(half, half)], self.passing.at[1], 3, 3, down),
            self.copy(self.wire.at[self.near_u(1)], self.atoms(0), 0, 1, up),
            self.copy(self.wire.at[self.near_u(3)], self.atoms(0), 1, 0, down),
        ]

    def spread_own(self):
        return pltpu.make_async_copy(self.wire.at[self.u], self.atoms(0), self.in_sems.at[self.chunk, 25])

    def spread_onward(self):
        half = ATOMS // 2
        return [
            self.copy(self.passing.at[0], self.atoms(3, 0, half), 4, 4, self.first_to(1, self.core)),
            self.copy(self.passing.at[1], self.atoms(1, half, half), 5, 5, self.first_to(3, self.core)),
        ]

    def start_spread(self):
        for copy in self.spread_sends():
            copy.start()
        self.spread_own().start()

    def forward_spread(self):
        for way, copy in enumerate(self.spread_onward()):
            self.arrival(self.passing.at[way], 2 + way).wait_recv()
            copy.start()

    def finish_spread(self):
        half = ATOMS // 2
        self.spread_own().wait()
        self.arrival(self.atoms(1), 0).wait_recv()
        self.arrival(self.atoms(3), 1).wait_recv()
        self.arrival(self.atoms(2, 0, half), 4).wait_recv()
        self.arrival(self.atoms(2, half, half), 5).wait_recv()

    def gather_first(self):
        own = self.block(0, self.core)
        return [
            self.copy(own, own, 6, 7, self.other_to(1, self.core)),
            self.copy(own, own, 7, 6, self.other_to(3, self.core)),
        ]

    def gather_second(self):
        half = RING * ATOMS // 2
        low, high = self.block(3, self.core, 0, half), self.block(1, self.core, half, half)
        return [
            self.copy(low, low, 8, 8, self.other_to(1, self.core)),
            self.copy(high, high, 9, 9, self.other_to(3, self.core)),
        ]

    def share(self, step):
        mine = self.block(step, self.core)
        return self.copy(mine, mine, 10 + step, 10 + step, self.first_to(0, 1 - self.core))

    def start_gather(self):
        for copy in self.gather_first():
            copy.start()
        self.share(0).start()

    def forward_gather(self):
        low, high = self.gather_second()
        self.arrival(self.block(3, self.core), 7).wait_recv()
        low.start()
        self.share(3).start()
        self.arrival(self.block(1, self.core), 6).wait_recv()
        high.start()
        self.share(1).start()

    def finish_gather(self):
        half = RING * ATOMS // 2
        self.arrival(self.block(2, self.core, 0, half), 8).wait_recv()
        self.arrival(self.block(2, self.core, half, half), 9).wait_recv()
        self.share(2).start()

    def finish_share(self):
        for step in range(RING):
            self.arrival(self.block(step, 1 - self.core), 10 + step).wait_recv()

    def place(self, step, core, at=0, count=SHARE):
        return self.recv.at[self.near_u(step), pl.ds(core * SHARE + at, count)]

    def far(self):
        return [
            self.copy(self.send.at[2, :, pl.ds(0, HALF_SHARE)], self.relay.at[0], 19, 19, self.first_to(1, self.core)),
            self.copy(
                self.send.at[2, :, pl.ds(HALF_SHARE, HALF_SHARE)], self.relay.at[1], 20, 20, self.first_to(3, self.core)
            ),
        ]

    def near(self):
        copies = []
        dst = self.place(0, self.core)
        for n, step in enumerate((1, 3)):
            for core in range(CORES):
                at = 14 + 2 * n
                copies.append(self.copy(self.send.at[step, core], dst, at + core, at + self.core, self.first_to(step, core)))
        other = 1 - self.core
        copies.append(self.copy(self.send.at[0, other], dst, 18, 18, self.first_to(0, other)))
        return copies

    def own(self):
        return pltpu.make_async_copy(
            self.send.at[0, self.core], self.place(0, self.core), self.in_sems.at[self.chunk, 26]
        )

    def onward(self):
        copies = []
        for way, step in enumerate((1, 3)):
            dst = self.place(RING - step, self.core, way * HALF_SHARE, HALF_SHARE)
            for core in range(CORES):
                at = 21 + 2 * way
                copies.append(self.copy(self.relay.at[way, core], dst, at + core, at + self.core, self.first_to(step, core)))
        return copies

    def start_far(self):
        for copy in self.far():
            copy.start()

    def start_near(self):
        for copy in self.near():
            copy.start()
        self.own().start()

    def forward_delivery(self):
        onward = self.onward()
        for way in range(2):
            self.arrival(self.relay.at[way], 19 + way).wait_recv()
            for copy in onward[2 * way : 2 * way + 2]:
                copy.start()

    def finish_delivery(self):
        for core in range(CORES):
            self.arrival(self.place(3, core), 14 + core).wait_recv()
            self.arrival(self.place(1, core), 16 + core).wait_recv()
            for way in range(2):
                at = 21 + 2 * way + core
                self.arrival(self.place(2, core, way * HALF_SHARE, HALF_SHARE), at).wait_recv()
        self.arrival(self.place(0, 1 - self.core), 18).wait_recv()
        self.own().wait()

    def finish_sends(self):
        copies = self.spread_sends() + self.spread_onward() + self.gather_first() + self.gather_second()
        copies += [self.share(step) for step in range(RING)] + self.far() + self.near() + self.onward()
        for copy in copies:
            copy.wait_send()


def main_kernel(
    blocks_hbm, domains, counts, coeff_hbm, out, *scratch
):
    relay_bufs = [scratch[4 * n : 4 * n + 4] for n in range(6)]
    single_bufs = [scratch[24 + 2 * n : 26 + 2 * n] for n in range(5)]
    wires, recvs = relay_bufs[0], relay_bufs[5]
    single_wires, single_recvs = single_bufs[0], single_bufs[4]
    asked, asked_smem, tables, places, request, ids, perm_main, perm_rest = scratch[34:42]
    coeff, coeff_t, perm, blk, total, sums, fresh, same, squares, blocks = scratch[42:52]
    out_sems, in_sems, single_out, single_in, ask_out, ask_in, local_sems, sum_out, sum_in = scratch[52:61]
    me = lax.axis_index("pairs")
    at_z = lax.axis_index("ri")
    planes = 2 * (sums.shape[1] - 1)
    above, below = lax.rem(at_z + 1, planes), lax.rem(at_z + planes - 1, planes)
    core = lax.rem(me, CORES)
    chip = lax.div(me, CORES)
    at_x = lax.rem(chip, RING)
    at_y = lax.div(chip, RING)

    def along_x(step, to_core):
        return (at_y * RING + lax.rem(at_x + step, RING)) * CORES + to_core

    def along_y(step, to_core):
        return (lax.rem(at_y + step, RING) * RING + at_x) * CORES + to_core

    peers = []
    for to_core in range(2):
        for step in range(1, RING):
            peers.append((along_y(step, to_core), step * CORES + to_core, (RING - step) * CORES + core))
            peers.append(
                (along_x(step, to_core), (RING + step) * CORES + to_core, (2 * RING - step) * CORES + core)
            )
    peers.append((along_x(0, 1 - core), 1 - core, core))

    barrier = pltpu.get_barrier_semaphore()
    for peer, _, _ in peers:
        pl.semaphore_signal(barrier, inc=1, device_id={"pairs": peer}, device_id_type=MESH)
    for plane in (above, below):
        pl.semaphore_signal(barrier, inc=1, device_id={"ri": plane}, device_id_type=MESH)

    def ask(n):
        peer, _, there = peers[n]
        return pltpu.make_async_remote_copy(
            src_ref=request,
            dst_ref=asked.at[there],
            send_sem=ask_out.at[n],
            recv_sem=ask_in.at[there],
            device_id={"pairs": peer},
            device_id_type=MESH,
        )

    ports = []
    for chunk in range(4):
        by_x = chunk % 2 == 0
        first_to, other_to = (along_x, along_y) if by_x else (along_y, along_x)
        u, v = (at_x, at_y) if by_x else (at_y, at_x)
        bufs = [group_bufs[chunk] for group_bufs in relay_bufs]
        ports.append(Relay(chunk, first_to, other_to, u, v, core, bufs, out_sems, in_sems))
    singles = []
    for n in range(2):
        gather_to, deliver_to = (along_x, along_y) if n == 0 else (along_y, along_x)
        bufs = [group_bufs[n] for group_bufs in single_bufs]
        singles.append(Ports(n, gather_to, deliver_to, *bufs, single_out, single_in, core))

    fetches = []
    for chunk in range(4):
        tiles = RESTS[chunk]
        cols = pl.ds(tiles[0] * LANES, len(tiles) * LANES)
        fetches.append(
            pltpu.make_async_copy(blocks_hbm.at[:, :, cols], blocks.at[:, :, cols], local_sems.at[4 + chunk])
        )
        fetches[chunk].start()
    fetch = pltpu.make_async_copy(coeff_hbm, coeff, local_sems.at[0])
    fetch.start()

    square = (ATOMS * MAIN, ATOMS * MAIN)
    out_at = lax.broadcasted_iota(jnp.int32, square, 0)
    from_at = lax.broadcasted_iota(jnp.int32, square, 1)
    band_at, atom_at = out_at & (MAIN - 1), lax.shift_right_logical(out_at, 4)
    perm_main[...] = jnp.where(band_at * ATOMS + atom_at == from_at, 1.0, 0.0).astype(jnp.bfloat16)
    rest_at = lax.shift_right_logical(band_at, 2) * (REM * ATOMS) + (band_at & (REM - 1)) * ATOMS + atom_at
    perm_rest[...] = jnp.where(rest_at == from_at, 1.0, 0.0).astype(jnp.bfloat16)

    def main_rows(tiles):
        flat = blocks[:MAIN, :, tiles[0] * LANES : (tiles[-1] + 1) * LANES]
        flat = flat.reshape(MAIN * ATOMS, len(tiles) * LANES)
        return jnp.dot(perm_main[...], flat, preferred_element_type=jnp.float32).astype(jnp.bfloat16)

    def form(chunk):
        fetches[chunk].wait()
        main = main_rows(MAINS[chunk])
        for n in range(len(MAINS[chunk])):
            wires[chunk][n] = main[:, n * LANES : (n + 1) * LANES].reshape(ATOMS, MAIN, LANES)
        parts = [blocks[MAIN:, :, t * LANES : (t + 1) * LANES].reshape(REM * ATOMS, LANES) for t in RESTS[chunk]]
        stacked = jnp.concatenate(parts, axis=0)
        depth = stacked.shape[0]
        late = jnp.dot(perm_rest[:, :depth], stacked, preferred_element_type=jnp.float32).astype(jnp.bfloat16)
        wires[chunk][RING - 1] = late.reshape(ATOMS, MAIN, LANES)

    form(0)
    pl.semaphore_wait(barrier, len(peers) + 2)
    ports[0].start_spread()
    for chunk in range(1, 4):
        form(chunk)
        ports[chunk].start_spread()
    for n in range(2):
        single_wires[n][...] = main_rows(SINGLES[n : n + 1]).reshape(ATOMS, MAIN, LANES)
    for chunk in (0, 1):
        ports[chunk].forward_spread()
    for chunk in (0, 1):
        ports[chunk].finish_spread()
        ports[chunk].start_gather()

    for chunk in (2, 3):
        ports[chunk].forward_spread()

    def parts_of(atom):
        owner = lax.shift_right_logical(atom, 4)
        chip = lax.shift_right_logical(owner, 1)
        return owner, owner & (CORES - 1), chip & (RING - 1), lax.shift_right_logical(chip, 2), atom & (ATOMS - 1)

    map_shape = (8, LANES)
    map_row = lax.broadcasted_iota(jnp.int32, map_shape, 0)
    map_lane = lax.broadcasted_iota(jnp.int32, map_shape, 1)
    atom_map = map_row * LANES + map_lane
    pairs = domains.shape[1]

    def mark(pair, seen):
        for k in range(DOM):
            seen = jnp.where(atom_map == domains[k, pair], 1, seen)
        return seen

    named = lax.fori_loop(0, pairs, mark, jnp.zeros(map_shape, jnp.int32))
    owner, owner_core, owner_x, owner_y, local = parts_of(atom_map)
    rank = named
    for shift in (1, 2, 4, 8):
        rank = rank + jnp.where(local >= shift, pltpu.roll(rank, shift, 1), 0)
    order = named
    for shift in (1, 2, 4, 8, 16, 32, 64):
        order = order + jnp.where(map_lane >= shift, pltpu.roll(order, shift, 1), 0)
    counted = order
    map_rows = ATOMS * RING * RING * CORES // LANES
    for n in range(map_rows - 1):
        order = order + jnp.where(map_row > n, counted[n : n + 1, LANES - 1 :], 0)
    rel_x = (owner_x + RING - at_x) & (RING - 1)
    rel_y = (owner_y + RING - at_y) & (RING - 1)
    tables[0] = order - 1
    tables[1] = ((rel_y * CORES + owner_core) * RING + rel_x) * CAP + rank - 1
    tables[2] = ((rel_x * CORES + owner_core) * RING + rel_y) * CAP + rank - 1
    table_copy = pltpu.make_async_copy(tables, places, local_sems.at[3])
    table_copy.start()

    ids[:map_rows, :] = jnp.where(named > 0, order, 0)[:map_rows]
    ids[map_rows:, :] = jnp.where(named > 0, rank, 0)[:map_rows]
    upright = ids[...].T
    list_shape = (LANES, LANES)
    list_row = lax.broadcasted_iota(jnp.int32, list_shape, 0)
    list_lane = lax.broadcasted_iota(jnp.int32, list_shape, 1)
    rows = [jnp.zeros((1, LANES), jnp.int32) for _ in range(CAP + 2)]
    for n in range(map_rows):
        owner, owner_core, owner_x, owner_y, local = parts_of(list_row + n * LANES)
        own_lane = jnp.where(owner == list_lane, local, 0)
        order_at = jnp.broadcast_to(upright[:, n : n + 1], list_shape)
        rank_at = jnp.broadcast_to(upright[:, map_rows + n : map_rows + n + 1], list_shape)
        for j in range(CAP):
            rows[j] += jnp.sum(jnp.where(rank_at == j + 1, own_lane, 0), axis=0, keepdims=True)
        for j, (u, v) in enumerate(((owner_x, owner_y), (owner_y, owner_x))):
            held_at = ((v * CORES + owner_core) * RING + u) * ATOMS + local
            rows[CAP + j] += jnp.sum(jnp.where(order_at == list_lane + 1, held_at, 0), axis=0, keepdims=True)
    for n in range(CAP + 2):
        request[n : n + 1, :] = rows[n]
    request[CAP + 2 :, :] = jnp.zeros((6 - CAP, LANES), jnp.int32)

    for n in range(len(peers)):
        ask(n).start()
    own_ask = pltpu.make_async_copy(request, asked.at[core], local_sems.at[1])
    own_ask.start()
    for chunk in (2, 3):
        ports[chunk].finish_spread()

    shape = (DEPTH, DOM * BAND)
    row = lax.broadcasted_iota(jnp.int32, shape, 0)
    col = lax.broadcasted_iota(jnp.int32, shape, 1)
    split = DOM * MAIN
    late = row - split
    source = jnp.where(
        row < split,
        lax.shift_right_logical(row, 4) * BAND + (row & (MAIN - 1)),
        lax.shift_right_arithmetic(late, 2) * BAND + MAIN + (late & (REM - 1)),
    )
    perm[...] = jnp.where((source == col) & (row < DOM * BAND), 1.0, 0.0).astype(jnp.bfloat16)
    same[...] = jnp.where(
        lax.broadcasted_iota(jnp.int32, same.shape, 0) == lax.broadcasted_iota(jnp.int32, same.shape, 1), 1.0, 0.0
    ).astype(jnp.bfloat16)
    for n in range(2):
        blk[n, DOM * BAND :, :] = jnp.zeros((DEPTH - DOM * BAND, blk.shape[2]), jnp.bfloat16)
    fetch.wait()

    group = coeff.shape[0] // planes
    half_ring = planes // 2

    def locate(item):
        step = (item + 1) // 2
        way = jnp.where(item == 0, 0, (item + 1) % 2)
        away = jnp.where(way == 0, half_ring - step, half_ring + step)
        return way, step, lax.rem(at_z + away, planes) * group

    def prepare(begin, end):
        def turn(item, _):
            first = locate(item)[2]
            ordered = [
                jnp.dot(perm[...], coeff[first + n], preferred_element_type=jnp.float32).astype(jnp.bfloat16)
                for n in range(group)
            ]
            for n in range(group):
                turned = lax.dot_general(
                    same[...], ordered[n], (((1,), (1,)), ((), ())), preferred_element_type=jnp.float32
                )
                coeff_t[first + n] = turned.astype(jnp.bfloat16)
            return 0

        lax.fori_loop(begin, end, turn, 0)

    prepare(0, 1)
    for chunk in (0, 1):
        ports[chunk].forward_gather()

    prepare(1, 3)

    own_ask.wait()
    for n in range(len(peers)):
        _, here, _ = peers[n]
        pltpu.make_async_remote_copy(
            src_ref=request,
            dst_ref=asked.at[here],
            send_sem=ask_out.at[n],
            recv_sem=ask_in.at[here],
            device_id={"pairs": peers[n][0]},
            device_id_type=MESH,
        ).wait_recv()
    to_smem = pltpu.make_async_copy(asked, asked_smem, local_sems.at[2])
    to_smem.start()
    to_smem.wait()

    def line_of(dest, on_row):
        return jnp.where(dest < CORES, dest, dest + ROW_LINES) if on_row else dest

    def pick_single(n):
        port = singles[n]
        owner_of = along_x if n == 0 else along_y

        def serve(dest, _):
            line = line_of(dest, n == 1)
            step, to_core = dest // CORES, dest % CORES
            for r in range(RING):
                for j in range(CAP):
                    atom = asked_smem[line, j, owner_of(r, core)]
                    found = port.wire[atom] if r == 0 else port.ring[r - 1, atom]
                    port.send[step, to_core, r * CAP + j] = found
            return 0

        lax.fori_loop(2 * CORES, 3 * CORES, serve, 0)
        port.start_far()

        def serve_near(dest, _):
            return serve(jnp.where(dest < 2 * CORES, dest, dest + CORES), 0)

        lax.fori_loop(0, 3 * CORES, serve_near, 0)
        port.start_near()

    def pick(chunk):
        port = ports[chunk]

        def serve(dest, _):
            line = line_of(dest, chunk % 2 == 0)
            step, to_core = dest // CORES, dest % CORES
            for n in range(SHARE):
                port.send[step, to_core, n] = port.table[asked_smem[line, CAP + chunk % 2, core * SHARE + n]]
            return 0

        lax.fori_loop(2 * CORES, 3 * CORES, serve, 0)
        port.start_far()

        def serve_near(dest, _):
            return serve(jnp.where(dest < 2 * CORES, dest, dest + CORES), 0)

        lax.fori_loop(0, 3 * CORES, serve_near, 0)
        port.start_near()

    for chunk in (0, 1):
        ports[chunk].finish_gather()
        ports[chunk + 2].start_gather()
    for chunk in (0, 1):
        ports[chunk].finish_share()
        pick(chunk)
    for single in singles:
        single.start_gather()
    prepare(3, 5)
    for chunk in (0, 1):
        ports[chunk].forward_delivery()
    for chunk in (2, 3):
        ports[chunk].forward_gather()
    for single in singles:
        single.forward_gather()
    prepare(5, 6)
    for chunk in (2, 3):
        ports[chunk].finish_gather()
    for n in range(2):
        singles[n].finish_gather()
        pick_single(n)
    for chunk in (2, 3):
        ports[chunk].finish_share()
        pick(chunk)
    prepare(6, planes - 1)
    for single in singles:
        single.forward_delivery()
    for chunk in (2, 3):
        ports[chunk].forward_delivery()

    pack_row = lax.broadcasted_iota(jnp.int32, (MAXPNO, MAXPNO), 0)
    pack_col = lax.broadcasted_iota(jnp.int32, (MAXPNO, MAXPNO), 1)
    pack_lane = lax.broadcasted_iota(jnp.int32, (MAXPNO, LANES), 1)
    fold_lane = lax.broadcasted_iota(jnp.int32, (FOLD_ROWS, LANES), 1)

    def assemble(pair, slot, chunks):
        base = MAIN * DOM
        begin = 0
        upper = lax.broadcasted_iota(jnp.int32, (8, LANES), 0) < REM

        names = [domains[k, pair] for k in range(DOM)]

        def named_at(table):
            return [places[table, lax.shift_right_logical(a, 7), a & (LANES - 1)] for a in names]

        at = named_at(0)
        for chunk in chunks:
            tiles = len(RESTS[chunk])
            for n in range(RING - 1):
                span = slice(begin + n * LANES, begin + (n + 1) * LANES)
                for k in range(DOM):
                    blk[slot, MAIN * k : MAIN * (k + 1), span] = recvs[chunk][n, at[k]]
            if tiles == RING:
                span = slice(begin + (RING - 1) * LANES, begin + RING * LANES)
                single_at = named_at(1 + chunk % 2)
                for k in range(DOM):
                    blk[slot, MAIN * k : MAIN * (k + 1), span] = single_recvs[chunk % 2][single_at[k]]
            for k in range(0, DOM, 4):
                rest = [recvs[chunk][RING - 1, at[k + n]].astype(jnp.float32) for n in range(4)]
                for half in range((tiles + 1) // 2):
                    parts = [r[8 * half : 8 * half + 8] for r in rest]
                    shifted = [pltpu.roll(part, REM, 0) for part in parts]
                    for q in range(2 * half, min(2 * half + 2, tiles)):
                        first, second = (parts, shifted) if q % 2 == 0 else (shifted, parts)
                        low = jnp.where(upper, first[0], second[1])
                        high = jnp.where(upper, first[2], second[3])
                        both = jnp.concatenate([low, high], axis=0).astype(jnp.bfloat16)
                        tile = slice(begin + q * LANES, begin + (q + 1) * LANES)
                        blk[slot, base + REM * k : base + REM * (k + 4), tile] = both
            begin += tiles * LANES
        return begin

    def multiply(pair, slot, cols):
        weights = coeff_t[pair]
        vecs = []
        for at in range(0, cols, 256):
            vec = jnp.dot(weights, blk[slot, :, at : at + 256], preferred_element_type=jnp.float32)
            vecs.append(vec.astype(jnp.bfloat16))
        vecs = jnp.concatenate(vecs, axis=1)
        return lax.dot_general(vecs, vecs, (((1,), (1,)), ((), ())), preferred_element_type=jnp.float32)

    early_cols = LANES * (len(RESTS[0]) + len(RESTS[1]))
    late_cols = LANES * (len(RESTS[2]) + len(RESTS[3]))
    part = HALF_PACK // 2

    def rows_of(half, piece):
        return pl.ds(pl.multiple_of(half * HALF_PACK + piece * part, 8), part)

    def chain(way, step, half, piece):
        rows = rows_of(half, piece)
        return pltpu.make_async_remote_copy(
            src_ref=sums.at[way, step, rows],
            dst_ref=sums.at[way, step + 1, rows],
            send_sem=sum_out.at[(way * half_ring + step) * 2 + half, piece],
            recv_sem=sum_in.at[(way * half_ring + step) * 2 + half, piece],
            device_id={"ri": jnp.where(way == 0, above, below)},
            device_id_type=MESH,
        )

    def first_half(step, _):
        pair = locate(step // 2)[2] + 2 * (step % 2)
        following = locate((step + 1) // 2)[2] + 2 * ((step + 1) % 2)
        assemble(pair + 1, 1, (0, 1))
        total[pair] = multiply(pair, 0, early_cols)
        assemble(following, 0, (0, 1))
        total[pair + 1] = multiply(pair + 1, 1, early_cols)
        return 0

    def block_products(slot, first, following, whole):
        chunks = (0, 1, 2, 3) if whole else (2, 3)
        cols = early_cols + late_cols if whole else late_cols

        def one(duo, _):
            pair = first + 2 * duo
            assemble(pair + 1, 1, chunks)
            here = multiply(pair, 0, cols)
            assemble(jnp.where(duo == 0, pair + 2, following), 0, chunks)
            there = multiply(pair + 1, 1, cols)
            if not whole:
                here += total[pair]
                there += total[pair + 1]
            squares[duo, :MAXPNO, :MAXPNO] = jnp.where(pack_row >= pack_col, here, there)
            diagonal = jnp.sum(jnp.where(pack_row == pack_col, there, 0.0), axis=0, keepdims=True)
            at = DIAG_AT + 2 * duo
            fresh[slot, pl.ds(at, 1), :] = diagonal[:, :LANES]
            fresh[slot, pl.ds(at + 1, 1), :REST] = diagonal[:, LANES:]
            return 0

        lax.fori_loop(0, 2, one, 0)
        fresh[slot, :MAXPNO, :] = squares[0, :MAXPNO, :LANES]
        fresh[slot, HALF_PACK : HALF_PACK + MAXPNO, :] = squares[1, :MAXPNO, :LANES]
        shared = jnp.where(
            pack_lane < REST, squares[0, :MAXPNO, LANES:], pltpu.roll(squares[1, :MAXPNO, LANES:], REST, 1)
        )
        fresh[slot, MAXPNO:HALF_PACK, :] = shared[:TOP]
        fresh[slot, HALF_PACK + MAXPNO : FOLD_AT, :] = shared[TOP:]
        folded = jnp.zeros((FOLD_ROWS, LANES), jnp.float32)
        for n in range(SQUARE_ROWS // FOLD_ROWS):
            rows = squares[1, n * FOLD_ROWS : (n + 1) * FOLD_ROWS, LANES:]
            moved = pltpu.roll(rows, (n * LEFT - SPARE) % LANES, 1)
            folded = jnp.where((fold_lane >= n * LEFT) & (fold_lane < (n + 1) * LEFT), moved, folded)
        fresh[slot, FOLD_AT:DIAG_AT, :] = folded

    def begin_half(slot, way, step, half):
        for piece in range(2):
            rows = rows_of(half, piece)
            sums[way, step, rows, :] = fresh[slot, rows, :]
            chain(way, step, half, piece).start()

    def add_half(way, step, half):
        for piece in range(2):
            rows = rows_of(half, piece)
            chain(way, step - 1, half, piece).wait_recv()
            sums[way, step, rows, :] = sums[way, step, rows, :] + fresh[way, rows, :]
            chain(way, step, half, piece).start()

    def ring_item(whole, item, _):
        way, step, first = locate(item)

        @pl.when(item == planes - 1)
        def _():
            prepare(planes - 1, planes)

        block_products(way, first, locate(item + 1)[2], whole)

        @pl.when(item == 0)
        def _():
            begin_half(0, 0, 0, 0)
            begin_half(0, 1, 0, 1)

        @pl.when(step == 1)
        def _():
            begin_half(way, way, step, 1 - way)

        @pl.when((step > 1) & (step < half_ring))
        def _():
            add_half(way, step, 1 - way)

        @pl.when((way == 1) & (step < half_ring))
        def _():
            add_half(0, step, 0)
            add_half(1, step, 1)

        @pl.when(item == 2)
        def _():
            for n in range(len(peers)):
                ask(n).wait_send()
            for port in ports:
                port.finish_sends()
            for single in singles:
                single.finish_served()
                single.finish_sends()

        return 0

    fresh[...] = jnp.zeros_like(fresh)
    squares[...] = jnp.zeros_like(squares)
    ahead = 4
    table_copy.wait()
    ports[0].finish_delivery()
    ports[1].finish_delivery()
    assemble(locate(0)[2], 0, (0, 1))
    lax.fori_loop(0, 2 * ahead, first_half, 0)
    for single in singles:
        single.finish_delivery()
    ports[2].finish_delivery()
    ports[3].finish_delivery()
    assemble(locate(0)[2], 0, (2, 3))
    lax.fori_loop(0, ahead, functools.partial(ring_item, False), 0)
    assemble(locate(ahead)[2], 0, (0, 1, 2, 3))
    lax.fori_loop(ahead, planes, functools.partial(ring_item, True), 0)
    for half in (1, 0):
        for piece in range(2):
            rows = rows_of(half, piece)
            for way in range(2):
                chain(way, half_ring - 1, half, piece).wait_recv()
            arrived = sums[0, half_ring, rows, :] + sums[1, half_ring, rows, :]
            out[rows, :] = arrived + fresh[0, rows, :]
    for n in range(group):
        count = counts[at_z * group + n].astype(jnp.float32)
        out[COUNTS + n : COUNTS + n + 1, :] = jnp.full((1, LANES), count)
    for step in range(half_ring):
        for way in range(2):
            for half in range(2):
                if step or half == way:
                    for piece in range(2):
                        chain(way, step, half, piece).wait_send()


def pair_products(blocks, domains, counts, coeff, planes):
    pair_dev, depth, slots = coeff.shape
    lines = 2 * RING * CORES
    bf16 = jnp.bfloat16
    tile = (MAIN, LANES)
    scratch = []
    for shape in (
        (RING, ATOMS),
        (RING * RING * CORES * ATOMS,),
        (2, ATOMS // 2),
        (RING, CORES, SHARE),
        (2, CORES, HALF_SHARE),
        (RING, SLOTS),
    ):
        scratch += [pltpu.VMEM(shape + tile, bf16)] * 4
    for shape in (
        (ATOMS,),
        (RING - 1, ATOMS),
        (RING, CORES, PICKS),
        (2, CORES, HALF),
        (RING * CORES * PICKS,),
    ):
        scratch += [pltpu.VMEM(shape + tile, bf16)] * 2
    scratch += [
        pltpu.VMEM((lines, 8, LANES), jnp.int32),
        pltpu.SMEM((lines, 8, LANES), jnp.int32),
        pltpu.VMEM((3, 8, LANES), jnp.int32),
        pltpu.SMEM((3, 8, LANES), jnp.int32),
        pltpu.VMEM((8, LANES), jnp.int32),
        pltpu.VMEM((8, LANES), jnp.int32),
        pltpu.VMEM((ATOMS * MAIN, ATOMS * MAIN), bf16),
        pltpu.VMEM((ATOMS * MAIN, ATOMS * MAIN), bf16),
        pltpu.VMEM((pair_dev, depth, slots), bf16),
        pltpu.VMEM((pair_dev, MAXPNO, DEPTH), bf16),
        pltpu.VMEM((DEPTH, depth), bf16),
        pltpu.VMEM((2, DEPTH, blocks.shape[2]), bf16),
        pltpu.VMEM((pair_dev, MAXPNO, MAXPNO), jnp.float32),
        pltpu.VMEM((2, planes // 2 + 1, PACK, LANES), jnp.float32),
        pltpu.VMEM((2, PACK, LANES), jnp.float32),
        pltpu.VMEM((MAXPNO, slots), bf16),
        pltpu.VMEM((2, SQUARE_ROWS, 2 * LANES), jnp.float32),
        pltpu.VMEM(blocks.shape, bf16),
        pltpu.SemaphoreType.DMA((4, 27)),
        pltpu.SemaphoreType.DMA((4, 27)),
        pltpu.SemaphoreType.DMA((2, 16)),
        pltpu.SemaphoreType.DMA((2, 16)),
        pltpu.SemaphoreType.DMA((lines,)),
        pltpu.SemaphoreType.DMA((lines,)),
        pltpu.SemaphoreType.DMA((8,)),
        pltpu.SemaphoreType.DMA((2 * planes, 2)),
        pltpu.SemaphoreType.DMA((2 * planes, 2)),
    ]
    return pl.pallas_call(
        main_kernel,
        out_shape=pltpu.VMEM((PACK, LANES), jnp.float32),
        in_specs=[
            pl.BlockSpec(memory_space=pl.ANY),
            pl.BlockSpec(memory_space=pltpu.SMEM),
            pl.BlockSpec(memory_space=pltpu.SMEM),
            pl.BlockSpec(memory_space=pl.ANY),
        ],
        out_specs=pl.BlockSpec(memory_space=pltpu.VMEM),
        scratch_shapes=scratch,
        compiler_params=params(60, collective_id=0, has_side_effects=True),
    )(blocks, domains, counts, coeff)


def tail_kernel(packed, amp, energy_row, energy_col, out, wide):
    slots = amp.shape[1]
    step = pl.program_id(0)
    full_row = lax.broadcasted_iota(jnp.int32, (slots, slots), 0)
    full_col = lax.broadcasted_iota(jnp.int32, (slots, slots), 1)
    lane = lax.broadcasted_iota(jnp.int32, (MAXPNO, LANES), 1)
    fold_lane = lax.broadcasted_iota(jnp.int32, (FOLD_ROWS, LANES), 1)
    wide[MAXPNO:, :] = jnp.zeros((slots - MAXPNO, slots), jnp.float32)

    def shared_at(begin, end):
        if end <= TOP:
            return packed[MAXPNO + begin : MAXPNO + end, :]
        return packed[HALF_PACK + MAXPNO + begin - TOP : HALF_PACK + MAXPNO + end - TOP, :]

    @pl.when(step == 0)
    def _():
        wide[:MAXPNO, :LANES] = packed[:MAXPNO, :]
        for begin, end in ((0, TOP), (TOP, MAXPNO)):
            wide[begin:end, LANES:] = jnp.where(lane[begin:end] < REST, shared_at(begin, end), 0.0)

    @pl.when(step == 1)
    def _():
        wide[:MAXPNO, :LANES] = packed[HALF_PACK : HALF_PACK + MAXPNO, :]
        for begin, end in ((0, TOP), (TOP, MAXPNO)):
            turned = pltpu.roll(shared_at(begin, end), SPARE, 1)
            wide[begin:end, LANES:] = jnp.where(lane[begin:end] < SPARE, turned, 0.0)
        folded = packed[FOLD_AT:DIAG_AT, :]
        for n in range(SQUARE_ROWS // FOLD_ROWS):
            begin, end = n * FOLD_ROWS, min((n + 1) * FOLD_ROWS, MAXPNO)
            moved = pltpu.roll(folded, (SPARE - n * LEFT) % LANES, 1)
            left = (fold_lane >= SPARE) & (fold_lane < REST)
            held = wide[begin:end, LANES:]
            wide[begin:end, LANES:] = jnp.where(left[: end - begin], moved[: end - begin], held)

    square = wide[...]
    at = DIAG_AT + 2 * step
    diagonal = jnp.concatenate([packed[pl.ds(at, 1), :], packed[pl.ds(at + 1, 1), :]], axis=1)
    on_diagonal = full_row == full_col
    for n in range(2):
        count = packed[pl.ds(COUNTS + 2 * step + n, 1), :][:, :1].astype(jnp.int32)
        row, col = full_row[:MAXPNO], full_col[:MAXPNO]
        if n == 0:
            held = jnp.where(full_row >= full_col, square, 0.0)
        else:
            held = jnp.where(full_row < full_col, square, jnp.where(on_diagonal, diagonal, 0.0))
        products = held[:MAXPNO] + jnp.where(row == col, 0.0, held.T[:MAXPNO])
        valid = (row < count) & (col < count)
        products = jnp.where(valid, products / NAUX, 0.0)
        amps = amp[n]
        contract = (((1,), (1,)), ((), ()))
        high = products.astype(jnp.bfloat16)
        left = products - high.astype(jnp.float32)
        mid = left.astype(jnp.bfloat16)
        low = (left - mid.astype(jnp.float32)).astype(jnp.bfloat16)
        coupled = lax.dot_general(low, amps, contract, preferred_element_type=jnp.float32)
        coupled += lax.dot_general(mid, amps, contract, preferred_element_type=jnp.float32)
        coupled += lax.dot_general(high, amps, contract, preferred_element_type=jnp.float32)
        energies = energy_col[n, :MAXPNO] + energy_row[pl.ds(2 * step + n, 1), :]
        result = products + coupled + energies * amps[:MAXPNO].astype(jnp.float32)
        out[n, :MAXPNO] = jnp.where(valid, result, 0.0)
        out[n, MAXPNO:] = jnp.zeros((slots - MAXPNO, slots), jnp.float32)


def tail(packed, amp, energy):
    subs, slots, _ = amp.shape
    return pl.pallas_call(
        tail_kernel,
        out_shape=jax.ShapeDtypeStruct((subs, slots, slots), jnp.float32),
        grid=(subs // 2,),
        in_specs=[
            pl.BlockSpec((PACK, LANES), lambda i: (0, 0)),
            pl.BlockSpec((2, slots, slots), lambda i: (i, 0, 0)),
            pl.BlockSpec((subs, slots), lambda i: (0, 0)),
            pl.BlockSpec((2, slots, 1), lambda i: (i, 0, 0)),
        ],
        out_specs=pl.BlockSpec((2, slots, slots), lambda i: (i, 0, 0)),
        scratch_shapes=[pltpu.VMEM((slots, slots), jnp.float32)],
        compiler_params=params(32),
    )(packed, amp, energy, energy[:, :, None])


def on_device(atom_blocks, domains, pno_counts, pno_coeffs, amplitudes, pno_energies):
    planes = lax.axis_size("ri")
    mine = pair_products(atom_blocks.transpose(1, 0, 2), domains.T, pno_counts, pno_coeffs, planes)
    return tail(mine, amplitudes, pno_energies)


def solution(mesh):
    placed = (
        P("pairs", None, "ri"),
        P("pairs", None),
        P("pairs"),
        P("pairs", None, None),
        P(("pairs", "ri"), None, None),
        P(("pairs", "ri"), None),
    )
    return jax.shard_map(
        on_device,
        mesh=mesh,
        in_specs=placed,
        out_specs=P(("pairs", "ri"), None, None),
        check_vma=False,
    )
```

```python
import functools

import jax
import jax.numpy as jnp
from jax import lax
from jax.experimental import pallas as pl
from jax.experimental.pallas import tpu as pltpu
from jax.sharding import PartitionSpec as P

NAUX = 14336
CAP = 3
MAXPNO = 200
MAIN = 16
REM = 4
SPLIT = 128
REST = MAXPNO - SPLIT
LANES = 128
MIB = 1 << 20
RING = 4
CORES = 2
ATOMS = 16
DOM = 12
BAND = MAIN + REM
PICKS = RING * CAP
HALF = PICKS // 2
DEPTH = 256
SPARE = LANES - REST
LEFT = REST - SPARE
FOLD_ROWS = 32
HALF_PACK = 320
PACK = 2 * HALF_PACK
TOP = HALF_PACK - MAXPNO
FOLD_AT = PACK - FOLD_ROWS - 8
DIAG_AT = PACK - 8
COUNTS = PACK - 4
SQUARE_ROWS = 224
SLOTS = 48
SHARE = SLOTS // CORES
HALF_SHARE = SHARE // 2
ROW_LINES = RING * CORES
MAINS = ((0, 1, 2), (3, 4, 5), (6, 7, 8), (10, 11, 12))
RESTS = ((0, 1, 2), (3, 4, 5), (6, 7, 8, 9), (10, 11, 12, 13))
SINGLES = (9, 13)
MESH = pl.DeviceIdType.MESH


def params(mib, **kw):
    return pltpu.CompilerParams(vmem_limit_bytes=mib * MIB, **kw)


class Ports:
    def __init__(self, chunk, gather_to, deliver_to, wire, ring, send, relay, recv, out_sems, in_sems, core):
        self.gather_to, self.deliver_to, self.core = gather_to, deliver_to, core
        self.wire, self.ring, self.send, self.relay, self.recv = wire, ring, send, relay, recv
        self.out_sems, self.in_sems, self.chunk = out_sems, in_sems, chunk

    def copy(self, src, dst, out_at, in_at, to):
        return pltpu.make_async_remote_copy(
            src_ref=src,
            dst_ref=dst,
            send_sem=self.out_sems.at[self.chunk, out_at],
            recv_sem=self.in_sems.at[self.chunk, in_at],
            device_id={"pairs": to},
            device_id_type=MESH,
        )

    def gather_first(self):
        up = self.copy(self.wire, self.ring.at[2], 0, 1, self.gather_to(1, self.core))
        down = self.copy(self.wire, self.ring.at[0], 1, 0, self.gather_to(3, self.core))
        return up, down

    def gather_second(self):
        half = ATOMS // 2
        low, high = pl.ds(0, half), pl.ds(half, half)
        up = self.copy(self.ring.at[2, low], self.ring.at[1, low], 2, 2, self.gather_to(1, self.core))
        down = self.copy(self.ring.at[0, high], self.ring.at[1, high], 3, 3, self.gather_to(3, self.core))
        return up, down

    def place(self, rel, core):
        return (rel * CORES + core) * PICKS

    def far(self):
        up = self.copy(self.send.at[2, :, pl.ds(0, HALF)], self.relay.at[0], 4, 4, self.deliver_to(1, self.core))
        down = self.copy(self.send.at[2, :, pl.ds(HALF, HALF)], self.relay.at[1], 5, 5, self.deliver_to(3, self.core))
        return up, down

    def near(self):
        copies = []
        for n, step in enumerate((1, 3)):
            for core in range(CORES):
                dst = self.recv.at[pl.ds(self.place(RING - step, self.core), PICKS)]
                at = 6 + 2 * n
                copies.append(self.copy(self.send.at[step, core], dst, at + core, at + self.core, self.deliver_to(step, core)))
        other = 1 - self.core
        dst = self.recv.at[pl.ds(self.place(0, self.core), PICKS)]
        copies.append(self.copy(self.send.at[0, other], dst, 10, 10, self.deliver_to(0, other)))
        return copies

    def own(self):
        return pltpu.make_async_copy(
            self.send.at[0, self.core],
            self.recv.at[pl.ds(self.place(0, self.core), PICKS)],
            self.in_sems.at[self.chunk, 11],
        )

    def onward(self):
        copies = []
        for way, step in enumerate((1, 3)):
            for core in range(CORES):
                dst = self.recv.at[pl.ds(self.place(2, self.core) + way * HALF, HALF)]
                at = 12 + 2 * way
                copies.append(self.copy(self.relay.at[way, core], dst, at + core, at + self.core, self.deliver_to(step, core)))
        return copies

    def start_gather(self):
        for copy in self.gather_first():
            copy.start()

    def forward_gather(self):
        up, down = self.gather_second()
        first_up, first_down = self.gather_first()
        first_up.wait_recv()
        up.start()
        first_down.wait_recv()
        down.start()

    def finish_gather(self):
        for copy in self.gather_second():
            copy.wait_recv()

    def start_far(self):
        for copy in self.far():
            copy.start()

    def start_near(self):
        for copy in self.near():
            copy.start()
        self.own().start()

    def forward_delivery(self):
        far, onward = self.far(), self.onward()
        for way in range(2):
            far[way].wait_recv()
            for copy in onward[2 * way : 2 * way + 2]:
                copy.start()

    def finish_delivery(self):
        for n, step in enumerate((1, 3)):
            for core in range(CORES):
                dst = self.recv.at[pl.ds(self.place(step, core), PICKS)]
                at = 6 + 2 * (1 - n)
                self.copy(dst, dst, at + core, at + core, self.deliver_to(1, self.core)).wait_recv()
        other = 1 - self.core
        dst = self.recv.at[pl.ds(self.place(0, other), PICKS)]
        self.copy(dst, dst, 10, 10, self.deliver_to(1, self.core)).wait_recv()
        self.own().wait()
        for way in range(2):
            for core in range(CORES):
                dst = self.recv.at[pl.ds(self.place(2, core) + way * HALF, HALF)]
                at = 12 + 2 * way
                self.copy(dst, dst, at + core, at + core, self.deliver_to(1, self.core)).wait_recv()

    def finish_served(self):
        for copy in self.far() + tuple(self.near()):
            copy.wait_send()

    def finish_sends(self):
        for copy in self.gather_first() + self.gather_second() + tuple(self.onward()):
            copy.wait_send()


class Relay:
    def __init__(self, chunk, first_to, other_to, u, v, core, bufs, out_sems, in_sems):
        self.chunk, self.first_to, self.other_to = chunk, first_to, other_to
        self.u, self.v, self.core = u, v, core
        self.wire, self.table, self.passing, self.send, self.relay, self.recv = bufs
        self.out_sems, self.in_sems = out_sems, in_sems

    def copy(self, src, dst, out_at, in_at, to):
        return pltpu.make_async_remote_copy(
            src_ref=src,
            dst_ref=dst,
            send_sem=self.out_sems.at[self.chunk, out_at],
            recv_sem=self.in_sems.at[self.chunk, in_at],
            device_id={"pairs": to},
            device_id_type=MESH,
        )

    def arrival(self, dst, at):
        return self.copy(dst, dst, at, at, self.first_to(1, self.core))

    def near_u(self, step):
        return lax.rem(self.u + step, RING)

    def near_v(self, step):
        return lax.rem(self.v + step, RING)

    def atoms(self, step, at=0, count=ATOMS):
        base = ((self.v * CORES + self.core) * RING + self.near_u(step)) * ATOMS
        return self.table.at[pl.ds(base + at, count)]

    def block(self, step, core, at=0, count=RING * ATOMS):
        return self.table.at[pl.ds((self.near_v(step) * CORES + core) * RING * ATOMS + at, count)]

    def spread_sends(self):
        half = ATOMS // 2
        far = self.near_u(2)
        up, down = self.first_to(1, self.core), self.first_to(3, self.core)
        return [
            self.copy(self.wire.at[far, pl.ds(0, half)], self.passing.at[0], 2, 2, up),
            self.copy(self.wire.at[far, pl.ds(half, half)], self.passing.at[1], 3, 3, down),
            self.copy(self.wire.at[self.near_u(1)], self.atoms(0), 0, 1, up),
            self.copy(self.wire.at[self.near_u(3)], self.atoms(0), 1, 0, down),
        ]

    def spread_own(self):
        return pltpu.make_async_copy(self.wire.at[self.u], self.atoms(0), self.in_sems.at[self.chunk, 25])

    def spread_onward(self):
        half = ATOMS // 2
        return [
            self.copy(self.passing.at[0], self.atoms(3, 0, half), 4, 4, self.first_to(1, self.core)),
            self.copy(self.passing.at[1], self.atoms(1, half, half), 5, 5, self.first_to(3, self.core)),
        ]

    def start_spread(self):
        for copy in self.spread_sends():
            copy.start()
        self.spread_own().start()

    def forward_spread(self):
        for way, copy in enumerate(self.spread_onward()):
            self.arrival(self.passing.at[way], 2 + way).wait_recv()
            copy.start()

    def finish_spread(self):
        half = ATOMS // 2
        self.spread_own().wait()
        self.arrival(self.atoms(1), 0).wait_recv()
        self.arrival(self.atoms(3), 1).wait_recv()
        self.arrival(self.atoms(2, 0, half), 4).wait_recv()
        self.arrival(self.atoms(2, half, half), 5).wait_recv()

    def gather_first(self):
        own = self.block(0, self.core)
        return [
            self.copy(own, own, 6, 7, self.other_to(1, self.core)),
            self.copy(own, own, 7, 6, self.other_to(3, self.core)),
        ]

    def gather_second(self):
        half = RING * ATOMS // 2
        low, high = self.block(3, self.core, 0, half), self.block(1, self.core, half, half)
        return [
            self.copy(low, low, 8, 8, self.other_to(1, self.core)),
            self.copy(high, high, 9, 9, self.other_to(3, self.core)),
        ]

    def share(self, step):
        mine = self.block(step, self.core)
        return self.copy(mine, mine, 10 + step, 10 + step, self.first_to(0, 1 - self.core))

    def start_gather(self):
        for copy in self.gather_first():
            copy.start()
        self.share(0).start()

    def forward_gather(self):
        low, high = self.gather_second()
        self.arrival(self.block(3, self.core), 7).wait_recv()
        low.start()
        self.share(3).start()
        self.arrival(self.block(1, self.core), 6).wait_recv()
        high.start()
        self.share(1).start()

    def finish_gather(self):
        half = RING * ATOMS // 2
        self.arrival(self.block(2, self.core, 0, half), 8).wait_recv()
        self.arrival(self.block(2, self.core, half, half), 9).wait_recv()
        self.share(2).start()

    def finish_share(self):
        for step in range(RING):
            self.arrival(self.block(step, 1 - self.core), 10 + step).wait_recv()

    def place(self, step, core, at=0, count=SHARE):
        return self.recv.at[self.near_u(step), pl.ds(core * SHARE + at, count)]

    def far(self):
        return [
            self.copy(self.send.at[2, :, pl.ds(0, HALF_SHARE)], self.relay.at[0], 19, 19, self.first_to(1, self.core)),
            self.copy(
                self.send.at[2, :, pl.ds(HALF_SHARE, HALF_SHARE)], self.relay.at[1], 20, 20, self.first_to(3, self.core)
            ),
        ]

    def near(self):
        copies = []
        dst = self.place(0, self.core)
        for n, step in enumerate((1, 3)):
            for core in range(CORES):
                at = 14 + 2 * n
                copies.append(self.copy(self.send.at[step, core], dst, at + core, at + self.core, self.first_to(step, core)))
        other = 1 - self.core
        copies.append(self.copy(self.send.at[0, other], dst, 18, 18, self.first_to(0, other)))
        return copies

    def own(self):
        return pltpu.make_async_copy(
            self.send.at[0, self.core], self.place(0, self.core), self.in_sems.at[self.chunk, 26]
        )

    def onward(self):
        copies = []
        for way, step in enumerate((1, 3)):
            dst = self.place(RING - step, self.core, way * HALF_SHARE, HALF_SHARE)
            for core in range(CORES):
                at = 21 + 2 * way
                copies.append(self.copy(self.relay.at[way, core], dst, at + core, at + self.core, self.first_to(step, core)))
        return copies

    def start_far(self):
        for copy in self.far():
            copy.start()

    def start_near(self):
        for copy in self.near():
            copy.start()
        self.own().start()

    def forward_delivery(self):
        onward = self.onward()
        for way in range(2):
            self.arrival(self.relay.at[way], 19 + way).wait_recv()
            for copy in onward[2 * way : 2 * way + 2]:
                copy.start()

    def finish_delivery(self):
        for core in range(CORES):
            self.arrival(self.place(3, core), 14 + core).wait_recv()
            self.arrival(self.place(1, core), 16 + core).wait_recv()
            for way in range(2):
                at = 21 + 2 * way + core
                self.arrival(self.place(2, core, way * HALF_SHARE, HALF_SHARE), at).wait_recv()
        self.arrival(self.place(0, 1 - self.core), 18).wait_recv()
        self.own().wait()

    def finish_sends(self):
        copies = self.spread_sends() + self.spread_onward() + self.gather_first() + self.gather_second()
        copies += [self.share(step) for step in range(RING)] + self.far() + self.near() + self.onward()
        for copy in copies:
            copy.wait_send()


def main_kernel(
    blocks_hbm, domains, counts, coeff_hbm, out, *scratch
):
    relay_bufs = [scratch[4 * n : 4 * n + 4] for n in range(6)]
    single_bufs = [scratch[24 + 2 * n : 26 + 2 * n] for n in range(5)]
    wires, recvs = relay_bufs[0], relay_bufs[5]
    single_wires, single_recvs = single_bufs[0], single_bufs[4]
    asked, asked_smem, tables, places, request, ids, perm_main, perm_rest = scratch[34:42]
    coeff, coeff_t, perm, blk, total, sums, fresh, same, squares, blocks = scratch[42:52]
    out_sems, in_sems, single_out, single_in, ask_out, ask_in, local_sems, sum_out, sum_in = scratch[52:61]
    me = lax.axis_index("pairs")
    at_z = lax.axis_index("ri")
    planes = 2 * (sums.shape[1] - 1)
    above, below = lax.rem(at_z + 1, planes), lax.rem(at_z + planes - 1, planes)
    core = lax.rem(me, CORES)
    chip = lax.div(me, CORES)
    at_x = lax.rem(chip, RING)
    at_y = lax.div(chip, RING)

    def along_x(step, to_core):
        return (at_y * RING + lax.rem(at_x + step, RING)) * CORES + to_core

    def along_y(step, to_core):
        return (lax.rem(at_y + step, RING) * RING + at_x) * CORES + to_core

    peers = []
    for to_core in range(2):
        for step in range(1, RING):
            peers.append((along_y(step, to_core), step * CORES + to_core, (RING - step) * CORES + core))
            peers.append(
                (along_x(step, to_core), (RING + step) * CORES + to_core, (2 * RING - step) * CORES + core)
            )
    peers.append((along_x(0, 1 - core), 1 - core, core))

    barrier = pltpu.get_barrier_semaphore()
    for peer, _, _ in peers:
        pl.semaphore_signal(barrier, inc=1, device_id={"pairs": peer}, device_id_type=MESH)
    for plane in (above, below):
        pl.semaphore_signal(barrier, inc=1, device_id={"ri": plane}, device_id_type=MESH)

    def ask(n):
        peer, _, there = peers[n]
        return pltpu.make_async_remote_copy(
            src_ref=request,
            dst_ref=asked.at[there],
            send_sem=ask_out.at[n],
            recv_sem=ask_in.at[there],
            device_id={"pairs": peer},
            device_id_type=MESH,
        )

    ports = []
    for chunk in range(4):
        by_x = chunk % 2 == 0
        first_to, other_to = (along_x, along_y) if by_x else (along_y, along_x)
        u, v = (at_x, at_y) if by_x else (at_y, at_x)
        bufs = [group_bufs[chunk] for group_bufs in relay_bufs]
        ports.append(Relay(chunk, first_to, other_to, u, v, core, bufs, out_sems, in_sems))
    singles = []
    for n in range(2):
        gather_to, deliver_to = (along_x, along_y) if n == 0 else (along_y, along_x)
        bufs = [group_bufs[n] for group_bufs in single_bufs]
        singles.append(Ports(n, gather_to, deliver_to, *bufs, single_out, single_in, core))

    fetches = []
    for chunk in range(4):
        tiles = RESTS[chunk]
        cols = pl.ds(tiles[0] * LANES, len(tiles) * LANES)
        fetches.append(
            pltpu.make_async_copy(blocks_hbm.at[:, :, cols], blocks.at[:, :, cols], local_sems.at[4 + chunk])
        )
        fetches[chunk].start()
    fetch = pltpu.make_async_copy(coeff_hbm, coeff, local_sems.at[0])
    fetch.start()

    square = (ATOMS * MAIN, ATOMS * MAIN)
    out_at = lax.broadcasted_iota(jnp.int32, square, 0)
    from_at = lax.broadcasted_iota(jnp.int32, square, 1)
    band_at, atom_at = out_at & (MAIN - 1), lax.shift_right_logical(out_at, 4)
    perm_main[...] = jnp.where(band_at * ATOMS + atom_at == from_at, 1.0, 0.0).astype(jnp.bfloat16)
    rest_at = lax.shift_right_logical(band_at, 2) * (REM * ATOMS) + (band_at & (REM - 1)) * ATOMS + atom_at
    perm_rest[...] = jnp.where(rest_at == from_at, 1.0, 0.0).astype(jnp.bfloat16)

    def main_rows(tiles):
        flat = blocks[:MAIN, :, tiles[0] * LANES : (tiles[-1] + 1) * LANES]
        flat = flat.reshape(MAIN * ATOMS, len(tiles) * LANES)
        return jnp.dot(perm_main[...], flat, preferred_element_type=jnp.float32).astype(jnp.bfloat16)

    def form(chunk):
        fetches[chunk].wait()
        main = main_rows(MAINS[chunk])
        for n in range(len(MAINS[chunk])):
            wires[chunk][n] = main[:, n * LANES : (n + 1) * LANES].reshape(ATOMS, MAIN, LANES)
        parts = [blocks[MAIN:, :, t * LANES : (t + 1) * LANES].reshape(REM * ATOMS, LANES) for t in RESTS[chunk]]
        stacked = jnp.concatenate(parts, axis=0)
        depth = stacked.shape[0]
        late = jnp.dot(perm_rest[:, :depth], stacked, preferred_element_type=jnp.float32).astype(jnp.bfloat16)
        wires[chunk][RING - 1] = late.reshape(ATOMS, MAIN, LANES)

    form(0)
    pl.semaphore_wait(barrier, len(peers) + 2)
    ports[0].start_spread()
    for chunk in range(1, 4):
        form(chunk)
        ports[chunk].start_spread()
    for n in range(2):
        single_wires[n][...] = main_rows(SINGLES[n : n + 1]).reshape(ATOMS, MAIN, LANES)
    for chunk in (0, 1):
        ports[chunk].forward_spread()
    for chunk in (0, 1):
        ports[chunk].finish_spread()
        ports[chunk].start_gather()

    for chunk in (2, 3):
        ports[chunk].forward_spread()

    def parts_of(atom):
        owner = lax.shift_right_logical(atom, 4)
        chip = lax.shift_right_logical(owner, 1)
        return owner, owner & (CORES - 1), chip & (RING - 1), lax.shift_right_logical(chip, 2), atom & (ATOMS - 1)

    map_shape = (8, LANES)
    map_row = lax.broadcasted_iota(jnp.int32, map_shape, 0)
    map_lane = lax.broadcasted_iota(jnp.int32, map_shape, 1)
    atom_map = map_row * LANES + map_lane
    pairs = domains.shape[1]

    def mark(pair, seen):
        for k in range(DOM):
            seen = jnp.where(atom_map == domains[k, pair], 1, seen)
        return seen

    named = lax.fori_loop(0, pairs, mark, jnp.zeros(map_shape, jnp.int32))
    owner, owner_core, owner_x, owner_y, local = parts_of(atom_map)
    rank = named
    for shift in (1, 2, 4, 8):
        rank = rank + jnp.where(local >= shift, pltpu.roll(rank, shift, 1), 0)
    order = named
    for shift in (1, 2, 4, 8, 16, 32, 64):
        order = order + jnp.where(map_lane >= shift, pltpu.roll(order, shift, 1), 0)
    counted = order
    map_rows = ATOMS * RING * RING * CORES // LANES
    for n in range(map_rows - 1):
        order = order + jnp.where(map_row > n, counted[n : n + 1, LANES - 1 :], 0)
    rel_x = (owner_x + RING - at_x) & (RING - 1)
    rel_y = (owner_y + RING - at_y) & (RING - 1)
    tables[0] = order - 1
    tables[1] = ((rel_y * CORES + owner_core) * RING + rel_x) * CAP + rank - 1
    tables[2] = ((rel_x * CORES + owner_core) * RING + rel_y) * CAP + rank - 1
    table_copy = pltpu.make_async_copy(tables, places, local_sems.at[3])
    table_copy.start()

    ids[:map_rows, :] = jnp.where(named > 0, order, 0)[:map_rows]
    ids[map_rows:, :] = jnp.where(named > 0, rank, 0)[:map_rows]
    upright = ids[...].T
    list_shape = (LANES, LANES)
    list_row = lax.broadcasted_iota(jnp.int32, list_shape, 0)
    list_lane = lax.broadcasted_iota(jnp.int32, list_shape, 1)
    rows = [jnp.zeros((1, LANES), jnp.int32) for _ in range(CAP + 2)]
    for n in range(map_rows):
        owner, owner_core, owner_x, owner_y, local = parts_of(list_row + n * LANES)
        own_lane = jnp.where(owner == list_lane, local, 0)
        order_at = jnp.broadcast_to(upright[:, n : n + 1], list_shape)
        rank_at = jnp.broadcast_to(upright[:, map_rows + n : map_rows + n + 1], list_shape)
        for j in range(CAP):
            rows[j] += jnp.sum(jnp.where(rank_at == j + 1, own_lane, 0), axis=0, keepdims=True)
        for j, (u, v) in enumerate(((owner_x, owner_y), (owner_y, owner_x))):
            held_at = ((v * CORES + owner_core) * RING + u) * ATOMS + local
            rows[CAP + j] += jnp.sum(jnp.where(order_at == list_lane + 1, held_at, 0), axis=0, keepdims=True)
    for n in range(CAP + 2):
        request[n : n + 1, :] = rows[n]
    request[CAP + 2 :, :] = jnp.zeros((6 - CAP, LANES), jnp.int32)

    for n in range(len(peers)):
        ask(n).start()
    own_ask = pltpu.make_async_copy(request, asked.at[core], local_sems.at[1])
    own_ask.start()
    for chunk in (2, 3):
        ports[chunk].finish_spread()

    shape = (DEPTH, DOM * BAND)
    row = lax.broadcasted_iota(jnp.int32, shape, 0)
    col = lax.broadcasted_iota(jnp.int32, shape, 1)
    split = DOM * MAIN
    late = row - split
    source = jnp.where(
        row < split,
        lax.shift_right_logical(row, 4) * BAND + (row & (MAIN - 1)),
        lax.shift_right_arithmetic(late, 2) * BAND + MAIN + (late & (REM - 1)),
    )
    perm[...] = jnp.where((source == col) & (row < DOM * BAND), 1.0, 0.0).astype(jnp.bfloat16)
    same[...] = jnp.where(
        lax.broadcasted_iota(jnp.int32, same.shape, 0) == lax.broadcasted_iota(jnp.int32, same.shape, 1), 1.0, 0.0
    ).astype(jnp.bfloat16)
    for n in range(2):
        blk[n, DOM * BAND :, :] = jnp.zeros((DEPTH - DOM * BAND, blk.shape[2]), jnp.bfloat16)
    fetch.wait()

    def prepare(begin, end):
        def turn(pair, _):
            ordered = [
                jnp.dot(perm[...], coeff[4 * pair + n], preferred_element_type=jnp.float32).astype(jnp.bfloat16)
                for n in range(4)
            ]
            for n in range(4):
                turned = lax.dot_general(
                    same[...], ordered[n], (((1,), (1,)), ((), ())), preferred_element_type=jnp.float32
                )
                coeff_t[4 * pair + n] = turned.astype(jnp.bfloat16)
            return 0

        lax.fori_loop(begin // 4, end // 4, turn, 0)

    prepare(0, 4)
    for chunk in (0, 1):
        ports[chunk].forward_gather()
    for chunk in (2, 3):
        ports[chunk].start_gather()

    for single in singles:
        single.start_gather()
    prepare(4, 12)

    own_ask.wait()
    for n in range(len(peers)):
        _, here, _ = peers[n]
        pltpu.make_async_remote_copy(
            src_ref=request,
            dst_ref=asked.at[here],
            send_sem=ask_out.at[n],
            recv_sem=ask_in.at[here],
            device_id={"pairs": peers[n][0]},
            device_id_type=MESH,
        ).wait_recv()
    to_smem = pltpu.make_async_copy(asked, asked_smem, local_sems.at[2])
    to_smem.start()
    to_smem.wait()

    def line_of(dest, on_row):
        return jnp.where(dest < CORES, dest, dest + ROW_LINES) if on_row else dest

    def pick_single(n):
        port = singles[n]
        owner_of = along_x if n == 0 else along_y

        def serve(dest, _):
            line = line_of(dest, n == 1)
            step, to_core = dest // CORES, dest % CORES
            for r in range(RING):
                for j in range(CAP):
                    atom = asked_smem[line, j, owner_of(r, core)]
                    found = port.wire[atom] if r == 0 else port.ring[r - 1, atom]
                    port.send[step, to_core, r * CAP + j] = found
            return 0

        lax.fori_loop(2 * CORES, 3 * CORES, serve, 0)
        port.start_far()

        def serve_near(dest, _):
            return serve(jnp.where(dest < 2 * CORES, dest, dest + CORES), 0)

        lax.fori_loop(0, 3 * CORES, serve_near, 0)
        port.start_near()

    def pick(chunk):
        port = ports[chunk]

        def serve(dest, _):
            line = line_of(dest, chunk % 2 == 0)
            step, to_core = dest // CORES, dest % CORES
            for n in range(SHARE):
                port.send[step, to_core, n] = port.table[asked_smem[line, CAP + chunk % 2, core * SHARE + n]]
            return 0

        lax.fori_loop(2 * CORES, 3 * CORES, serve, 0)
        port.start_far()

        def serve_near(dest, _):
            return serve(jnp.where(dest < 2 * CORES, dest, dest + CORES), 0)

        lax.fori_loop(0, 3 * CORES, serve_near, 0)
        port.start_near()

    for chunk in (0, 1):
        ports[chunk].finish_gather()
    for chunk in (0, 1):
        ports[chunk].finish_share()
        pick(chunk)
    for chunk in (2, 3):
        ports[chunk].forward_gather()
    for single in singles:
        single.forward_gather()
    prepare(12, 20)
    for chunk in (0, 1):
        ports[chunk].forward_delivery()
    prepare(20, 24)
    for chunk in (2, 3):
        ports[chunk].finish_gather()
    for n in range(2):
        singles[n].finish_gather()
        pick_single(n)
    for chunk in (2, 3):
        ports[chunk].finish_share()
        pick(chunk)
    prepare(24, 32)
    for single in singles:
        single.forward_delivery()
    for chunk in (2, 3):
        ports[chunk].forward_delivery()

    pack_row = lax.broadcasted_iota(jnp.int32, (MAXPNO, MAXPNO), 0)
    pack_col = lax.broadcasted_iota(jnp.int32, (MAXPNO, MAXPNO), 1)
    pack_lane = lax.broadcasted_iota(jnp.int32, (MAXPNO, LANES), 1)
    fold_lane = lax.broadcasted_iota(jnp.int32, (FOLD_ROWS, LANES), 1)

    def assemble(pair, slot, chunks):
        base = MAIN * DOM
        begin = 0
        upper = lax.broadcasted_iota(jnp.int32, (8, LANES), 0) < REM

        names = [domains[k, pair] for k in range(DOM)]

        def named_at(table):
            return [places[table, lax.shift_right_logical(a, 7), a & (LANES - 1)] for a in names]

        at = named_at(0)
        for chunk in chunks:
            tiles = len(RESTS[chunk])
            for n in range(RING - 1):
                span = slice(begin + n * LANES, begin + (n + 1) * LANES)
                for k in range(DOM):
                    blk[slot, MAIN * k : MAIN * (k + 1), span] = recvs[chunk][n, at[k]]
            if tiles == RING:
                span = slice(begin + (RING - 1) * LANES, begin + RING * LANES)
                single_at = named_at(1 + chunk % 2)
                for k in range(DOM):
                    blk[slot, MAIN * k : MAIN * (k + 1), span] = single_recvs[chunk % 2][single_at[k]]
            for k in range(0, DOM, 4):
                rest = [recvs[chunk][RING - 1, at[k + n]].astype(jnp.float32) for n in range(4)]
                for half in range((tiles + 1) // 2):
                    parts = [r[8 * half : 8 * half + 8] for r in rest]
                    shifted = [pltpu.roll(part, REM, 0) for part in parts]
                    for q in range(2 * half, min(2 * half + 2, tiles)):
                        first, second = (parts, shifted) if q % 2 == 0 else (shifted, parts)
                        low = jnp.where(upper, first[0], second[1])
                        high = jnp.where(upper, first[2], second[3])
                        both = jnp.concatenate([low, high], axis=0).astype(jnp.bfloat16)
                        tile = slice(begin + q * LANES, begin + (q + 1) * LANES)
                        blk[slot, base + REM * k : base + REM * (k + 4), tile] = both
            begin += tiles * LANES
        return begin

    def multiply(pair, slot, cols):
        weights = coeff_t[pair]
        vecs = []
        for at in range(0, cols, 256):
            vec = jnp.dot(weights, blk[slot, :, at : at + 256], preferred_element_type=jnp.float32)
            vecs.append(vec.astype(jnp.bfloat16))
        vecs = jnp.concatenate(vecs, axis=1)
        return lax.dot_general(vecs, vecs, (((1,), (1,)), ((), ())), preferred_element_type=jnp.float32)

    early_cols = LANES * (len(RESTS[0]) + len(RESTS[1]))
    late_cols = LANES * (len(RESTS[2]) + len(RESTS[3]))
    group = coeff.shape[0] // planes
    half_ring = planes // 2
    part = HALF_PACK // 2

    def rows_of(half, piece):
        return pl.ds(pl.multiple_of(half * HALF_PACK + piece * part, 8), part)

    def chain(way, step, half, piece):
        rows = rows_of(half, piece)
        return pltpu.make_async_remote_copy(
            src_ref=sums.at[way, step, rows],
            dst_ref=sums.at[way, step + 1, rows],
            send_sem=sum_out.at[(way * half_ring + step) * 2 + half, piece],
            recv_sem=sum_in.at[(way * half_ring + step) * 2 + half, piece],
            device_id={"ri": jnp.where(way == 0, above, below)},
            device_id_type=MESH,
        )

    def locate(item):
        step = (item + 1) // 2
        way = jnp.where(item == 0, 0, (item + 1) % 2)
        away = jnp.where(way == 0, half_ring - step, half_ring + step)
        return way, step, lax.rem(at_z + away, planes) * group

    def first_half(step, _):
        pair = locate(step // 2)[2] + 2 * (step % 2)
        following = locate((step + 1) // 2)[2] + 2 * ((step + 1) % 2)
        assemble(pair + 1, 1, (0, 1))
        total[pair] = multiply(pair, 0, early_cols)
        assemble(following, 0, (0, 1))
        total[pair + 1] = multiply(pair + 1, 1, early_cols)
        return 0

    def block_products(slot, first, following, whole):
        chunks = (0, 1, 2, 3) if whole else (2, 3)
        cols = early_cols + late_cols if whole else late_cols

        def one(duo, _):
            pair = first + 2 * duo
            assemble(pair + 1, 1, chunks)
            here = multiply(pair, 0, cols)
            assemble(jnp.where(duo == 0, pair + 2, following), 0, chunks)
            there = multiply(pair + 1, 1, cols)
            if not whole:
                here += total[pair]
                there += total[pair + 1]
            squares[duo, :MAXPNO, :MAXPNO] = jnp.where(pack_row >= pack_col, here, there)
            diagonal = jnp.sum(jnp.where(pack_row == pack_col, there, 0.0), axis=0, keepdims=True)
            at = DIAG_AT + 2 * duo
            fresh[slot, pl.ds(at, 1), :] = diagonal[:, :LANES]
            fresh[slot, pl.ds(at + 1, 1), :REST] = diagonal[:, LANES:]
            return 0

        lax.fori_loop(0, 2, one, 0)
        fresh[slot, :MAXPNO, :] = squares[0, :MAXPNO, :LANES]
        fresh[slot, HALF_PACK : HALF_PACK + MAXPNO, :] = squares[1, :MAXPNO, :LANES]
        shared = jnp.where(
            pack_lane < REST, squares[0, :MAXPNO, LANES:], pltpu.roll(squares[1, :MAXPNO, LANES:], REST, 1)
        )
        fresh[slot, MAXPNO:HALF_PACK, :] = shared[:TOP]
        fresh[slot, HALF_PACK + MAXPNO : FOLD_AT, :] = shared[TOP:]
        folded = jnp.zeros((FOLD_ROWS, LANES), jnp.float32)
        for n in range(SQUARE_ROWS // FOLD_ROWS):
            rows = squares[1, n * FOLD_ROWS : (n + 1) * FOLD_ROWS, LANES:]
            moved = pltpu.roll(rows, (n * LEFT - SPARE) % LANES, 1)
            folded = jnp.where((fold_lane >= n * LEFT) & (fold_lane < (n + 1) * LEFT), moved, folded)
        fresh[slot, FOLD_AT:DIAG_AT, :] = folded

    def begin_half(slot, way, step, half):
        for piece in range(2):
            rows = rows_of(half, piece)
            sums[way, step, rows, :] = fresh[slot, rows, :]
            chain(way, step, half, piece).start()

    def add_half(way, step, half):
        for piece in range(2):
            rows = rows_of(half, piece)
            chain(way, step - 1, half, piece).wait_recv()
            sums[way, step, rows, :] = sums[way, step, rows, :] + fresh[way, rows, :]
            chain(way, step, half, piece).start()

    def ring_item(whole, item, _):
        way, step, first = locate(item)
        block_products(way, first, locate(item + 1)[2], whole)

        @pl.when(item == 0)
        def _():
            begin_half(0, 0, 0, 0)
            begin_half(0, 1, 0, 1)

        @pl.when(step == 1)
        def _():
            begin_half(way, way, step, 1 - way)

        @pl.when((step > 1) & (step < half_ring))
        def _():
            add_half(way, step, 1 - way)

        @pl.when((way == 1) & (step < half_ring))
        def _():
            add_half(0, step, 0)
            add_half(1, step, 1)

        @pl.when(item == 2)
        def _():
            for n in range(len(peers)):
                ask(n).wait_send()
            for port in ports:
                port.finish_sends()
            for single in singles:
                single.finish_served()
                single.finish_sends()

        return 0

    fresh[...] = jnp.zeros_like(fresh)
    squares[...] = jnp.zeros_like(squares)
    ahead = 5
    table_copy.wait()
    ports[0].finish_delivery()
    ports[1].finish_delivery()
    assemble(locate(0)[2], 0, (0, 1))
    lax.fori_loop(0, 2 * ahead, first_half, 0)
    for single in singles:
        single.finish_delivery()
    ports[2].finish_delivery()
    ports[3].finish_delivery()
    assemble(locate(0)[2], 0, (2, 3))
    lax.fori_loop(0, ahead, functools.partial(ring_item, False), 0)
    assemble(locate(ahead)[2], 0, (0, 1, 2, 3))
    lax.fori_loop(ahead, planes, functools.partial(ring_item, True), 0)
    for half in (1, 0):
        for piece in range(2):
            rows = rows_of(half, piece)
            for way in range(2):
                chain(way, half_ring - 1, half, piece).wait_recv()
            arrived = sums[0, half_ring, rows, :] + sums[1, half_ring, rows, :]
            out[rows, :] = arrived + fresh[0, rows, :]
    for n in range(group):
        count = counts[at_z * group + n].astype(jnp.float32)
        out[COUNTS + n : COUNTS + n + 1, :] = jnp.full((1, LANES), count)
    for step in range(half_ring):
        for way in range(2):
            for half in range(2):
                if step or half == way:
                    for piece in range(2):
                        chain(way, step, half, piece).wait_send()


def pair_products(blocks, domains, counts, coeff, planes):
    pair_dev, depth, slots = coeff.shape
    lines = 2 * RING * CORES
    bf16 = jnp.bfloat16
    tile = (MAIN, LANES)
    scratch = []
    for shape in (
        (RING, ATOMS),
        (RING * RING * CORES * ATOMS,),
        (2, ATOMS // 2),
        (RING, CORES, SHARE),
        (2, CORES, HALF_SHARE),
        (RING, SLOTS),
    ):
        scratch += [pltpu.VMEM(shape + tile, bf16)] * 4
    for shape in (
        (ATOMS,),
        (RING - 1, ATOMS),
        (RING, CORES, PICKS),
        (2, CORES, HALF),
        (RING * CORES * PICKS,),
    ):
        scratch += [pltpu.VMEM(shape + tile, bf16)] * 2
    scratch += [
        pltpu.VMEM((lines, 8, LANES), jnp.int32),
        pltpu.SMEM((lines, 8, LANES), jnp.int32),
        pltpu.VMEM((3, 8, LANES), jnp.int32),
        pltpu.SMEM((3, 8, LANES), jnp.int32),
        pltpu.VMEM((8, LANES), jnp.int32),
        pltpu.VMEM((8, LANES), jnp.int32),
        pltpu.VMEM((ATOMS * MAIN, ATOMS * MAIN), bf16),
        pltpu.VMEM((ATOMS * MAIN, ATOMS * MAIN), bf16),
        pltpu.VMEM((pair_dev, depth, slots), bf16),
        pltpu.VMEM((pair_dev, MAXPNO, DEPTH), bf16),
        pltpu.VMEM((DEPTH, depth), bf16),
        pltpu.VMEM((2, DEPTH, blocks.shape[2]), bf16),
        pltpu.VMEM((pair_dev, MAXPNO, MAXPNO), jnp.float32),
        pltpu.VMEM((2, planes // 2 + 1, PACK, LANES), jnp.float32),
        pltpu.VMEM((2, PACK, LANES), jnp.float32),
        pltpu.VMEM((MAXPNO, slots), bf16),
        pltpu.VMEM((2, SQUARE_ROWS, 2 * LANES), jnp.float32),
        pltpu.VMEM(blocks.shape, bf16),
        pltpu.SemaphoreType.DMA((4, 27)),
        pltpu.SemaphoreType.DMA((4, 27)),
        pltpu.SemaphoreType.DMA((2, 16)),
        pltpu.SemaphoreType.DMA((2, 16)),
        pltpu.SemaphoreType.DMA((lines,)),
        pltpu.SemaphoreType.DMA((lines,)),
        pltpu.SemaphoreType.DMA((8,)),
        pltpu.SemaphoreType.DMA((2 * planes, 2)),
        pltpu.SemaphoreType.DMA((2 * planes, 2)),
    ]
    return pl.pallas_call(
        main_kernel,
        out_shape=pltpu.VMEM((PACK, LANES), jnp.float32),
        in_specs=[
            pl.BlockSpec(memory_space=pl.ANY),
            pl.BlockSpec(memory_space=pltpu.SMEM),
            pl.BlockSpec(memory_space=pltpu.SMEM),
            pl.BlockSpec(memory_space=pl.ANY),
        ],
        out_specs=pl.BlockSpec(memory_space=pltpu.VMEM),
        scratch_shapes=scratch,
        compiler_params=params(60, collective_id=0, has_side_effects=True),
    )(blocks, domains, counts, coeff)


def tail_kernel(packed, amp, energy_row, energy_col, out, wide):
    slots = amp.shape[1]
    step = pl.program_id(0)
    full_row = lax.broadcasted_iota(jnp.int32, (slots, slots), 0)
    full_col = lax.broadcasted_iota(jnp.int32, (slots, slots), 1)
    lane = lax.broadcasted_iota(jnp.int32, (MAXPNO, LANES), 1)
    fold_lane = lax.broadcasted_iota(jnp.int32, (FOLD_ROWS, LANES), 1)
    wide[MAXPNO:, :] = jnp.zeros((slots - MAXPNO, slots), jnp.float32)

    def shared_at(begin, end):
        if end <= TOP:
            return packed[MAXPNO + begin : MAXPNO + end, :]
        return packed[HALF_PACK + MAXPNO + begin - TOP : HALF_PACK + MAXPNO + end - TOP, :]

    @pl.when(step == 0)
    def _():
        wide[:MAXPNO, :LANES] = packed[:MAXPNO, :]
        for begin, end in ((0, TOP), (TOP, MAXPNO)):
            wide[begin:end, LANES:] = jnp.where(lane[begin:end] < REST, shared_at(begin, end), 0.0)

    @pl.when(step == 1)
    def _():
        wide[:MAXPNO, :LANES] = packed[HALF_PACK : HALF_PACK + MAXPNO, :]
        for begin, end in ((0, TOP), (TOP, MAXPNO)):
            turned = pltpu.roll(shared_at(begin, end), SPARE, 1)
            wide[begin:end, LANES:] = jnp.where(lane[begin:end] < SPARE, turned, 0.0)
        folded = packed[FOLD_AT:DIAG_AT, :]
        for n in range(SQUARE_ROWS // FOLD_ROWS):
            begin, end = n * FOLD_ROWS, min((n + 1) * FOLD_ROWS, MAXPNO)
            moved = pltpu.roll(folded, (SPARE - n * LEFT) % LANES, 1)
            left = (fold_lane >= SPARE) & (fold_lane < REST)
            held = wide[begin:end, LANES:]
            wide[begin:end, LANES:] = jnp.where(left[: end - begin], moved[: end - begin], held)

    square = wide[...]
    at = DIAG_AT + 2 * step
    diagonal = jnp.concatenate([packed[pl.ds(at, 1), :], packed[pl.ds(at + 1, 1), :]], axis=1)
    on_diagonal = full_row == full_col
    for n in range(2):
        count = packed[pl.ds(COUNTS + 2 * step + n, 1), :][:, :1].astype(jnp.int32)
        row, col = full_row[:MAXPNO], full_col[:MAXPNO]
        if n == 0:
            held = jnp.where(full_row >= full_col, square, 0.0)
        else:
            held = jnp.where(full_row < full_col, square, jnp.where(on_diagonal, diagonal, 0.0))
        products = held[:MAXPNO] + jnp.where(row == col, 0.0, held.T[:MAXPNO])
        valid = (row < count) & (col < count)
        products = jnp.where(valid, products / NAUX, 0.0)
        amps = amp[n]
        contract = (((1,), (1,)), ((), ()))
        high = products.astype(jnp.bfloat16)
        left = products - high.astype(jnp.float32)
        mid = left.astype(jnp.bfloat16)
        low = (left - mid.astype(jnp.float32)).astype(jnp.bfloat16)
        coupled = lax.dot_general(low, amps, contract, preferred_element_type=jnp.float32)
        coupled += lax.dot_general(mid, amps, contract, preferred_element_type=jnp.float32)
        coupled += lax.dot_general(high, amps, contract, preferred_element_type=jnp.float32)
        energies = energy_col[n, :MAXPNO] + energy_row[pl.ds(2 * step + n, 1), :]
        result = products + coupled + energies * amps[:MAXPNO].astype(jnp.float32)
        out[n, :MAXPNO] = jnp.where(valid, result, 0.0)
        out[n, MAXPNO:] = jnp.zeros((slots - MAXPNO, slots), jnp.float32)


def tail(packed, amp, energy):
    subs, slots, _ = amp.shape
    return pl.pallas_call(
        tail_kernel,
        out_shape=jax.ShapeDtypeStruct((subs, slots, slots), jnp.float32),
        grid=(subs // 2,),
        in_specs=[
            pl.BlockSpec((PACK, LANES), lambda i: (0, 0)),
            pl.BlockSpec((2, slots, slots), lambda i: (i, 0, 0)),
            pl.BlockSpec((subs, slots), lambda i: (0, 0)),
            pl.BlockSpec((2, slots, 1), lambda i: (i, 0, 0)),
        ],
        out_specs=pl.BlockSpec((2, slots, slots), lambda i: (i, 0, 0)),
        scratch_shapes=[pltpu.VMEM((slots, slots), jnp.float32)],
        compiler_params=params(32),
    )(packed, amp, energy, energy[:, :, None])


def on_device(atom_blocks, domains, pno_counts, pno_coeffs, amplitudes, pno_energies):
    planes = lax.axis_size("ri")
    mine = pair_products(atom_blocks.transpose(1, 0, 2), domains.T, pno_counts, pno_coeffs, planes)
    return tail(mine, amplitudes, pno_energies)


def solution(mesh):
    placed = (
        P("pairs", None, "ri"),
        P("pairs", None),
        P("pairs"),
        P("pairs", None, None),
        P(("pairs", "ri"), None, None),
        P(("pairs", "ri"), None),
    )
    return jax.shard_map(
        on_device,
        mesh=mesh,
        in_specs=placed,
        out_specs=P(("pairs", "ri"), None, None),
        check_vma=False,
    )
```

```python
import functools

import jax
import jax.numpy as jnp
from jax import lax
from jax.experimental import pallas as pl
from jax.experimental.pallas import tpu as pltpu
from jax.sharding import PartitionSpec as P

NAUX = 14336
CAP = 3
MAXPNO = 200
MAIN = 16
REM = 4
SPLIT = 128
REST = MAXPNO - SPLIT
LANES = 128
MIB = 1 << 20
RING = 4
CORES = 2
ATOMS = 16
DOM = 12
BAND = MAIN + REM
PICKS = RING * CAP
HALF = PICKS // 2
DEPTH = 256
SPARE = LANES - REST
LEFT = REST - SPARE
FOLD_ROWS = 32
HALF_PACK = 320
PACK = 2 * HALF_PACK
TOP = HALF_PACK - MAXPNO
FOLD_AT = PACK - FOLD_ROWS - 8
DIAG_AT = PACK - 8
COUNTS = PACK - 4
SQUARE_ROWS = 224
SLOTS = 48
SHARE = SLOTS // CORES
HALF_SHARE = SHARE // 2
ROW_LINES = RING * CORES
MAINS = ((0, 1, 2), (3, 4, 5), (6, 7, 8), (10, 11, 12))
RESTS = ((0, 1, 2), (3, 4, 5), (6, 7, 8, 9), (10, 11, 12, 13))
SINGLES = (9, 13)
MESH = pl.DeviceIdType.MESH


def params(mib, **kw):
    return pltpu.CompilerParams(vmem_limit_bytes=mib * MIB, **kw)


class Ports:
    def __init__(self, chunk, gather_to, deliver_to, wire, ring, send, relay, recv, out_sems, in_sems, core):
        self.gather_to, self.deliver_to, self.core = gather_to, deliver_to, core
        self.wire, self.ring, self.send, self.relay, self.recv = wire, ring, send, relay, recv
        self.out_sems, self.in_sems, self.chunk = out_sems, in_sems, chunk

    def copy(self, src, dst, out_at, in_at, to):
        return pltpu.make_async_remote_copy(
            src_ref=src,
            dst_ref=dst,
            send_sem=self.out_sems.at[self.chunk, out_at],
            recv_sem=self.in_sems.at[self.chunk, in_at],
            device_id={"pairs": to},
            device_id_type=MESH,
        )

    def gather_first(self):
        up = self.copy(self.wire, self.ring.at[2], 0, 1, self.gather_to(1, self.core))
        down = self.copy(self.wire, self.ring.at[0], 1, 0, self.gather_to(3, self.core))
        return up, down

    def gather_second(self):
        half = ATOMS // 2
        low, high = pl.ds(0, half), pl.ds(half, half)
        up = self.copy(self.ring.at[2, low], self.ring.at[1, low], 2, 2, self.gather_to(1, self.core))
        down = self.copy(self.ring.at[0, high], self.ring.at[1, high], 3, 3, self.gather_to(3, self.core))
        return up, down

    def place(self, rel, core):
        return (rel * CORES + core) * PICKS

    def far(self):
        up = self.copy(self.send.at[2, :, pl.ds(0, HALF)], self.relay.at[0], 4, 4, self.deliver_to(1, self.core))
        down = self.copy(self.send.at[2, :, pl.ds(HALF, HALF)], self.relay.at[1], 5, 5, self.deliver_to(3, self.core))
        return up, down

    def near(self):
        copies = []
        for n, step in enumerate((1, 3)):
            for core in range(CORES):
                dst = self.recv.at[pl.ds(self.place(RING - step, self.core), PICKS)]
                at = 6 + 2 * n
                copies.append(self.copy(self.send.at[step, core], dst, at + core, at + self.core, self.deliver_to(step, core)))
        other = 1 - self.core
        dst = self.recv.at[pl.ds(self.place(0, self.core), PICKS)]
        copies.append(self.copy(self.send.at[0, other], dst, 10, 10, self.deliver_to(0, other)))
        return copies

    def own(self):
        return pltpu.make_async_copy(
            self.send.at[0, self.core],
            self.recv.at[pl.ds(self.place(0, self.core), PICKS)],
            self.in_sems.at[self.chunk, 11],
        )

    def onward(self):
        copies = []
        for way, step in enumerate((1, 3)):
            for core in range(CORES):
                dst = self.recv.at[pl.ds(self.place(2, self.core) + way * HALF, HALF)]
                at = 12 + 2 * way
                copies.append(self.copy(self.relay.at[way, core], dst, at + core, at + self.core, self.deliver_to(step, core)))
        return copies

    def start_gather(self):
        for copy in self.gather_first():
            copy.start()

    def forward_gather(self):
        up, down = self.gather_second()
        first_up, first_down = self.gather_first()
        first_up.wait_recv()
        up.start()
        first_down.wait_recv()
        down.start()

    def finish_gather(self):
        for copy in self.gather_second():
            copy.wait_recv()

    def start_far(self):
        for copy in self.far():
            copy.start()

    def start_near(self):
        for copy in self.near():
            copy.start()
        self.own().start()

    def forward_delivery(self):
        far, onward = self.far(), self.onward()
        for way in range(2):
            far[way].wait_recv()
            for copy in onward[2 * way : 2 * way + 2]:
                copy.start()

    def finish_delivery(self):
        for n, step in enumerate((1, 3)):
            for core in range(CORES):
                dst = self.recv.at[pl.ds(self.place(step, core), PICKS)]
                at = 6 + 2 * (1 - n)
                self.copy(dst, dst, at + core, at + core, self.deliver_to(1, self.core)).wait_recv()
        other = 1 - self.core
        dst = self.recv.at[pl.ds(self.place(0, other), PICKS)]
        self.copy(dst, dst, 10, 10, self.deliver_to(1, self.core)).wait_recv()
        self.own().wait()
        for way in range(2):
            for core in range(CORES):
                dst = self.recv.at[pl.ds(self.place(2, core) + way * HALF, HALF)]
                at = 12 + 2 * way
                self.copy(dst, dst, at + core, at + core, self.deliver_to(1, self.core)).wait_recv()

    def finish_served(self):
        for copy in self.far() + tuple(self.near()):
            copy.wait_send()

    def finish_sends(self):
        for copy in self.gather_first() + self.gather_second() + tuple(self.onward()):
            copy.wait_send()


class Relay:
    def __init__(self, chunk, first_to, other_to, u, v, core, bufs, out_sems, in_sems):
        self.chunk, self.first_to, self.other_to = chunk, first_to, other_to
        self.u, self.v, self.core = u, v, core
        self.wire, self.table, self.passing, self.send, self.relay, self.recv = bufs
        self.out_sems, self.in_sems = out_sems, in_sems

    def copy(self, src, dst, out_at, in_at, to):
        return pltpu.make_async_remote_copy(
            src_ref=src,
            dst_ref=dst,
            send_sem=self.out_sems.at[self.chunk, out_at],
            recv_sem=self.in_sems.at[self.chunk, in_at],
            device_id={"pairs": to},
            device_id_type=MESH,
        )

    def arrival(self, dst, at):
        return self.copy(dst, dst, at, at, self.first_to(1, self.core))

    def near_u(self, step):
        return lax.rem(self.u + step, RING)

    def near_v(self, step):
        return lax.rem(self.v + step, RING)

    def atoms(self, step, at=0, count=ATOMS):
        base = ((self.v * CORES + self.core) * RING + self.near_u(step)) * ATOMS
        return self.table.at[pl.ds(base + at, count)]

    def block(self, step, core, at=0, count=RING * ATOMS):
        return self.table.at[pl.ds((self.near_v(step) * CORES + core) * RING * ATOMS + at, count)]

    def spread_sends(self):
        half = ATOMS // 2
        far = self.near_u(2)
        up, down = self.first_to(1, self.core), self.first_to(3, self.core)
        return [
            self.copy(self.wire.at[far, pl.ds(0, half)], self.passing.at[0], 2, 2, up),
            self.copy(self.wire.at[far, pl.ds(half, half)], self.passing.at[1], 3, 3, down),
            self.copy(self.wire.at[self.near_u(1)], self.atoms(0), 0, 1, up),
            self.copy(self.wire.at[self.near_u(3)], self.atoms(0), 1, 0, down),
        ]

    def spread_own(self):
        return pltpu.make_async_copy(self.wire.at[self.u], self.atoms(0), self.in_sems.at[self.chunk, 25])

    def spread_onward(self):
        half = ATOMS // 2
        return [
            self.copy(self.passing.at[0], self.atoms(3, 0, half), 4, 4, self.first_to(1, self.core)),
            self.copy(self.passing.at[1], self.atoms(1, half, half), 5, 5, self.first_to(3, self.core)),
        ]

    def start_spread(self):
        for copy in self.spread_sends():
            copy.start()
        self.spread_own().start()

    def forward_spread(self):
        for way, copy in enumerate(self.spread_onward()):
            self.arrival(self.passing.at[way], 2 + way).wait_recv()
            copy.start()

    def finish_spread(self):
        half = ATOMS // 2
        self.spread_own().wait()
        self.arrival(self.atoms(1), 0).wait_recv()
        self.arrival(self.atoms(3), 1).wait_recv()
        self.arrival(self.atoms(2, 0, half), 4).wait_recv()
        self.arrival(self.atoms(2, half, half), 5).wait_recv()

    def gather_first(self):
        own = self.block(0, self.core)
        return [
            self.copy(own, own, 6, 7, self.other_to(1, self.core)),
            self.copy(own, own, 7, 6, self.other_to(3, self.core)),
        ]

    def gather_second(self):
        half = RING * ATOMS // 2
        low, high = self.block(3, self.core, 0, half), self.block(1, self.core, half, half)
        return [
            self.copy(low, low, 8, 8, self.other_to(1, self.core)),
            self.copy(high, high, 9, 9, self.other_to(3, self.core)),
        ]

    def share(self, step):
        mine = self.block(step, self.core)
        return self.copy(mine, mine, 10 + step, 10 + step, self.first_to(0, 1 - self.core))

    def start_gather(self):
        for copy in self.gather_first():
            copy.start()
        self.share(0).start()

    def forward_gather(self):
        low, high = self.gather_second()
        self.arrival(self.block(3, self.core), 7).wait_recv()
        low.start()
        self.share(3).start()
        self.arrival(self.block(1, self.core), 6).wait_recv()
        high.start()
        self.share(1).start()

    def finish_gather(self):
        half = RING * ATOMS // 2
        self.arrival(self.block(2, self.core, 0, half), 8).wait_recv()
        self.arrival(self.block(2, self.core, half, half), 9).wait_recv()
        self.share(2).start()

    def finish_share(self):
        for step in range(RING):
            self.arrival(self.block(step, 1 - self.core), 10 + step).wait_recv()

    def place(self, step, core, at=0, count=SHARE):
        return self.recv.at[self.near_u(step), pl.ds(core * SHARE + at, count)]

    def far(self):
        return [
            self.copy(self.send.at[2, :, pl.ds(0, HALF_SHARE)], self.relay.at[0], 19, 19, self.first_to(1, self.core)),
            self.copy(
                self.send.at[2, :, pl.ds(HALF_SHARE, HALF_SHARE)], self.relay.at[1], 20, 20, self.first_to(3, self.core)
            ),
        ]

    def near(self):
        copies = []
        dst = self.place(0, self.core)
        for n, step in enumerate((1, 3)):
            for core in range(CORES):
                at = 14 + 2 * n
                copies.append(self.copy(self.send.at[step, core], dst, at + core, at + self.core, self.first_to(step, core)))
        other = 1 - self.core
        copies.append(self.copy(self.send.at[0, other], dst, 18, 18, self.first_to(0, other)))
        return copies

    def own(self):
        return pltpu.make_async_copy(
            self.send.at[0, self.core], self.place(0, self.core), self.in_sems.at[self.chunk, 26]
        )

    def onward(self):
        copies = []
        for way, step in enumerate((1, 3)):
            dst = self.place(RING - step, self.core, way * HALF_SHARE, HALF_SHARE)
            for core in range(CORES):
                at = 21 + 2 * way
                copies.append(self.copy(self.relay.at[way, core], dst, at + core, at + self.core, self.first_to(step, core)))
        return copies

    def start_far(self):
        for copy in self.far():
            copy.start()

    def start_near(self):
        for copy in self.near():
            copy.start()
        self.own().start()

    def forward_delivery(self):
        onward = self.onward()
        for way in range(2):
            self.arrival(self.relay.at[way], 19 + way).wait_recv()
            for copy in onward[2 * way : 2 * way + 2]:
                copy.start()

    def finish_delivery(self):
        for core in range(CORES):
            self.arrival(self.place(3, core), 14 + core).wait_recv()
            self.arrival(self.place(1, core), 16 + core).wait_recv()
            for way in range(2):
                at = 21 + 2 * way + core
                self.arrival(self.place(2, core, way * HALF_SHARE, HALF_SHARE), at).wait_recv()
        self.arrival(self.place(0, 1 - self.core), 18).wait_recv()
        self.own().wait()

    def finish_sends(self):
        copies = self.spread_sends() + self.spread_onward() + self.gather_first() + self.gather_second()
        copies += [self.share(step) for step in range(RING)] + self.far() + self.near() + self.onward()
        for copy in copies:
            copy.wait_send()


def main_kernel(
    blocks_hbm, domains, counts, coeff_hbm, out, *scratch
):
    relay_bufs = [scratch[4 * n : 4 * n + 4] for n in range(6)]
    single_bufs = [scratch[24 + 2 * n : 26 + 2 * n] for n in range(5)]
    wires, recvs = relay_bufs[0], relay_bufs[5]
    single_wires, single_recvs = single_bufs[0], single_bufs[4]
    asked, asked_smem, tables, places, request, ids, perm_main, perm_rest = scratch[34:42]
    coeff, coeff_t, perm, blk, total, sums, fresh, same, squares, blocks = scratch[42:52]
    out_sems, in_sems, single_out, single_in, ask_out, ask_in, local_sems, sum_out, sum_in = scratch[52:61]
    me = lax.axis_index("pairs")
    at_z = lax.axis_index("ri")
    planes = 2 * (sums.shape[1] - 1)
    above, below = lax.rem(at_z + 1, planes), lax.rem(at_z + planes - 1, planes)
    core = lax.rem(me, CORES)
    chip = lax.div(me, CORES)
    at_x = lax.rem(chip, RING)
    at_y = lax.div(chip, RING)

    def along_x(step, to_core):
        return (at_y * RING + lax.rem(at_x + step, RING)) * CORES + to_core

    def along_y(step, to_core):
        return (lax.rem(at_y + step, RING) * RING + at_x) * CORES + to_core

    peers = []
    for to_core in range(2):
        for step in range(1, RING):
            peers.append((along_y(step, to_core), step * CORES + to_core, (RING - step) * CORES + core))
            peers.append(
                (along_x(step, to_core), (RING + step) * CORES + to_core, (2 * RING - step) * CORES + core)
            )
    peers.append((along_x(0, 1 - core), 1 - core, core))

    barrier = pltpu.get_barrier_semaphore()
    for peer, _, _ in peers:
        pl.semaphore_signal(barrier, inc=1, device_id={"pairs": peer}, device_id_type=MESH)
    for plane in (above, below):
        pl.semaphore_signal(barrier, inc=1, device_id={"ri": plane}, device_id_type=MESH)

    def ask(n):
        peer, _, there = peers[n]
        return pltpu.make_async_remote_copy(
            src_ref=request,
            dst_ref=asked.at[there],
            send_sem=ask_out.at[n],
            recv_sem=ask_in.at[there],
            device_id={"pairs": peer},
            device_id_type=MESH,
        )

    ports = []
    for chunk in range(4):
        by_x = chunk % 2 == 0
        first_to, other_to = (along_x, along_y) if by_x else (along_y, along_x)
        u, v = (at_x, at_y) if by_x else (at_y, at_x)
        bufs = [group_bufs[chunk] for group_bufs in relay_bufs]
        ports.append(Relay(chunk, first_to, other_to, u, v, core, bufs, out_sems, in_sems))
    singles = []
    for n in range(2):
        gather_to, deliver_to = (along_x, along_y) if n == 0 else (along_y, along_x)
        bufs = [group_bufs[n] for group_bufs in single_bufs]
        singles.append(Ports(n, gather_to, deliver_to, *bufs, single_out, single_in, core))

    fetches = []
    for chunk in range(4):
        tiles = RESTS[chunk]
        cols = pl.ds(tiles[0] * LANES, len(tiles) * LANES)
        fetches.append(
            pltpu.make_async_copy(blocks_hbm.at[:, :, cols], blocks.at[:, :, cols], local_sems.at[4 + chunk])
        )
        fetches[chunk].start()
    fetch = pltpu.make_async_copy(coeff_hbm, coeff, local_sems.at[0])
    fetch.start()

    square = (ATOMS * MAIN, ATOMS * MAIN)
    out_at = lax.broadcasted_iota(jnp.int32, square, 0)
    from_at = lax.broadcasted_iota(jnp.int32, square, 1)
    band_at, atom_at = out_at & (MAIN - 1), lax.shift_right_logical(out_at, 4)
    perm_main[...] = jnp.where(band_at * ATOMS + atom_at == from_at, 1.0, 0.0).astype(jnp.bfloat16)
    rest_at = lax.shift_right_logical(band_at, 2) * (REM * ATOMS) + (band_at & (REM - 1)) * ATOMS + atom_at
    perm_rest[...] = jnp.where(rest_at == from_at, 1.0, 0.0).astype(jnp.bfloat16)

    def main_rows(tiles):
        flat = blocks[:MAIN, :, tiles[0] * LANES : (tiles[-1] + 1) * LANES]
        flat = flat.reshape(MAIN * ATOMS, len(tiles) * LANES)
        return jnp.dot(perm_main[...], flat, preferred_element_type=jnp.float32).astype(jnp.bfloat16)

    def form(chunk):
        fetches[chunk].wait()
        main = main_rows(MAINS[chunk])
        for n in range(len(MAINS[chunk])):
            wires[chunk][n] = main[:, n * LANES : (n + 1) * LANES].reshape(ATOMS, MAIN, LANES)
        parts = [blocks[MAIN:, :, t * LANES : (t + 1) * LANES].reshape(REM * ATOMS, LANES) for t in RESTS[chunk]]
        stacked = jnp.concatenate(parts, axis=0)
        depth = stacked.shape[0]
        late = jnp.dot(perm_rest[:, :depth], stacked, preferred_element_type=jnp.float32).astype(jnp.bfloat16)
        wires[chunk][RING - 1] = late.reshape(ATOMS, MAIN, LANES)

    form(0)
    pl.semaphore_wait(barrier, len(peers) + 2)
    ports[0].start_spread()
    for chunk in range(1, 4):
        form(chunk)
        ports[chunk].start_spread()
    for n in range(2):
        single_wires[n][...] = main_rows(SINGLES[n : n + 1]).reshape(ATOMS, MAIN, LANES)
    for chunk in (0, 1):
        ports[chunk].forward_spread()
    for chunk in (0, 1):
        ports[chunk].finish_spread()
        ports[chunk].start_gather()

    for chunk in (2, 3):
        ports[chunk].forward_spread()

    def parts_of(atom):
        owner = lax.shift_right_logical(atom, 4)
        chip = lax.shift_right_logical(owner, 1)
        return owner, owner & (CORES - 1), chip & (RING - 1), lax.shift_right_logical(chip, 2), atom & (ATOMS - 1)

    map_shape = (8, LANES)
    map_row = lax.broadcasted_iota(jnp.int32, map_shape, 0)
    map_lane = lax.broadcasted_iota(jnp.int32, map_shape, 1)
    atom_map = map_row * LANES + map_lane
    pairs = domains.shape[1]

    def mark(pair, seen):
        for k in range(DOM):
            seen = jnp.where(atom_map == domains[k, pair], 1, seen)
        return seen

    named = lax.fori_loop(0, pairs, mark, jnp.zeros(map_shape, jnp.int32))
    owner, owner_core, owner_x, owner_y, local = parts_of(atom_map)
    rank = named
    for shift in (1, 2, 4, 8):
        rank = rank + jnp.where(local >= shift, pltpu.roll(rank, shift, 1), 0)
    order = named
    for shift in (1, 2, 4, 8, 16, 32, 64):
        order = order + jnp.where(map_lane >= shift, pltpu.roll(order, shift, 1), 0)
    counted = order
    map_rows = ATOMS * RING * RING * CORES // LANES
    for n in range(map_rows - 1):
        order = order + jnp.where(map_row > n, counted[n : n + 1, LANES - 1 :], 0)
    rel_x = (owner_x + RING - at_x) & (RING - 1)
    rel_y = (owner_y + RING - at_y) & (RING - 1)
    tables[0] = order - 1
    tables[1] = ((rel_y * CORES + owner_core) * RING + rel_x) * CAP + rank - 1
    tables[2] = ((rel_x * CORES + owner_core) * RING + rel_y) * CAP + rank - 1
    table_copy = pltpu.make_async_copy(tables, places, local_sems.at[3])
    table_copy.start()

    ids[:map_rows, :] = jnp.where(named > 0, order, 0)[:map_rows]
    ids[map_rows:, :] = jnp.where(named > 0, rank, 0)[:map_rows]
    upright = ids[...].T
    list_shape = (LANES, LANES)
    list_row = lax.broadcasted_iota(jnp.int32, list_shape, 0)
    list_lane = lax.broadcasted_iota(jnp.int32, list_shape, 1)
    rows = [jnp.zeros((1, LANES), jnp.int32) for _ in range(CAP + 2)]
    for n in range(map_rows):
        owner, owner_core, owner_x, owner_y, local = parts_of(list_row + n * LANES)
        own_lane = jnp.where(owner == list_lane, local, 0)
        order_at = jnp.broadcast_to(upright[:, n : n + 1], list_shape)
        rank_at = jnp.broadcast_to(upright[:, map_rows + n : map_rows + n + 1], list_shape)
        for j in range(CAP):
            rows[j] += jnp.sum(jnp.where(rank_at == j + 1, own_lane, 0), axis=0, keepdims=True)
        for j, (u, v) in enumerate(((owner_x, owner_y), (owner_y, owner_x))):
            held_at = ((v * CORES + owner_core) * RING + u) * ATOMS + local
            rows[CAP + j] += jnp.sum(jnp.where(order_at == list_lane + 1, held_at, 0), axis=0, keepdims=True)
    for n in range(CAP + 2):
        request[n : n + 1, :] = rows[n]
    request[CAP + 2 :, :] = jnp.zeros((6 - CAP, LANES), jnp.int32)

    for n in range(len(peers)):
        ask(n).start()
    own_ask = pltpu.make_async_copy(request, asked.at[core], local_sems.at[1])
    own_ask.start()
    for chunk in (2, 3):
        ports[chunk].finish_spread()

    shape = (DEPTH, DOM * BAND)
    row = lax.broadcasted_iota(jnp.int32, shape, 0)
    col = lax.broadcasted_iota(jnp.int32, shape, 1)
    split = DOM * MAIN
    late = row - split
    source = jnp.where(
        row < split,
        lax.shift_right_logical(row, 4) * BAND + (row & (MAIN - 1)),
        lax.shift_right_arithmetic(late, 2) * BAND + MAIN + (late & (REM - 1)),
    )
    perm[...] = jnp.where((source == col) & (row < DOM * BAND), 1.0, 0.0).astype(jnp.bfloat16)
    same[...] = jnp.where(
        lax.broadcasted_iota(jnp.int32, same.shape, 0) == lax.broadcasted_iota(jnp.int32, same.shape, 1), 1.0, 0.0
    ).astype(jnp.bfloat16)
    for n in range(2):
        blk[n, DOM * BAND :, :] = jnp.zeros((DEPTH - DOM * BAND, blk.shape[2]), jnp.bfloat16)
    fetch.wait()

    def prepare(begin, end):
        def turn(pair, _):
            ordered = [
                jnp.dot(perm[...], coeff[4 * pair + n], preferred_element_type=jnp.float32).astype(jnp.bfloat16)
                for n in range(4)
            ]
            for n in range(4):
                turned = lax.dot_general(
                    same[...], ordered[n], (((1,), (1,)), ((), ())), preferred_element_type=jnp.float32
                )
                coeff_t[4 * pair + n] = turned.astype(jnp.bfloat16)
            return 0

        lax.fori_loop(begin // 4, end // 4, turn, 0)

    prepare(0, 4)
    for chunk in (0, 1):
        ports[chunk].forward_gather()
    for chunk in (2, 3):
        ports[chunk].start_gather()

    for single in singles:
        single.start_gather()
    prepare(4, 12)

    own_ask.wait()
    for n in range(len(peers)):
        _, here, _ = peers[n]
        pltpu.make_async_remote_copy(
            src_ref=request,
            dst_ref=asked.at[here],
            send_sem=ask_out.at[n],
            recv_sem=ask_in.at[here],
            device_id={"pairs": peers[n][0]},
            device_id_type=MESH,
        ).wait_recv()
    to_smem = pltpu.make_async_copy(asked, asked_smem, local_sems.at[2])
    to_smem.start()
    to_smem.wait()

    def line_of(dest, on_row):
        return jnp.where(dest < CORES, dest, dest + ROW_LINES) if on_row else dest

    def pick_single(n):
        port = singles[n]
        owner_of = along_x if n == 0 else along_y

        def serve(dest, _):
            line = line_of(dest, n == 1)
            step, to_core = dest // CORES, dest % CORES
            for r in range(RING):
                for j in range(CAP):
                    atom = asked_smem[line, j, owner_of(r, core)]
                    found = port.wire[atom] if r == 0 else port.ring[r - 1, atom]
                    port.send[step, to_core, r * CAP + j] = found
            return 0

        lax.fori_loop(2 * CORES, 3 * CORES, serve, 0)
        port.start_far()

        def serve_near(dest, _):
            return serve(jnp.where(dest < 2 * CORES, dest, dest + CORES), 0)

        lax.fori_loop(0, 3 * CORES, serve_near, 0)
        port.start_near()

    def pick(chunk):
        port = ports[chunk]

        def serve(dest, _):
            line = line_of(dest, chunk % 2 == 0)
            step, to_core = dest // CORES, dest % CORES
            for n in range(SHARE):
                port.send[step, to_core, n] = port.table[asked_smem[line, CAP + chunk % 2, core * SHARE + n]]
            return 0

        lax.fori_loop(2 * CORES, 3 * CORES, serve, 0)
        port.start_far()

        def serve_near(dest, _):
            return serve(jnp.where(dest < 2 * CORES, dest, dest + CORES), 0)

        lax.fori_loop(0, 3 * CORES, serve_near, 0)
        port.start_near()

    for chunk in (0, 1):
        ports[chunk].finish_gather()
    for chunk in (0, 1):
        ports[chunk].finish_share()
        pick(chunk)
    for chunk in (2, 3):
        ports[chunk].forward_gather()
    for single in singles:
        single.forward_gather()
    prepare(12, 20)
    for chunk in (0, 1):
        ports[chunk].forward_delivery()
    prepare(20, 24)
    for chunk in (2, 3):
        ports[chunk].finish_gather()
    for n in range(2):
        singles[n].finish_gather()
        pick_single(n)
    for chunk in (2, 3):
        ports[chunk].finish_share()
        pick(chunk)
    prepare(24, 32)
    for single in singles:
        single.forward_delivery()
    for chunk in (2, 3):
        ports[chunk].forward_delivery()

    pack_row = lax.broadcasted_iota(jnp.int32, (MAXPNO, MAXPNO), 0)
    pack_col = lax.broadcasted_iota(jnp.int32, (MAXPNO, MAXPNO), 1)
    pack_lane = lax.broadcasted_iota(jnp.int32, (MAXPNO, LANES), 1)
    fold_lane = lax.broadcasted_iota(jnp.int32, (FOLD_ROWS, LANES), 1)

    def assemble(pair, slot, chunks):
        base = MAIN * DOM
        begin = 0
        upper = lax.broadcasted_iota(jnp.int32, (8, LANES), 0) < REM

        names = [domains[k, pair] for k in range(DOM)]

        def named_at(table):
            return [places[table, lax.shift_right_logical(a, 7), a & (LANES - 1)] for a in names]

        at = named_at(0)
        for chunk in chunks:
            tiles = len(RESTS[chunk])
            for n in range(RING - 1):
                span = slice(begin + n * LANES, begin + (n + 1) * LANES)
                for k in range(DOM):
                    blk[slot, MAIN * k : MAIN * (k + 1), span] = recvs[chunk][n, at[k]]
            if tiles == RING:
                span = slice(begin + (RING - 1) * LANES, begin + RING * LANES)
                single_at = named_at(1 + chunk % 2)
                for k in range(DOM):
                    blk[slot, MAIN * k : MAIN * (k + 1), span] = single_recvs[chunk % 2][single_at[k]]
            for k in range(0, DOM, 4):
                rest = [recvs[chunk][RING - 1, at[k + n]].astype(jnp.float32) for n in range(4)]
                for half in range((tiles + 1) // 2):
                    parts = [r[8 * half : 8 * half + 8] for r in rest]
                    shifted = [pltpu.roll(part, REM, 0) for part in parts]
                    for q in range(2 * half, min(2 * half + 2, tiles)):
                        first, second = (parts, shifted) if q % 2 == 0 else (shifted, parts)
                        low = jnp.where(upper, first[0], second[1])
                        high = jnp.where(upper, first[2], second[3])
                        both = jnp.concatenate([low, high], axis=0).astype(jnp.bfloat16)
                        tile = slice(begin + q * LANES, begin + (q + 1) * LANES)
                        blk[slot, base + REM * k : base + REM * (k + 4), tile] = both
            begin += tiles * LANES
        return begin

    def multiply(pair, slot, cols):
        weights = coeff_t[pair]
        vecs = []
        for at in range(0, cols, 256):
            vec = jnp.dot(weights, blk[slot, :, at : at + 256], preferred_element_type=jnp.float32)
            vecs.append(vec.astype(jnp.bfloat16))
        vecs = jnp.concatenate(vecs, axis=1)
        return lax.dot_general(vecs, vecs, (((1,), (1,)), ((), ())), preferred_element_type=jnp.float32)

    early_cols = LANES * (len(RESTS[0]) + len(RESTS[1]))
    late_cols = LANES * (len(RESTS[2]) + len(RESTS[3]))
    group = coeff.shape[0] // planes
    half_ring = planes // 2
    part = HALF_PACK // 2

    def rows_of(half, piece):
        return pl.ds(pl.multiple_of(half * HALF_PACK + piece * part, 8), part)

    def chain(way, step, half, piece):
        rows = rows_of(half, piece)
        return pltpu.make_async_remote_copy(
            src_ref=sums.at[way, step, rows],
            dst_ref=sums.at[way, step + 1, rows],
            send_sem=sum_out.at[(way * half_ring + step) * 2 + half, piece],
            recv_sem=sum_in.at[(way * half_ring + step) * 2 + half, piece],
            device_id={"ri": jnp.where(way == 0, above, below)},
            device_id_type=MESH,
        )

    def locate(item):
        step = (item + 1) // 2
        way = jnp.where(item == 0, 0, (item + 1) % 2)
        away = jnp.where(way == 0, half_ring - step, half_ring + step)
        return way, step, lax.rem(at_z + away, planes) * group

    def first_half(step, _):
        pair = locate(step // 2)[2] + 2 * (step % 2)
        following = locate((step + 1) // 2)[2] + 2 * ((step + 1) % 2)
        assemble(pair + 1, 1, (0, 1))
        total[pair] = multiply(pair, 0, early_cols)
        assemble(following, 0, (0, 1))
        total[pair + 1] = multiply(pair + 1, 1, early_cols)
        return 0

    def block_products(slot, first, following, whole):
        chunks = (0, 1, 2, 3) if whole else (2, 3)
        cols = early_cols + late_cols if whole else late_cols

        def one(duo, _):
            pair = first + 2 * duo
            assemble(pair + 1, 1, chunks)
            here = multiply(pair, 0, cols)
            assemble(jnp.where(duo == 0, pair + 2, following), 0, chunks)
            there = multiply(pair + 1, 1, cols)
            if not whole:
                here += total[pair]
                there += total[pair + 1]
            squares[duo, :MAXPNO, :MAXPNO] = jnp.where(pack_row >= pack_col, here, there)
            diagonal = jnp.sum(jnp.where(pack_row == pack_col, there, 0.0), axis=0, keepdims=True)
            at = DIAG_AT + 2 * duo
            fresh[slot, pl.ds(at, 1), :] = diagonal[:, :LANES]
            fresh[slot, pl.ds(at + 1, 1), :REST] = diagonal[:, LANES:]
            return 0

        lax.fori_loop(0, 2, one, 0)
        fresh[slot, :MAXPNO, :] = squares[0, :MAXPNO, :LANES]
        fresh[slot, HALF_PACK : HALF_PACK + MAXPNO, :] = squares[1, :MAXPNO, :LANES]
        shared = jnp.where(
            pack_lane < REST, squares[0, :MAXPNO, LANES:], pltpu.roll(squares[1, :MAXPNO, LANES:], REST, 1)
        )
        fresh[slot, MAXPNO:HALF_PACK, :] = shared[:TOP]
        fresh[slot, HALF_PACK + MAXPNO : FOLD_AT, :] = shared[TOP:]
        folded = jnp.zeros((FOLD_ROWS, LANES), jnp.float32)
        for n in range(SQUARE_ROWS // FOLD_ROWS):
            rows = squares[1, n * FOLD_ROWS : (n + 1) * FOLD_ROWS, LANES:]
            moved = pltpu.roll(rows, (n * LEFT - SPARE) % LANES, 1)
            folded = jnp.where((fold_lane >= n * LEFT) & (fold_lane < (n + 1) * LEFT), moved, folded)
        fresh[slot, FOLD_AT:DIAG_AT, :] = folded

    def begin_half(slot, way, step, half):
        for piece in range(2):
            rows = rows_of(half, piece)
            sums[way, step, rows, :] = fresh[slot, rows, :]
            chain(way, step, half, piece).start()

    def add_half(way, step, half):
        for piece in range(2):
            rows = rows_of(half, piece)
            chain(way, step - 1, half, piece).wait_recv()
            sums[way, step, rows, :] = sums[way, step, rows, :] + fresh[way, rows, :]
            chain(way, step, half, piece).start()

    def ring_item(whole, item, _):
        way, step, first = locate(item)
        block_products(way, first, locate(item + 1)[2], whole)

        @pl.when(item == 0)
        def _():
            begin_half(0, 0, 0, 0)
            begin_half(0, 1, 0, 1)

        @pl.when(step == 1)
        def _():
            begin_half(way, way, step, 1 - way)

        @pl.when((step > 1) & (step < half_ring))
        def _():
            add_half(way, step, 1 - way)

        @pl.when((way == 1) & (step < half_ring))
        def _():
            add_half(0, step, 0)
            add_half(1, step, 1)

        return 0

    fresh[...] = jnp.zeros_like(fresh)
    squares[...] = jnp.zeros_like(squares)
    ahead = 4
    table_copy.wait()
    ports[0].finish_delivery()
    ports[1].finish_delivery()
    assemble(locate(0)[2], 0, (0, 1))
    lax.fori_loop(0, 2 * ahead, first_half, 0)
    for n in range(len(peers)):
        ask(n).wait_send()
    for chunk in (0, 1):
        ports[chunk].finish_sends()
    for single in singles:
        single.finish_delivery()
    ports[2].finish_delivery()
    ports[3].finish_delivery()
    assemble(locate(0)[2], 0, (2, 3))
    lax.fori_loop(0, ahead, functools.partial(ring_item, False), 0)
    assemble(locate(ahead)[2], 0, (0, 1, 2, 3))
    lax.fori_loop(ahead, planes, functools.partial(ring_item, True), 0)
    for chunk in (2, 3):
        ports[chunk].finish_sends()
    for single in singles:
        single.finish_served()
        single.finish_sends()
    for half in (1, 0):
        for piece in range(2):
            rows = rows_of(half, piece)
            for way in range(2):
                chain(way, half_ring - 1, half, piece).wait_recv()
            arrived = sums[0, half_ring, rows, :] + sums[1, half_ring, rows, :]
            out[rows, :] = arrived + fresh[0, rows, :]
    for n in range(group):
        count = counts[at_z * group + n].astype(jnp.float32)
        out[COUNTS + n : COUNTS + n + 1, :] = jnp.full((1, LANES), count)
    for step in range(half_ring):
        for way in range(2):
            for half in range(2):
                if step or half == way:
                    for piece in range(2):
                        chain(way, step, half, piece).wait_send()


def pair_products(blocks, domains, counts, coeff, planes):
    pair_dev, depth, slots = coeff.shape
    lines = 2 * RING * CORES
    bf16 = jnp.bfloat16
    tile = (MAIN, LANES)
    scratch = []
    for shape in (
        (RING, ATOMS),
        (RING * RING * CORES * ATOMS,),
        (2, ATOMS // 2),
        (RING, CORES, SHARE),
        (2, CORES, HALF_SHARE),
        (RING, SLOTS),
    ):
        scratch += [pltpu.VMEM(shape + tile, bf16)] * 4
    for shape in (
        (ATOMS,),
        (RING - 1, ATOMS),
        (RING, CORES, PICKS),
        (2, CORES, HALF),
        (RING * CORES * PICKS,),
    ):
        scratch += [pltpu.VMEM(shape + tile, bf16)] * 2
    scratch += [
        pltpu.VMEM((lines, 8, LANES), jnp.int32),
        pltpu.SMEM((lines, 8, LANES), jnp.int32),
        pltpu.VMEM((3, 8, LANES), jnp.int32),
        pltpu.SMEM((3, 8, LANES), jnp.int32),
        pltpu.VMEM((8, LANES), jnp.int32),
        pltpu.VMEM((8, LANES), jnp.int32),
        pltpu.VMEM((ATOMS * MAIN, ATOMS * MAIN), bf16),
        pltpu.VMEM((ATOMS * MAIN, ATOMS * MAIN), bf16),
        pltpu.VMEM((pair_dev, depth, slots), bf16),
        pltpu.VMEM((pair_dev, MAXPNO, DEPTH), bf16),
        pltpu.VMEM((DEPTH, depth), bf16),
        pltpu.VMEM((2, DEPTH, blocks.shape[2]), bf16),
        pltpu.VMEM((pair_dev, MAXPNO, MAXPNO), jnp.float32),
        pltpu.VMEM((2, planes // 2 + 1, PACK, LANES), jnp.float32),
        pltpu.VMEM((2, PACK, LANES), jnp.float32),
        pltpu.VMEM((MAXPNO, slots), bf16),
        pltpu.VMEM((2, SQUARE_ROWS, 2 * LANES), jnp.float32),
        pltpu.VMEM(blocks.shape, bf16),
        pltpu.SemaphoreType.DMA((4, 27)),
        pltpu.SemaphoreType.DMA((4, 27)),
        pltpu.SemaphoreType.DMA((2, 16)),
        pltpu.SemaphoreType.DMA((2, 16)),
        pltpu.SemaphoreType.DMA((lines,)),
        pltpu.SemaphoreType.DMA((lines,)),
        pltpu.SemaphoreType.DMA((8,)),
        pltpu.SemaphoreType.DMA((2 * planes, 2)),
        pltpu.SemaphoreType.DMA((2 * planes, 2)),
    ]
    return pl.pallas_call(
        main_kernel,
        out_shape=pltpu.VMEM((PACK, LANES), jnp.float32),
        in_specs=[
            pl.BlockSpec(memory_space=pl.ANY),
            pl.BlockSpec(memory_space=pltpu.SMEM),
            pl.BlockSpec(memory_space=pltpu.SMEM),
            pl.BlockSpec(memory_space=pl.ANY),
        ],
        out_specs=pl.BlockSpec(memory_space=pltpu.VMEM),
        scratch_shapes=scratch,
        compiler_params=params(60, collective_id=0, has_side_effects=True),
    )(blocks, domains, counts, coeff)


def tail_kernel(packed, amp, energy_row, energy_col, out, wide):
    slots = amp.shape[1]
    step = pl.program_id(0)
    full_row = lax.broadcasted_iota(jnp.int32, (slots, slots), 0)
    full_col = lax.broadcasted_iota(jnp.int32, (slots, slots), 1)
    lane = lax.broadcasted_iota(jnp.int32, (MAXPNO, LANES), 1)
    fold_lane = lax.broadcasted_iota(jnp.int32, (FOLD_ROWS, LANES), 1)
    wide[MAXPNO:, :] = jnp.zeros((slots - MAXPNO, slots), jnp.float32)

    def shared_at(begin, end):
        if end <= TOP:
            return packed[MAXPNO + begin : MAXPNO + end, :]
        return packed[HALF_PACK + MAXPNO + begin - TOP : HALF_PACK + MAXPNO + end - TOP, :]

    @pl.when(step == 0)
    def _():
        wide[:MAXPNO, :LANES] = packed[:MAXPNO, :]
        for begin, end in ((0, TOP), (TOP, MAXPNO)):
            wide[begin:end, LANES:] = jnp.where(lane[begin:end] < REST, shared_at(begin, end), 0.0)

    @pl.when(step == 1)
    def _():
        wide[:MAXPNO, :LANES] = packed[HALF_PACK : HALF_PACK + MAXPNO, :]
        for begin, end in ((0, TOP), (TOP, MAXPNO)):
            turned = pltpu.roll(shared_at(begin, end), SPARE, 1)
            wide[begin:end, LANES:] = jnp.where(lane[begin:end] < SPARE, turned, 0.0)
        folded = packed[FOLD_AT:DIAG_AT, :]
        for n in range(SQUARE_ROWS // FOLD_ROWS):
            begin, end = n * FOLD_ROWS, min((n + 1) * FOLD_ROWS, MAXPNO)
            moved = pltpu.roll(folded, (SPARE - n * LEFT) % LANES, 1)
            left = (fold_lane >= SPARE) & (fold_lane < REST)
            held = wide[begin:end, LANES:]
            wide[begin:end, LANES:] = jnp.where(left[: end - begin], moved[: end - begin], held)

    square = wide[...]
    at = DIAG_AT + 2 * step
    diagonal = jnp.concatenate([packed[pl.ds(at, 1), :], packed[pl.ds(at + 1, 1), :]], axis=1)
    on_diagonal = full_row == full_col
    for n in range(2):
        count = packed[pl.ds(COUNTS + 2 * step + n, 1), :][:, :1].astype(jnp.int32)
        row, col = full_row[:MAXPNO], full_col[:MAXPNO]
        if n == 0:
            held = jnp.where(full_row >= full_col, square, 0.0)
        else:
            held = jnp.where(full_row < full_col, square, jnp.where(on_diagonal, diagonal, 0.0))
        products = held[:MAXPNO] + jnp.where(row == col, 0.0, held.T[:MAXPNO])
        valid = (row < count) & (col < count)
        products = jnp.where(valid, products / NAUX, 0.0)
        amps = amp[n]
        contract = (((1,), (1,)), ((), ()))
        high = products.astype(jnp.bfloat16)
        left = products - high.astype(jnp.float32)
        mid = left.astype(jnp.bfloat16)
        low = (left - mid.astype(jnp.float32)).astype(jnp.bfloat16)
        coupled = lax.dot_general(low, amps, contract, preferred_element_type=jnp.float32)
        coupled += lax.dot_general(mid, amps, contract, preferred_element_type=jnp.float32)
        coupled += lax.dot_general(high, amps, contract, preferred_element_type=jnp.float32)
        energies = energy_col[n, :MAXPNO] + energy_row[pl.ds(2 * step + n, 1), :]
        result = products + coupled + energies * amps[:MAXPNO].astype(jnp.float32)
        out[n, :MAXPNO] = jnp.where(valid, result, 0.0)
        out[n, MAXPNO:] = jnp.zeros((slots - MAXPNO, slots), jnp.float32)


def tail(packed, amp, energy):
    subs, slots, _ = amp.shape
    return pl.pallas_call(
        tail_kernel,
        out_shape=jax.ShapeDtypeStruct((subs, slots, slots), jnp.float32),
        grid=(subs // 2,),
        in_specs=[
            pl.BlockSpec((PACK, LANES), lambda i: (0, 0)),
            pl.BlockSpec((2, slots, slots), lambda i: (i, 0, 0)),
            pl.BlockSpec((subs, slots), lambda i: (0, 0)),
            pl.BlockSpec((2, slots, 1), lambda i: (i, 0, 0)),
        ],
        out_specs=pl.BlockSpec((2, slots, slots), lambda i: (i, 0, 0)),
        scratch_shapes=[pltpu.VMEM((slots, slots), jnp.float32)],
        compiler_params=params(32),
    )(packed, amp, energy, energy[:, :, None])


def on_device(atom_blocks, domains, pno_counts, pno_coeffs, amplitudes, pno_energies):
    planes = lax.axis_size("ri")
    mine = pair_products(atom_blocks.transpose(1, 0, 2), domains.T, pno_counts, pno_coeffs, planes)
    return tail(mine, amplitudes, pno_energies)


def solution(mesh):
    placed = (
        P("pairs", None, "ri"),
        P("pairs", None),
        P("pairs"),
        P("pairs", None, None),
        P(("pairs", "ri"), None, None),
        P(("pairs", "ri"), None),
    )
    return jax.shard_map(
        on_device,
        mesh=mesh,
        in_specs=placed,
        out_specs=P(("pairs", "ri"), None, None),
        check_vma=False,
    )
```
